256 devices in a mesh: ctx: 32 (over y, x, core), tp: 8 (over z).
Axes of the slice: x: 4, y: 4, z: 8, core: 2. Of those that a mesh axis runs over, the one named last changes fastest.
Arguments:
- streams: bfloat16 [4096, 3, 4096], P(('ctx', 'tp')), may hold values from -6 to 6
- short_taps: float32 [3, 3, 4096], P(None, None, 'tp'), may hold values from -3.5 to 3.5
- residues: float32 [16, 4096], P(None, 'tp'), may hold values from -0.0546875 to 0.0546875
- rates: float32 [16, 4096], P(None, 'tp'), may hold values from 0.5 to 200
- bias: float32 [4096], P('tp'), may hold values from -1 to 1
Outputs:
- mixed: bfloat16 [4096, 4096], P('ctx', 'tp')
The draws below stay inside these ranges and needn't reach their ends.
All inputs are finite; a program needn't handle non-finite values.
Results may differ from the reference program's by a relative error of at most 0.0015.
Values may be sent and summed in bfloat16 or wider, within the bound.
No kernel may reach another device: no remote copies, remote signals or barrier semaphores. Data moves between devices by JAX's collectives and lax.ppermute only.
A program may use at most 64 MiB of HBM per device.

```python
import math
import jax
import jax.numpy as jnp

WIDTH = 4096
MODES = 16
TOKENS = 4096


def levels(key, extent, split, low, largest):
    gain, own = 1.0, jax.random.fold_in(key, 6)
    for position, blocks in split:
        heights = jnp.exp(jax.random.uniform(jax.random.fold_in(own, position), (blocks,), jnp.float32, low / len(split), largest / len(split)))
        gain = gain * jnp.repeat(heights, extent[position] // blocks).reshape([-1 if axis == position else 1 for axis in range(len(extent))])
    return gain


def gaussian(rng, dims, deviation, limit, cuts=(), kind=jnp.bfloat16):
    level = levels(rng, dims, cuts, -0.22, 0.18) if cuts else 1.0
    values = jax.random.normal(rng, dims, jnp.float32) * deviation * level
    return jnp.minimum(jnp.maximum(values, -limit), limit).astype(kind)


def setup_inputs(seed: int = 0) -> dict:
    key_of = jax.random.split(jax.random.key(seed), 6)
    streams = gaussian(key_of[0], (TOKENS, 3, WIDTH), 1.0, 6.0, ((0, 256),))
    short_taps = gaussian(key_of[1], (3, 3, WIDTH), 3 ** -0.5, 3.5, ((2, 8),), jnp.float32)
    residues = gaussian(key_of[2], (MODES, WIDTH), (3 * TOKENS) ** -0.5, 0.0546875, ((1, 8),), jnp.float32)
    rates = jnp.clip(jnp.exp(math.log(200.0) - 5.9914645 * jax.random.uniform(key_of[3], (MODES, WIDTH), jnp.float32) ** levels(key_of[3], (MODES, WIDTH), ((1, 8),), -0.2, 0.2)), 0.5, 200.0)
    bias = jnp.clip(jax.random.uniform(key_of[4], (WIDTH,), jnp.float32, -1.0, 1.0) * levels(key_of[4], (WIDTH,), ((0, 8),), -0.4, 0.0), -1.0, 1.0)
    return dict(streams=streams, short_taps=short_taps, residues=residues, rates=rates, bias=bias)


def reference(streams, short_taps, residues, rates, bias):
    values = streams.astype(jnp.float32)
    padded = jnp.pad(values, ((2, 0), (0, 0), (0, 0)))
    feat = short_taps[0] * padded[2:] + short_taps[1] * padded[1:-1] + short_taps[2] * padded[:-2]
    signal = feat[:, 1] * feat[:, 2]
    length = signal.shape[0]
    where = jnp.arange(length, dtype=jnp.int32).astype(jnp.float32)[:, None] / length
    filt = jnp.zeros_like(signal)
    for mode in range(residues.shape[0]):
        filt = filt + residues[mode] * jnp.exp(-rates[mode] * where)
    spectrum = jnp.fft.rfft(signal, n=2 * length, axis=0) * jnp.fft.rfft(filt, n=2 * length, axis=0)
    conv = jnp.fft.irfft(spectrum, n=2 * length, axis=0)[:length]
    return (feat[:, 0] * (conv + bias * signal)).astype(jnp.bfloat16)
```

```python
import jax
import jax.numpy as jnp
from jax import lax
from jax.experimental import pallas as pl
from jax.experimental.pallas import tpu as pltpu
from jax.sharding import PartitionSpec as P

LENGTH = 4096
SUB = 16
SHIFTS = (4, 3, 5, 2, 6, 1, 7)
LANES = 128
VMEM = pl.BlockSpec(memory_space=pltpu.VMEM)


def row_iota():
    return lax.broadcasted_iota(jnp.int32, (8, LANES), 0)


def spread(row):
    return jnp.broadcast_to(row, (8, LANES))


def fill_tokens(blocks, order, stream, scratch):
    me = lax.axis_index("tp")
    count = len(blocks)
    for block, shift in zip(blocks, order):
        source = lax.rem(me - shift + count, count)
        at = pl.multiple_of(source * SUB, SUB)
        for group in range(scratch.shape[0]):
            lanes = pl.ds(group * LANES, LANES)
            scratch[group, pl.ds(at, SUB), :] = block[stream, :, lanes].astype(jnp.float32)


def featurize(scratch, stream, lanes, taps_ref, halo_ref):
    group = lanes.start // LANES
    values = [scratch[group, pl.ds(i, 8, stride=SUB), :] for i in range(SUB)]
    first = row_iota() == 0
    back = []
    for far in (2, 1):
        halo = halo_ref[stream, 2 - far : 3 - far, lanes].astype(jnp.float32)
        back.append(jnp.where(first, spread(halo), pltpu.roll(values[SUB - far], 1, 0)))
    joined = back + values
    t0, t1, t2 = (spread(taps_ref[j, stream : stream + 1, lanes]) for j in range(3))
    return [t0 * joined[i + 2] + t1 * joined[i + 1] + t2 * joined[i] for i in range(SUB)]


def state_kernel(order, *refs):
    count = len(order)
    blocks = refs[:count]
    halo_ref, taps_ref, rates_ref, state_ref, ends_ref, signal_ref, one, two = refs[count:]
    modes, channels = rates_ref.shape
    fill_tokens(blocks, order, 1, one)
    fill_tokens(blocks, order, 2, two)
    step = row_iota().astype(jnp.float32)
    remaining = (7.0 - step) * (SUB / LENGTH)
    for start in range(0, channels, LANES):
        lanes = pl.ds(start, LANES)
        left = featurize(one, 1, lanes, taps_ref, halo_ref)
        right = featurize(two, 2, lanes, taps_ref, halo_ref)
        signal = [a * b for a, b in zip(left, right)]
        for i in range(SUB):
            signal_ref[i, :, lanes] = signal[i]
        for mode in range(modes):
            rate = spread(rates_ref[mode : mode + 1, lanes])
            decay = jnp.exp(rate * (-1.0 / LENGTH))
            state = signal[0]
            for i in range(1, SUB):
                state = state * decay + signal[i]
            ends_ref[mode, :, lanes] = state
            weight = jnp.exp(-rate * remaining)
            state_ref[mode : mode + 1, lanes] = jnp.sum(state * weight, axis=0, keepdims=True)


def local_kernel(order, *refs):
    count = len(order)
    blocks = refs[:count]
    (halo_ref, taps_ref, rates_ref, residues_ref, bias_ref, ends_ref, signal_ref, local_ref, front_ref, zero) = refs[count:]
    modes, channels = rates_ref.shape
    fill_tokens(blocks, order, 0, zero)
    rows = row_iota()
    step = rows.astype(jnp.float32)
    for start in range(0, channels, LANES):
        lanes = pl.ds(start, LANES)
        front = featurize(zero, 0, lanes, taps_ref, halo_ref)
        for i in range(SUB):
            front_ref[i, :, lanes] = front[i]
        signal = [signal_ref[i, :, lanes] for i in range(SUB)]
        taps = [jnp.zeros((8, LANES), jnp.float32) for _ in range(SUB // 8)]
        for mode in range(modes):
            rate = spread(rates_ref[mode : mode + 1, lanes])
            residue = spread(residues_ref[mode : mode + 1, lanes])
            for part in range(SUB // 8):
                taps[part] = taps[part] + residue * jnp.exp(-rate * ((step + 8.0 * part) * (1.0 / LENGTH)))
        bias = spread(bias_ref[0:1, lanes])
        total = [bias * signal[i] for i in range(SUB)]
        for lag in range(SUB):
            tap = spread(taps[lag // 8][lag % 8 : lag % 8 + 1])
            for i in range(lag, SUB):
                total[i] = total[i] + tap * signal[i - lag]
        for mode in range(modes):
            rate = spread(rates_ref[mode : mode + 1, lanes])
            residue = spread(residues_ref[mode : mode + 1, lanes])
            decay = jnp.exp(rate * (-1.0 / LENGTH))
            state = ends_ref[mode, :, lanes]
            for far in (1, 2, 4):
                power = jnp.exp(rate * (-far * SUB / LENGTH))
                state = state + jnp.where(rows >= far, power * pltpu.roll(state, far, 0), 0.0)
            carried = jnp.where(rows >= 1, pltpu.roll(state, 1, 0), 0.0) * residue
            for i in range(SUB):
                carried = carried * decay
                total[i] = total[i] + carried
        for i in range(SUB):
            local_ref[i, :, lanes] = total[i]


def final_kernel(carry_ref, rates_ref, residues_ref, local_ref, front_ref, out_ref, natural):
    modes, channels = rates_ref.shape
    step = row_iota().astype(jnp.float32)
    for start in range(0, channels, LANES):
        lanes = pl.ds(start, LANES)
        total = [local_ref[i, :, lanes] for i in range(SUB)]
        for mode in range(modes):
            rate = spread(rates_ref[mode : mode + 1, lanes])
            decay = jnp.exp(rate * (-1.0 / LENGTH))
            first = residues_ref[mode : mode + 1, lanes] * carry_ref[mode : mode + 1, lanes]
            carried = spread(first) * jnp.exp(-rate * ((step * SUB + 1.0) * (1.0 / LENGTH)))
            total[0] = total[0] + carried
            for i in range(1, SUB):
                carried = carried * decay
                total[i] = total[i] + carried
        for i in range(SUB):
            natural[start // LANES, pl.ds(i, 8, stride=SUB), :] = front_ref[i, :, lanes] * total[i]
        out_ref[:, lanes] = natural[start // LANES].astype(out_ref.dtype)


def scan_states(state, rates, mesh):
    index = lax.axis_index("ctx")
    core = index % 2
    column = (index // 2) % 4
    line = index // 8
    total_blocks = lax.axis_size("ctx")

    def power(blocks):
        return jnp.exp(rates * (-jnp.asarray(blocks, jnp.float32) / total_blocks))

    other = lax.ppermute(state, "ctx", [(i, i ^ 1) for i in range(total_blocks)])
    upper = core == 1
    pair = jnp.where(upper, state + power(1) * other, other + power(1) * state)
    inner = jnp.where(upper, other, 0.0)

    def across(value, weight, size, wrap):
        parts = {}
        for by in (2, 1, 3):
            route = []
            for i in range(total_blocks):
                place = (i // weight) % size
                if wrap or place + by < size:
                    route.append((i, i + ((place + by) % size - place) * weight))
            parts[by] = lax.ppermute(value, "ctx", route)
        return parts

    got = across(pair, 2, 4, True)
    before = jnp.zeros_like(pair)
    whole = power(2 * (3 - column)) * pair
    for by, part in got.items():
        before = before + jnp.where(column >= by, power(2 * (by - 1)) * part, 0.0)
        whole = whole + power(2 * (3 - (column - by) % 4)) * part
    got = across(whole, 8, 4, False)
    above = jnp.zeros_like(pair)
    for by, part in got.items():
        above = above + jnp.where(line >= by, power(8 * (by - 1)) * part, 0.0)
    return above * power(2 * column + core) + before * power(core) + inner


def body(streams, short_taps, residues, rates, bias):
    parts = lax.axis_size("tp")
    me = lax.axis_index("tp")
    channels = rates.shape[1]
    modes = rates.shape[0]
    by_stream = jnp.transpose(streams, (1, 0, 2))

    def block_for(shift):
        at = ((me + shift) % parts) * channels
        return lax.dynamic_slice(by_stream, (0, 0, at), (3, SUB, channels))

    order = SHIFTS + (0,)
    blocks = [
        lax.ppermute(block_for(shift), "tp", [(i, (i + shift) % parts) for i in range(parts)]) for shift in SHIFTS
    ] + [block_for(0)]
    tails = [block[:, SUB - 2 :] for block in blocks]
    tail = tails[0]
    for shift, piece in zip(order[1:], tails[1:]):
        tail = jnp.where((me - shift) % parts == parts - 1, piece, tail)
    ctx = lax.axis_size("ctx")
    halo = lax.ppermute(tail, "ctx", [(i, i + 1) for i in range(ctx - 1)])
    f32 = jnp.float32
    tokens = SUB * parts
    wide = jax.ShapeDtypeStruct((SUB, parts, channels), f32)
    limit = pltpu.CompilerParams(vmem_limit_bytes=24 << 20)
    state, ends, signal = pl.pallas_call(
        lambda *refs: state_kernel(order, *refs),
        out_shape=(
            jax.ShapeDtypeStruct((modes, channels), f32),
            jax.ShapeDtypeStruct((modes, parts, channels), f32),
            wide,
        ),
        in_specs=[VMEM] * 11,
        out_specs=(VMEM,) * 3,
        scratch_shapes=[pltpu.VMEM((channels // LANES, tokens, LANES), f32)] * 2,
        compiler_params=limit,
        name="state",
    )(*blocks, halo, short_taps, rates)
    carry = scan_states(state, rates, None)
    local, front = pl.pallas_call(
        lambda *refs: local_kernel(order, *refs),
        out_shape=(wide, wide),
        in_specs=[VMEM] * 15,
        out_specs=(VMEM,) * 2,
        scratch_shapes=[pltpu.VMEM((channels // LANES, tokens, LANES), f32)],
        compiler_params=limit,
        cost_estimate=pl.CostEstimate(flops=8 << 20, bytes_accessed=2 << 20, transcendentals=0),
        name="local",
    )(*blocks, halo, short_taps, rates, residues, bias[None], ends, signal)
    return pl.pallas_call(
        final_kernel,
        out_shape=jax.ShapeDtypeStruct((tokens, channels), jnp.bfloat16),
        in_specs=[VMEM] * 5,
        out_specs=VMEM,
        scratch_shapes=[pltpu.VMEM((channels // LANES, tokens, LANES), f32)],
        compiler_params=limit,
        name="final",
    )(carry, rates, residues, local, front)


def solution(mesh):
    in_specs = (
        P(("ctx", "tp"), None, None),
        P(None, None, "tp"),
        P(None, "tp"),
        P(None, "tp"),
        P("tp"),
    )
    out_specs = P("ctx", "tp")
    return jax.shard_map(body, mesh=mesh, in_specs=in_specs, out_specs=out_specs, check_vma=False)
```

```python
import jax
import jax.numpy as jnp
from jax import lax
from jax.experimental import pallas as pl
from jax.experimental.pallas import tpu as pltpu
from jax.sharding import PartitionSpec as P

LENGTH = 4096
SUB = 16
PIECES = 7
LANES = 128
VMEM = pl.BlockSpec(memory_space=pltpu.VMEM)


def row_iota():
    return lax.broadcasted_iota(jnp.int32, (8, LANES), 0)


def spread(row):
    return jnp.broadcast_to(row, (8, LANES))


def fill_tokens(blocks, stream, scratch):
    me = lax.axis_index("tp")
    turn = 2 * lax.rem(lax.axis_index("ctx"), 2) - 1
    for block, shift in blocks:
        source = lax.rem(me - turn * shift + 8, 8)
        at = pl.multiple_of(source * SUB, SUB)
        for group in range(scratch.shape[0]):
            lanes = pl.ds(group * LANES, LANES)
            scratch[group, pl.ds(at, SUB), :] = block[stream, :, lanes].astype(jnp.float32)


def arrange(refs):
    far, near, *single = refs
    shifts = (-3, 2, -2, -1, 0)
    return [(far.at[0], 3), (near.at[0], 1), (near.at[1], 4), *zip(single, shifts)]


def featurize(scratch, stream, lanes, taps_ref, halo_ref):
    group = lanes.start // LANES
    values = [scratch[group, pl.ds(i, 8, stride=SUB), :] for i in range(SUB)]
    first = row_iota() == 0
    back = []
    for far in (2, 1):
        halo = halo_ref[stream, 2 - far : 3 - far, lanes].astype(jnp.float32)
        back.append(jnp.where(first, spread(halo), pltpu.roll(values[SUB - far], 1, 0)))
    joined = back + values
    t0, t1, t2 = (spread(taps_ref[j, stream : stream + 1, lanes]) for j in range(3))
    return [t0 * joined[i + 2] + t1 * joined[i + 1] + t2 * joined[i] for i in range(SUB)]


def state_kernel(*refs):
    blocks = arrange(refs[:PIECES])
    halo_ref, taps_ref, rates_ref, state_ref, ends_ref, signal_ref, one, two = refs[PIECES:]
    modes, channels = rates_ref.shape
    fill_tokens(blocks, 1, one)
    fill_tokens(blocks, 2, two)
    step = row_iota().astype(jnp.float32)
    remaining = (7.0 - step) * (SUB / LENGTH)
    for start in range(0, channels, LANES):
        lanes = pl.ds(start, LANES)
        left = featurize(one, 1, lanes, taps_ref, halo_ref)
        right = featurize(two, 2, lanes, taps_ref, halo_ref)
        signal = [a * b for a, b in zip(left, right)]
        for i in range(SUB):
            signal_ref[i, :, lanes] = signal[i]
        for mode in range(modes):
            rate = spread(rates_ref[mode : mode + 1, lanes])
            decay = jnp.exp(rate * (-1.0 / LENGTH))
            state = signal[0]
            for i in range(1, SUB):
                state = state * decay + signal[i]
            ends_ref[mode, :, lanes] = state
            weight = jnp.exp(-rate * remaining)
            state_ref[mode : mode + 1, lanes] = jnp.sum(state * weight, axis=0, keepdims=True)


def local_kernel(*refs):
    blocks = arrange(refs[:PIECES])
    halo_ref, taps_ref, rates_ref, residues_ref, bias_ref, ends_ref, signal_ref, local_ref, front_ref, zero = refs[PIECES:]
    modes, channels = rates_ref.shape
    fill_tokens(blocks, 0, zero)
    rows = row_iota()
    step = rows.astype(jnp.float32)
    for start in range(0, channels, LANES):
        lanes = pl.ds(start, LANES)
        front = featurize(zero, 0, lanes, taps_ref, halo_ref)
        for i in range(SUB):
            front_ref[i, :, lanes] = front[i]
        signal = [signal_ref[i, :, lanes] for i in range(SUB)]
        taps = [jnp.zeros((8, LANES), jnp.float32) for _ in range(SUB // 8)]
        for mode in range(modes):
            rate = spread(rates_ref[mode : mode + 1, lanes])
            residue = spread(residues_ref[mode : mode + 1, lanes])
            for part in range(SUB // 8):
                taps[part] = taps[part] + residue * jnp.exp(-rate * ((step + 8.0 * part) * (1.0 / LENGTH)))
        bias = spread(bias_ref[0:1, lanes])
        total = [bias * signal[i] for i in range(SUB)]
        for lag in range(SUB):
            tap = spread(taps[lag // 8][lag % 8 : lag % 8 + 1])
            for i in range(lag, SUB):
                total[i] = total[i] + tap * signal[i - lag]
        for mode in range(modes):
            rate = spread(rates_ref[mode : mode + 1, lanes])
            residue = spread(residues_ref[mode : mode + 1, lanes])
            decay = jnp.exp(rate * (-1.0 / LENGTH))
            state = ends_ref[mode, :, lanes]
            for far in (1, 2, 4):
                power = jnp.exp(rate * (-far * SUB / LENGTH))
                state = state + jnp.where(rows >= far, power * pltpu.roll(state, far, 0), 0.0)
            carried = jnp.where(rows >= 1, pltpu.roll(state, 1, 0), 0.0) * residue
            for i in range(SUB):
                carried = carried * decay
                total[i] = total[i] + carried
        for i in range(SUB):
            local_ref[i, :, lanes] = total[i]


def final_kernel(carry_ref, rates_ref, residues_ref, local_ref, front_ref, out_ref, natural):
    modes, channels = rates_ref.shape
    step = row_iota().astype(jnp.float32)
    for start in range(0, channels, LANES):
        lanes = pl.ds(start, LANES)
        total = [local_ref[i, :, lanes] for i in range(SUB)]
        for mode in range(modes):
            rate = spread(rates_ref[mode : mode + 1, lanes])
            decay = jnp.exp(rate * (-1.0 / LENGTH))
            first = residues_ref[mode : mode + 1, lanes] * carry_ref[mode : mode + 1, lanes]
            carried = spread(first) * jnp.exp(-rate * ((step * SUB + 1.0) * (1.0 / LENGTH)))
            total[0] = total[0] + carried
            for i in range(1, SUB):
                carried = carried * decay
                total[i] = total[i] + carried
        for i in range(SUB):
            natural[start // LANES, pl.ds(i, 8, stride=SUB), :] = front_ref[i, :, lanes] * total[i]
        out_ref[:, lanes] = natural[start // LANES].astype(out_ref.dtype)


def scan_states(state, rates):
    index = lax.axis_index("ctx")
    blocks = lax.axis_size("ctx")
    carry = jnp.zeros_like(state)

    def power(count):
        return jnp.exp(rates * (-jnp.asarray(count, jnp.float32) / blocks))

    for level, flip in enumerate((1, 2, 6, 8, 24)):
        size = 1 << level
        last = 2 * size == blocks
        route = [(i, i ^ flip) for i in range(blocks) if not (last and i & size)]
        other = lax.ppermute(state, "ctx", route)
        upper = (index & size) != 0
        carry = carry + jnp.where(upper, power(index % size) * other, 0.0)
        if not last:
            state = jnp.where(upper, state + power(size) * other, other + power(size) * state)
    return carry


def body(streams, short_taps, residues, rates, bias):
    parts = lax.axis_size("tp")
    ctx = lax.axis_size("ctx")
    me = lax.axis_index("tp")
    turn = 2 * (lax.axis_index("ctx") % 2) - 1
    modes, channels = rates.shape
    tokens = SUB * parts
    f32 = jnp.float32
    by_stream = jnp.transpose(streams, (1, 0, 2))

    def block_for(shift):
        at = ((me + turn * shift) % parts) * channels
        return lax.dynamic_slice(by_stream, (0, 0, at), (3, SUB, channels))

    def send(block, shift):
        route = []
        for c in range(ctx):
            step = shift if c % 2 else -shift
            route += [(c * parts + z, c * parts + (z + step) % parts) for z in range(parts)]
        return lax.ppermute(block, ("ctx", "tp"), route)

    far = send(jnp.stack([block_for(3), block_for(4)]), 3)
    single = [send(block_for(shift), shift) for shift in (-3, 2, -2)]
    own = block_for(1)
    for later in single[:2]:
        own = jnp.where(me < 0, later, own)
    near = send(jnp.stack([own, far[1]]), 1)
    single += [send(block_for(-1), -1), block_for(0)]
    pieces = [far, near, *single]

    ends = ((far[0], 3), (near[0], 1), (near[1], 4), *zip(single, (-3, 2, -2, -1, 0)))
    tail = single[-1][:, SUB - 2 :]
    for block, shift in ends[:-1]:
        tail = jnp.where((me - turn * shift) % parts == parts - 1, block[:, SUB - 2 :], tail)
    halo = lax.ppermute(tail, "ctx", [(i, i + 1) for i in range(ctx - 1)])
    wide = jax.ShapeDtypeStruct((SUB, parts, channels), f32)
    limit = pltpu.CompilerParams(vmem_limit_bytes=24 << 20)
    state, ends, signal = pl.pallas_call(
        state_kernel,
        out_shape=(
            jax.ShapeDtypeStruct((modes, channels), f32),
            jax.ShapeDtypeStruct((modes, parts, channels), f32),
            wide,
        ),
        in_specs=[VMEM] * (PIECES + 3),
        out_specs=(VMEM,) * 3,
        scratch_shapes=[pltpu.VMEM((channels // LANES, tokens, LANES), f32)] * 2,
        compiler_params=limit,
        name="state",
    )(*pieces, halo, short_taps, rates)
    carry = scan_states(state, rates)
    local, front = pl.pallas_call(
        local_kernel,
        out_shape=(wide, wide),
        in_specs=[VMEM] * (PIECES + 7),
        out_specs=(VMEM,) * 2,
        scratch_shapes=[pltpu.VMEM((channels // LANES, tokens, LANES), f32)],
        compiler_params=limit,
        cost_estimate=pl.CostEstimate(flops=8 << 20, bytes_accessed=2 << 20, transcendentals=0),
        name="local",
    )(*pieces, halo, short_taps, rates, residues, bias[None], ends, signal)
    return pl.pallas_call(
        final_kernel,
        out_shape=jax.ShapeDtypeStruct((tokens, channels), jnp.bfloat16),
        in_specs=[VMEM] * 5,
        out_specs=VMEM,
        scratch_shapes=[pltpu.VMEM((channels // LANES, tokens, LANES), f32)],
        compiler_params=limit,
        name="final",
    )(carry, rates, residues, local, front)


def solution(mesh):
    in_specs = (
        P(("ctx", "tp"), None, None),
        P(None, None, "tp"),
        P(None, "tp"),
        P(None, "tp"),
        P("tp"),
    )
    out_specs = P("ctx", "tp")
    return jax.shard_map(body, mesh=mesh, in_specs=in_specs, out_specs=out_specs, check_vma=False)
```

```python
import jax
import jax.numpy as jnp
from jax import lax
from jax.experimental import pallas as pl
from jax.experimental.pallas import tpu as pltpu
from jax.sharding import PartitionSpec as P

LENGTH = 4096
SUB = 16
SHIFTS = (4, 3, 5, 2, 6, 1, 7)
LANES = 128
VMEM = pl.BlockSpec(memory_space=pltpu.VMEM)


def row_iota():
    return lax.broadcasted_iota(jnp.int32, (8, LANES), 0)


def spread(row):
    return jnp.broadcast_to(row, (8, LANES))


def gather_kernel(streams_ref, out_ref, sems):
    count, _, channels = out_ref.shape
    copies = [
        pltpu.make_async_copy(
            streams_ref.at[s, :, pl.ds(d * channels, channels)],
            out_ref.at[d, pl.ds(s * SUB, SUB), :],
            sems.at[d * 3 + s],
        )
        for d in range(count)
        for s in range(3)
    ]
    for copy in copies:
        copy.start()
    for copy in copies:
        copy.wait()


def fill_tokens(blocks_ref, stream, scratch):
    for source in range(blocks_ref.shape[0]):
        for group in range(scratch.shape[0]):
            lanes = pl.ds(group * LANES, LANES)
            rows = blocks_ref[source, pl.ds(stream * SUB, SUB), lanes]
            scratch[group, pl.ds(source * SUB, SUB), :] = rows.astype(jnp.float32)


def featurize(scratch, stream, lanes, taps_ref, halo_ref):
    group = lanes.start // LANES
    values = [scratch[group, pl.ds(i, 8, stride=SUB), :] for i in range(SUB)]
    first = row_iota() == 0
    back = []
    for far in (2, 1):
        moved = pltpu.roll(values[SUB - far], 1, 0)
        if halo_ref is not None:
            halo = halo_ref[stream, 2 - far : 3 - far, lanes].astype(jnp.float32)
            moved = jnp.where(first, spread(halo), moved)
        back.append(moved)
    joined = back + values
    t0, t1, t2 = (spread(taps_ref[j, stream : stream + 1, lanes]) for j in range(3))
    return [t0 * joined[i + 2] + t1 * joined[i + 1] + t2 * joined[i] for i in range(SUB)]


def state_kernel(blocks_ref, taps_ref, rates_ref, residues_ref, bias_ref, state_ref, ends_ref, signal_ref, one, two):
    del residues_ref, bias_ref
    modes, channels = rates_ref.shape
    fill_tokens(blocks_ref, 1, one)
    fill_tokens(blocks_ref, 2, two)
    rows = row_iota()
    step = rows.astype(jnp.float32)
    remaining = (7.0 - step) * (SUB / LENGTH)
    for start in range(0, channels, LANES):
        lanes = pl.ds(start, LANES)
        left = featurize(one, 1, lanes, taps_ref, None)
        right = featurize(two, 2, lanes, taps_ref, None)
        signal = [a * b for a, b in zip(left, right)]
        for i in range(2):
            signal[i] = jnp.where(rows == 0, 0.0, signal[i])
        for i in range(SUB):
            signal_ref[i, :, lanes] = signal[i]
        for mode in range(modes):
            rate = spread(rates_ref[mode : mode + 1, lanes])
            decay = jnp.exp(rate * (-1.0 / LENGTH))
            state = signal[0]
            for i in range(1, SUB):
                state = state * decay + signal[i]
            ends_ref[mode, :, lanes] = state
            weight = jnp.exp(-rate * remaining)
            state_ref[mode : mode + 1, lanes] = jnp.sum(state * weight, axis=0, keepdims=True)


def local_kernel(
    blocks_ref, halo_ref, edge_ref, taps_ref, rates_ref, residues_ref, bias_ref, ends_ref, signal_ref, local_ref, front_ref, zero
):
    modes, channels = rates_ref.shape
    fill_tokens(blocks_ref, 0, zero)
    rows = row_iota()
    step = rows.astype(jnp.float32)
    for start in range(0, channels, LANES):
        lanes = pl.ds(start, LANES)
        front = featurize(zero, 0, lanes, taps_ref, halo_ref)
        for i in range(SUB):
            front_ref[i, :, lanes] = front[i]
        signal = [signal_ref[i, :, lanes] for i in range(SUB)]
        edge = [jnp.where(rows == 0, spread(edge_ref[i : i + 1, lanes]), 0.0) for i in range(2)]
        for i in range(2):
            signal[i] = signal[i] + edge[i]
        taps = [jnp.zeros((8, LANES), jnp.float32) for _ in range(SUB // 8)]
        for mode in range(modes):
            rate = spread(rates_ref[mode : mode + 1, lanes])
            residue = spread(residues_ref[mode : mode + 1, lanes])
            for part in range(SUB // 8):
                taps[part] = taps[part] + residue * jnp.exp(-rate * ((step + 8.0 * part) * (1.0 / LENGTH)))
        bias = spread(bias_ref[0:1, lanes])
        total = [bias * signal[i] for i in range(SUB)]
        for lag in range(SUB):
            tap = spread(taps[lag // 8][lag % 8 : lag % 8 + 1])
            for i in range(lag, SUB):
                total[i] = total[i] + tap * signal[i - lag]
        for mode in range(modes):
            rate = spread(rates_ref[mode : mode + 1, lanes])
            residue = spread(residues_ref[mode : mode + 1, lanes])
            decay = jnp.exp(rate * (-1.0 / LENGTH))
            state = ends_ref[mode, :, lanes] + jnp.exp(rate * (-14.0 / LENGTH)) * (decay * edge[0] + edge[1])
            for far in (1, 2, 4):
                power = jnp.exp(rate * (-far * SUB / LENGTH))
                state = state + jnp.where(rows >= far, power * pltpu.roll(state, far, 0), 0.0)
            carried = jnp.where(rows >= 1, pltpu.roll(state, 1, 0), 0.0) * residue
            for i in range(SUB):
                carried = carried * decay
                total[i] = total[i] + carried
        for i in range(SUB):
            local_ref[i, :, lanes] = total[i]


def final_kernel(mine_ref, other_ref, rates_ref, residues_ref, local_ref, front_ref, out_ref, natural):
    modes, channels = rates_ref.shape
    step = row_iota().astype(jnp.float32)
    core = lax.rem(lax.axis_index("ctx"), 2)
    half = channels // 2
    for start in range(0, channels, LANES):
        lanes = pl.ds(start, LANES)
        within = pl.ds(start % half, LANES)
        own = core == start // half
        total = [local_ref[i, :, lanes] for i in range(SUB)]
        for mode in range(modes):
            rate = spread(rates_ref[mode : mode + 1, lanes])
            decay = jnp.exp(rate * (-1.0 / LENGTH))
            carry = jnp.where(own, mine_ref[mode : mode + 1, within], other_ref[mode : mode + 1, within])
            first = residues_ref[mode : mode + 1, lanes] * carry
            carried = spread(first) * jnp.exp(-rate * ((step * SUB + 1.0) * (1.0 / LENGTH)))
            total[0] = total[0] + carried
            for i in range(1, SUB):
                carried = carried * decay
                total[i] = total[i] + carried
        for i in range(SUB):
            natural[start // LANES, pl.ds(i, 8, stride=SUB), :] = front_ref[i, :, lanes] * total[i]
        out_ref[:, lanes] = natural[start // LANES].astype(out_ref.dtype)


def scan_states(state, rates):
    index = lax.axis_index("ctx")
    blocks = lax.axis_size("ctx")
    chips = blocks // 2
    chip, core = index // 2, index % 2
    modes, channels = state.shape
    half = channels // 2
    swap = [(i, i ^ 1) for i in range(blocks)]

    def power(rate, count):
        return jnp.exp(rate * (-jnp.asarray(count, jnp.float32) / blocks))

    def pick(value, which):
        return jnp.where(which == 0, value[:, :half], value[:, half:])

    rate = pick(rates, core)
    got = lax.ppermute(pick(state, 1 - core), "ctx", swap)
    kept = pick(state, core)
    lower = jnp.where(core == 0, kept, got)
    upper = jnp.where(core == 0, got, kept)
    pair = upper + power(rate, 1) * lower
    groups = [[2 * k + c for k in range(chips)] for c in range(2)]
    every = lax.all_to_all(
        jnp.broadcast_to(pair[None], (chips, modes, half)), "ctx", 0, 0, axis_index_groups=groups, tiled=True
    )
    before = jnp.zeros_like(pair)
    for k in range(chips - 1):
        ahead = jnp.maximum(chip - 1 - k, 0)
        before = before + jnp.where(k < chip, power(rate, 2 * ahead), 0.0) * every[k]
    after = power(rate, 1) * before + lower
    mine = jnp.where(core == 0, before, after)
    return mine, lax.ppermute(jnp.where(core == 0, after, before), "ctx", swap)


def body(streams, short_taps, residues, rates, bias):
    parts = lax.axis_size("tp")
    ctx = lax.axis_size("ctx")
    modes, channels = rates.shape
    tokens = SUB * parts
    f32 = jnp.float32
    limit = pltpu.CompilerParams(vmem_limit_bytes=24 << 20)
    outgoing = pl.pallas_call(
        gather_kernel,
        out_shape=jax.ShapeDtypeStruct((parts, 3 * SUB, channels), streams.dtype),
        in_specs=[pl.BlockSpec(memory_space=pl.ANY)],
        out_specs=VMEM,
        scratch_shapes=[pltpu.SemaphoreType.DMA((3 * parts,))],
        compiler_params=limit,
        name="gather",
    )(jnp.transpose(streams, (1, 0, 2)))
    blocks = lax.all_to_all(outgoing, "tp", 0, 0, tiled=True)
    ends_of = [slice(s * SUB + SUB - 2, s * SUB + SUB) for s in range(3)]
    tail = jnp.stack([blocks[parts - 1, rows] for rows in ends_of])
    halo = lax.ppermute(tail, "ctx", [(i, i + 1) for i in range(ctx - 1)])
    wide = jax.ShapeDtypeStruct((SUB, parts, channels), f32)
    state, ends, signal = pl.pallas_call(
        state_kernel,
        out_shape=(
            jax.ShapeDtypeStruct((modes, channels), f32),
            jax.ShapeDtypeStruct((modes, parts, channels), f32),
            wide,
        ),
        in_specs=[VMEM] * 5,
        out_specs=(VMEM,) * 3,
        scratch_shapes=[pltpu.VMEM((channels // LANES, tokens, LANES), f32)] * 2,
        compiler_params=limit,
        cost_estimate=pl.CostEstimate(flops=8 << 20, bytes_accessed=2 << 20, transcendentals=0),
        name="state",
    )(blocks, short_taps, rates, residues, bias[None])
    edge = None
    for s in (1, 2):
        x = [blocks[0, s * SUB + i].astype(f32) for i in range(2)]
        h = [halo[s, i].astype(f32) for i in range(2)]
        t0, t1, t2 = (short_taps[j, s] for j in range(3))
        feat = jnp.stack([t0 * x[0] + t1 * h[1] + t2 * h[0], t0 * x[1] + t1 * x[0] + t2 * h[1]])
        edge = feat if edge is None else edge * feat
    state = state + jnp.exp(rates * (-(tokens - 2.0) / LENGTH)) * (jnp.exp(rates * (-1.0 / LENGTH)) * edge[0] + edge[1])
    mine, other = scan_states(state, rates)
    local, front = pl.pallas_call(
        local_kernel,
        out_shape=(wide, wide),
        in_specs=[VMEM] * 9,
        out_specs=(VMEM,) * 2,
        scratch_shapes=[pltpu.VMEM((channels // LANES, tokens, LANES), f32)],
        compiler_params=limit,
        cost_estimate=pl.CostEstimate(flops=8 << 20, bytes_accessed=2 << 20, transcendentals=0),
        name="local",
    )(blocks, halo, edge, short_taps, rates, residues, bias[None], ends, signal)
    return pl.pallas_call(
        final_kernel,
        out_shape=jax.ShapeDtypeStruct((tokens, channels), jnp.bfloat16),
        in_specs=[VMEM] * 6,
        out_specs=VMEM,
        scratch_shapes=[pltpu.VMEM((channels // LANES, tokens, LANES), f32)],
        compiler_params=limit,
        name="final",
    )(mine, other, rates, residues, local, front)


def solution(mesh):
    in_specs = (
        P(("ctx", "tp"), None, None),
        P(None, None, "tp"),
        P(None, "tp"),
        P(None, "tp"),
        P("tp"),
    )
    out_specs = P("ctx", "tp")
    return jax.shard_map(body, mesh=mesh, in_specs=in_specs, out_specs=out_specs, check_vma=False)
```

```python
import jax
import jax.numpy as jnp
from jax import lax
from jax.experimental import pallas as pl
from jax.experimental.pallas import tpu as pltpu
from jax.sharding import PartitionSpec as P

LENGTH = 4096
SUB = 16
SHIFTS = (4, 3, 5, 2, 6, 1, 7)
LANES = 128
BLOCK = 128
CHIPS = 16
VMEM = pl.BlockSpec(memory_space=pltpu.VMEM)


def row_iota():
    return lax.broadcasted_iota(jnp.int32, (8, LANES), 0)


def spread(row):
    return jnp.broadcast_to(row, (8, LANES))


def gather_kernel(streams_ref, out_ref, sems):
    count, _, channels = out_ref.shape
    copies = [
        pltpu.make_async_copy(
            streams_ref.at[s, :, pl.ds(d * channels, channels)],
            out_ref.at[d, pl.ds(s * SUB, SUB), :],
            sems.at[d * 3 + s],
        )
        for d in range(count)
        for s in range(3)
    ]
    for copy in copies:
        copy.start()
    for copy in copies:
        copy.wait()


def fill_tokens(blocks_ref, stream, scratch):
    for source in range(blocks_ref.shape[0]):
        for group in range(scratch.shape[0]):
            lanes = pl.ds(group * LANES, LANES)
            rows = blocks_ref[source, pl.ds(stream * SUB, SUB), lanes]
            scratch[group, pl.ds(source * SUB, SUB), :] = rows.astype(jnp.float32)


def featurize(scratch, stream, lanes, taps_ref):
    group = lanes.start // LANES
    values = [scratch[group, pl.ds(i, 8, stride=SUB), :] for i in range(SUB)]
    first = row_iota() == 0
    joined = [jnp.where(first, 0.0, pltpu.roll(values[SUB - far], 1, 0)) for far in (2, 1)] + values
    t0, t1, t2 = (spread(taps_ref[j, stream : stream + 1, lanes]) for j in range(3))
    return [t0 * joined[i + 2] + t1 * joined[i + 1] + t2 * joined[i] for i in range(SUB)]


def power(rate, tokens):
    return jnp.exp(rate * (-float(tokens) / LENGTH))


def core_index():
    return lax.rem(lax.axis_index("ctx"), 2)


def half_of(value, which):
    half = value.shape[-1] // 2
    return jnp.where(which == 0, value[:, :half], value[:, half:])


TAIL = 4


def edge_signal(tail, head, taps):
    result = None
    for n, (t0, t1, t2) in enumerate(taps):
        x0, x1 = (head[2 * n + i : 2 * n + i + 1] for i in range(2))
        h0, h1 = (tail[2 * n + i : 2 * n + i + 1] for i in range(2))
        feats = (t0 * x0 + t1 * h1 + t2 * h0, t0 * x1 + t1 * x0 + t2 * h1)
        result = feats if result is None else tuple(a * b for a, b in zip(result, feats))
    return result


def half_taps(taps_ref, core):
    return [[half_of(taps_ref[j, s : s + 1, :], core) for j in range(3)] for s in (1, 2)]


def state_kernel(
    blocks_ref, taps_ref, rates_ref, residues_ref, bias_ref, kept_ref, sent_ref, ends_ref, signal_ref, one, two, full
):
    del residues_ref, bias_ref
    modes, channels = rates_ref.shape
    fill_tokens(blocks_ref, 1, one)
    fill_tokens(blocks_ref, 2, two)
    rows = row_iota()
    step = rows.astype(jnp.float32)
    remaining = (7.0 - step) * (SUB / LENGTH)
    full[modes:, :] = jnp.zeros((SUB, channels), jnp.float32)
    for n, s in enumerate((1, 2)):
        full[modes + 2 * n : modes + 2 * n + 2, :] = blocks_ref[0, s * SUB : (s + 1) * SUB, :].astype(jnp.float32)[:2]
    for n, s in enumerate((1, 2, 0)):
        at = modes + TAIL + 2 * n
        full[at : at + 2, :] = blocks_ref[7, s * SUB : (s + 1) * SUB, :].astype(jnp.float32)[SUB - 2 :]
    for start in range(0, channels, LANES):
        lanes = pl.ds(start, LANES)
        left = featurize(one, 1, lanes, taps_ref)
        right = featurize(two, 2, lanes, taps_ref)
        signal = [a * b for a, b in zip(left, right)]
        for i in range(2):
            signal[i] = jnp.where(rows == 0, 0.0, signal[i])
        for i in range(SUB):
            signal_ref[i, :, lanes] = signal[i]
        for mode in range(modes):
            rate = spread(rates_ref[mode : mode + 1, lanes])
            decay = jnp.exp(rate * (-1.0 / LENGTH))
            state = signal[0]
            for i in range(1, SUB):
                state = state * decay + signal[i]
            ends_ref[mode, :, lanes] = state
            weight = jnp.exp(-rate * remaining)
            full[mode : mode + 1, lanes] = jnp.sum(state * weight, axis=0, keepdims=True)
    core = core_index()
    kept_ref[...] = half_of(full[...], core)
    sent_ref[...] = half_of(full[...], 1 - core)


def pair_kernel(kept_ref, got_ref, rates_ref, taps_ref, out_ref, lower_ref):
    modes = rates_ref.shape[0]
    core = core_index()
    rate = half_of(rates_ref[...], core)
    kept, got = kept_ref[...], got_ref[...]
    lower = jnp.where(core == 0, kept, got)
    upper = jnp.where(core == 0, got, kept)
    low_edge, high_edge = lower[modes:], upper[modes:]
    s0, s1 = edge_signal(low_edge[TAIL:], high_edge, half_taps(taps_ref, core))
    inner = power(rate, BLOCK - 2) * (power(rate, 1) * s0 + s1)
    state = upper[:modes] + inner + power(rate, BLOCK) * lower[:modes]
    rows = lax.broadcasted_iota(jnp.int32, low_edge.shape, 0)
    edge = jnp.where(rows < TAIL, low_edge, high_edge).astype(jnp.bfloat16)
    high = state.astype(jnp.bfloat16)
    rest = (state - high.astype(jnp.float32)).astype(jnp.bfloat16)
    for chip in range(CHIPS):
        out_ref[chip, 0:SUB, :] = high
        out_ref[chip, SUB : 2 * SUB, :] = rest
        out_ref[chip, 2 * SUB : 3 * SUB, :] = edge
    lower_ref[...] = lower


def merge_kernel(every_ref, lower_ref, rates_ref, taps_ref, mine_ref, other_ref):
    modes = rates_ref.shape[0]
    core = core_index()
    chip = lax.div(lax.axis_index("ctx"), 2)
    rate = half_of(rates_ref[...], core)
    taps = half_taps(taps_ref, core)
    single, pair = power(rate, 1), power(rate, 2 * BLOCK)
    last = power(rate, 2 * BLOCK - 2)
    carry = jnp.zeros_like(rate)
    before = jnp.zeros_like(rate)
    halo = jnp.zeros_like(rate)
    first = [jnp.zeros_like(rate[:1])] * 2
    for k in range(CHIPS):
        edge = every_ref[k, 2 * SUB : 3 * SUB, :].astype(jnp.float32)
        pieces = edge_signal(before[TAIL:], edge, taps)
        first = [jnp.where(chip == k, new, old) for new, old in zip(pieces, first)]
        halo = jnp.where(chip == k, before, halo)
        if k < CHIPS - 1:
            state = every_ref[k, 0:SUB, :].astype(jnp.float32) + every_ref[k, SUB : 2 * SUB, :].astype(jnp.float32)
            state = state + last * (single * pieces[0] + pieces[1])
            carry = jnp.where(k < chip, carry * pair + state, carry)
        before = edge
    lower = lower_ref[...]
    inner = power(rate, BLOCK - 2) * (single * first[0] + first[1])
    carries = carry, power(rate, BLOCK) * carry + lower[:modes] + inner
    halos = halo[TAIL : TAIL + 8], lower[modes + TAIL : modes + TAIL + 8]
    for ref, which in ((mine_ref, core), (other_ref, 1 - core)):
        ref[0:modes, :] = jnp.where(which == 0, *carries)
        ref[modes:, :] = jnp.where(which == 0, *halos)


def local_kernel(blocks_ref, taps_ref, rates_ref, residues_ref, bias_ref, ends_ref, signal_ref, local_ref, front_ref, zero):
    modes, channels = rates_ref.shape
    fill_tokens(blocks_ref, 0, zero)
    rows = row_iota()
    step = rows.astype(jnp.float32)
    for start in range(0, channels, LANES):
        lanes = pl.ds(start, LANES)
        front = featurize(zero, 0, lanes, taps_ref)
        for i in range(SUB):
            front_ref[i, :, lanes] = front[i]
        signal = [signal_ref[i, :, lanes] for i in range(SUB)]
        taps = [jnp.zeros((8, LANES), jnp.float32) for _ in range(SUB // 8)]
        for mode in range(modes):
            rate = spread(rates_ref[mode : mode + 1, lanes])
            residue = spread(residues_ref[mode : mode + 1, lanes])
            for part in range(SUB // 8):
                taps[part] = taps[part] + residue * jnp.exp(-rate * ((step + 8.0 * part) * (1.0 / LENGTH)))
        bias = spread(bias_ref[0:1, lanes])
        total = [bias * signal[i] for i in range(SUB)]
        for lag in range(SUB):
            tap = spread(taps[lag // 8][lag % 8 : lag % 8 + 1])
            for i in range(lag, SUB):
                total[i] = total[i] + tap * signal[i - lag]
        for mode in range(modes):
            rate = spread(rates_ref[mode : mode + 1, lanes])
            residue = spread(residues_ref[mode : mode + 1, lanes])
            decay = jnp.exp(rate * (-1.0 / LENGTH))
            state = ends_ref[mode, :, lanes]
            for far in (1, 2, 4):
                state = state + jnp.where(rows >= far, power(rate, far * SUB) * pltpu.roll(state, far, 0), 0.0)
            carried = jnp.where(rows >= 1, pltpu.roll(state, 1, 0), 0.0) * residue
            for i in range(SUB):
                carried = carried * decay
                total[i] = total[i] + carried
        for i in range(SUB):
            local_ref[i, :, lanes] = total[i]


def final_kernel(
    mine_ref, other_ref, blocks_ref, taps_ref, rates_ref, residues_ref, bias_ref, local_ref, front_ref, out_ref, natural
):
    modes, channels = rates_ref.shape
    rows = row_iota()
    step = rows.astype(jnp.float32)
    core = core_index()
    half = channels // 2

    def at_first(row):
        return jnp.where(rows == 0, spread(row), 0.0)

    for start in range(0, channels, LANES):
        lanes = pl.ds(start, LANES)
        within = pl.ds(start % half, LANES)
        got = jnp.where(core == start // half, mine_ref[:, within], other_ref[:, within])
        halo = got[modes:]
        head = [blocks_ref[0, s * SUB : (s + 1) * SUB, lanes].astype(jnp.float32)[:2] for s in (1, 2)]
        taps = [[taps_ref[j, s : s + 1, lanes] for j in range(3)] for s in (1, 2, 0)]
        s0, s1 = edge_signal(halo, jnp.concatenate(head, axis=0), taps[:2])
        _, t1, t2 = taps[2]
        bias = bias_ref[0:1, lanes]
        total = [local_ref[i, :, lanes] for i in range(SUB)]
        front = [front_ref[i, :, lanes] for i in range(SUB)]
        total[0] = total[0] + at_first(bias * s0)
        total[1] = total[1] + at_first(bias * s1)
        front[0] = front[0] + at_first(t1 * halo[5:6] + t2 * halo[4:5])
        front[1] = front[1] + at_first(t2 * halo[5:6])
        for mode in range(modes):
            row = rates_ref[mode : mode + 1, lanes]
            residue = residues_ref[mode : mode + 1, lanes]
            grow = jnp.exp(row * (1.0 / LENGTH))
            rate = spread(row)
            decay = jnp.exp(rate * (-1.0 / LENGTH))
            start_row = spread(residue * (got[mode : mode + 1] + grow * s0))
            later = jnp.where(rows >= 1, spread(residue * (grow * (grow * s1))), 0.0)
            carried = (start_row + later) * jnp.exp(-rate * ((step * SUB + 1.0) * (1.0 / LENGTH)))
            total[0] = total[0] + carried
            carried = carried * decay + at_first(residue * s1)
            total[1] = total[1] + carried
            for i in range(2, SUB):
                carried = carried * decay
                total[i] = total[i] + carried
        for i in range(SUB):
            natural[start // LANES, pl.ds(i, 8, stride=SUB), :] = front[i] * total[i]
        out_ref[:, lanes] = natural[start // LANES].astype(out_ref.dtype)


def body(streams, short_taps, residues, rates, bias):
    parts = lax.axis_size("tp")
    ctx = lax.axis_size("ctx")
    modes, channels = rates.shape
    half = channels // 2
    tokens = SUB * parts
    f32 = jnp.float32
    wide = jax.ShapeDtypeStruct((SUB, parts, channels), f32)
    packed = jax.ShapeDtypeStruct((modes + SUB, half), f32)
    carried = jax.ShapeDtypeStruct((modes + 8, half), f32)
    plane = pltpu.VMEM((channels // LANES, tokens, LANES), f32)
    bias = bias[None]

    def kernel(function, out_shape, operands, scratch=(), cost=None, in_specs=None, limit=24):
        several = isinstance(out_shape, tuple)
        return pl.pallas_call(
            function,
            out_shape=out_shape,
            in_specs=in_specs or [VMEM] * len(operands),
            out_specs=(VMEM,) * len(out_shape) if several else VMEM,
            scratch_shapes=list(scratch),
            compiler_params=pltpu.CompilerParams(vmem_limit_bytes=limit << 20),
            cost_estimate=cost,
            name=function.__name__,
        )(*operands)

    outgoing = kernel(
        gather_kernel,
        jax.ShapeDtypeStruct((parts, 3 * SUB, channels), streams.dtype),
        (jnp.transpose(streams, (1, 0, 2)),),
        [pltpu.SemaphoreType.DMA((3 * parts,))],
        in_specs=[pl.BlockSpec(memory_space=pl.ANY)],
        limit=60,
    )
    blocks = lax.all_to_all(outgoing, "tp", 0, 0, tiled=True)
    kept, sent, ends, signal = kernel(
        state_kernel,
        (packed, packed, jax.ShapeDtypeStruct((modes, parts, channels), f32), wide),
        (blocks, short_taps, rates, residues, bias),
        [plane, plane, pltpu.VMEM((modes + SUB, channels), f32)],
    )
    swap = [(i, i ^ 1) for i in range(ctx)]
    got = lax.ppermute(sent, "ctx", swap)
    every, lower = kernel(
        pair_kernel,
        (jax.ShapeDtypeStruct((CHIPS, 3 * SUB, half), jnp.bfloat16), packed),
        (kept, got, rates, short_taps),
    )
    groups = [[2 * k + c for k in range(CHIPS)] for c in range(2)]
    every = lax.all_to_all(every, "ctx", 0, 0, axis_index_groups=groups, tiled=True)
    mine, other = kernel(merge_kernel, (carried, carried), (every, lower, rates, short_taps))
    other = lax.ppermute(other, "ctx", swap)
    local, front = kernel(
        local_kernel,
        (wide, wide),
        (blocks, short_taps, rates, residues, bias, ends, signal),
        [plane],
        cost=pl.CostEstimate(flops=8 << 20, bytes_accessed=2 << 20, transcendentals=0),
    )
    return kernel(
        final_kernel,
        jax.ShapeDtypeStruct((tokens, channels), jnp.bfloat16),
        (mine, other, blocks, short_taps, rates, residues, bias, local, front),
        [plane],
    )


def solution(mesh):
    in_specs = (
        P(("ctx", "tp"), None, None),
        P(None, None, "tp"),
        P(None, "tp"),
        P(None, "tp"),
        P("tp"),
    )
    out_specs = P("ctx", "tp")
    return jax.shard_map(body, mesh=mesh, in_specs=in_specs, out_specs=out_specs, check_vma=False)
```

```python
import jax
import jax.numpy as jnp
from jax import lax
from jax.experimental import pallas as pl
from jax.experimental.pallas import tpu as pltpu
from jax.sharding import PartitionSpec as P

LENGTH = 4096
SUB = 16
SHIFTS = (4, 1, 3, 5, 2, 6, 7, 0)
LANES = 128
BLOCK = 128
VMEM = pl.BlockSpec(memory_space=pltpu.VMEM)


def row_iota():
    return lax.broadcasted_iota(jnp.int32, (8, LANES), 0)


def spread(row):
    return jnp.broadcast_to(row, (8, LANES))


def fill_tokens(blocks, stream, scratch):
    for block, source in blocks:
        at = pl.multiple_of(source * SUB, SUB)
        for group in range(scratch.shape[0]):
            lanes = pl.ds(group * LANES, LANES)
            scratch[group, pl.ds(at, SUB), :] = block[stream, :, lanes].astype(jnp.float32)


def with_sources(refs):
    me = lax.axis_index("tp")
    return [(ref, lax.rem(me - shift + 8, 8)) for ref, shift in zip(refs, SHIFTS)]


def featurize(scratch, stream, lanes, taps_ref):
    group = lanes.start // LANES
    values = [scratch[group, pl.ds(i, 8, stride=SUB), :] for i in range(SUB)]
    first = row_iota() == 0
    joined = [jnp.where(first, 0.0, pltpu.roll(values[SUB - far], 1, 0)) for far in (2, 1)] + values
    t0, t1, t2 = (spread(taps_ref[j, stream : stream + 1, lanes]) for j in range(3))
    return [t0 * joined[i + 2] + t1 * joined[i + 1] + t2 * joined[i] for i in range(SUB)]


def power(rate, tokens):
    return jnp.exp(rate * (-float(tokens) / LENGTH))


def core_index():
    return lax.rem(lax.axis_index("ctx"), 2)


def half_of(value, which):
    half = value.shape[-1] // 2
    return jnp.where(which == 0, value[:, :half], value[:, half:])


TAIL = 4


def edge_signal(tail, head, taps):
    result = None
    for n, (t0, t1, t2) in enumerate(taps):
        x0, x1 = (head[2 * n + i : 2 * n + i + 1] for i in range(2))
        h0, h1 = (tail[2 * n + i : 2 * n + i + 1] for i in range(2))
        feats = (t0 * x0 + t1 * h1 + t2 * h0, t0 * x1 + t1 * x0 + t2 * h1)
        result = feats if result is None else tuple(a * b for a, b in zip(result, feats))
    return result


def half_taps(taps_ref, core):
    return [[half_of(taps_ref[j, s : s + 1, :], core) for j in range(3)] for s in (1, 2)]


def state_kernel(*refs):
    blocks = with_sources(refs[: len(SHIFTS)])
    taps_ref, rates_ref, _, _, kept_ref, sent_ref, edge_ref, ends_ref, signal_ref, one, two, full = refs[len(SHIFTS) :]
    modes, channels = rates_ref.shape
    fill_tokens(blocks, 1, one)
    fill_tokens(blocks, 2, two)
    rows = row_iota()
    step = rows.astype(jnp.float32)
    remaining = (7.0 - step) * (SUB / LENGTH)
    full[modes:, :] = jnp.zeros((SUB, channels), jnp.float32)
    for group in range(channels // LANES):
        lanes = pl.ds(group * LANES, LANES)
        for n, scratch in enumerate((one, two)):
            full[modes + 2 * n : modes + 2 * n + 2, lanes] = scratch[group, 0:2, :]
            full[modes + TAIL + 2 * n : modes + TAIL + 2 * n + 2, lanes] = scratch[group, BLOCK - 2 : BLOCK, :]
    for block, source in blocks:

        @pl.when(source == 7)
        def _(block=block):
            full[modes + TAIL + 4 : modes + TAIL + 6, :] = block[0].astype(jnp.float32)[SUB - 2 :]

    for start in range(0, channels, LANES):
        lanes = pl.ds(start, LANES)
        left = featurize(one, 1, lanes, taps_ref)
        right = featurize(two, 2, lanes, taps_ref)
        signal = [a * b for a, b in zip(left, right)]
        for i in range(2):
            signal[i] = jnp.where(rows == 0, 0.0, signal[i])
        for i in range(SUB):
            signal_ref[i, :, lanes] = signal[i]
        for mode in range(modes):
            rate = spread(rates_ref[mode : mode + 1, lanes])
            decay = jnp.exp(rate * (-1.0 / LENGTH))
            state = signal[0]
            for i in range(1, SUB):
                state = state * decay + signal[i]
            ends_ref[mode, :, lanes] = state
            weight = jnp.exp(-rate * remaining)
            full[mode : mode + 1, lanes] = jnp.sum(state * weight, axis=0, keepdims=True)
    edge_ref[...] = full[modes:, :]
    core = core_index()
    kept_ref[...] = half_of(full[...], core)
    sent_ref[...] = half_of(full[...], 1 - core)


def pack(state, edge, out_ref):
    high = state.astype(jnp.bfloat16)
    out_ref[0:SUB, :] = high
    out_ref[SUB : 2 * SUB, :] = (state - high.astype(jnp.float32)).astype(jnp.bfloat16)
    out_ref[2 * SUB : 3 * SUB, :] = edge.astype(jnp.bfloat16)


def join_edges(first, last):
    rows = lax.broadcasted_iota(jnp.int32, first.shape, 0)
    return jnp.where(rows < TAIL, first, last)


def pair_kernel(kept_ref, got_ref, rates_ref, taps_ref, out_ref, lower_ref):
    modes = rates_ref.shape[0]
    core = core_index()
    rate = half_of(rates_ref[...], core)
    kept, got = kept_ref[...], got_ref[...]
    lower = jnp.where(core == 0, kept, got)
    upper = jnp.where(core == 0, got, kept)
    s0, s1 = edge_signal(lower[modes + TAIL :], upper[modes:], half_taps(taps_ref, core))
    inner = power(rate, BLOCK - 2) * (power(rate, 1) * s0 + s1)
    state = upper[:modes] + inner + power(rate, BLOCK) * lower[:modes]
    pack(state, join_edges(lower[modes:], upper[modes:]), out_ref)
    lower_ref[...] = lower


def chain(refs, place, tokens, rate, taps, opened):
    single, whole, last = power(rate, 1), power(rate, tokens), power(rate, tokens - 2)
    size = len(refs)
    carry = halo = before = total = jnp.zeros_like(rate)
    first = (jnp.zeros_like(rate[:1]),) * 2
    head = None
    for k in range(size):
        piece = refs[0][...]
        for by in range(1, size):
            piece = jnp.where(lax.rem(place - k + size, size) == by, refs[by][...], piece)
        state = piece[0:SUB].astype(jnp.float32) + piece[SUB : 2 * SUB].astype(jnp.float32)
        edge = piece[2 * SUB :].astype(jnp.float32)
        pieces = edge_signal(before[TAIL:], edge, taps)
        carry = jnp.where(place == k, total, carry)
        halo = jnp.where(place == k, before, halo)
        first = [jnp.where(place == k, new, old) for new, old in zip(pieces, first)]
        inner = last * (single * pieces[0] + pieces[1])
        if k == 0:
            head = edge
            total = state + inner if opened else state
        else:
            total = total * whole + state + inner
        before = edge
    return carry, first, halo, total, join_edges(head, before)


def place_of(stride):
    return lax.rem(lax.div(lax.axis_index("ctx"), stride), 4)


def row_kernel(own_ref, one_ref, three_ref, two_ref, rates_ref, taps_ref, out_ref, inside_ref):
    modes = rates_ref.shape[0]
    core = core_index()
    rate = half_of(rates_ref[...], core)
    refs = (own_ref, one_ref, two_ref, three_ref)
    carry, first, halo, total, edges = chain(refs, place_of(2), 2 * BLOCK, rate, half_taps(taps_ref, core), False)
    pack(total, edges, out_ref)
    inside_ref[0:modes, :] = carry
    inside_ref[modes : 2 * modes, :] = halo
    for i in range(2):
        inside_ref[2 * modes + i : 2 * modes + i + 1, :] = first[i]


def merge_kernel(
    own_ref, one_ref, three_ref, two_ref, inside_ref, lower_ref, rates_ref, taps_ref, mine_ref, other_ref
):
    modes = rates_ref.shape[0]
    core = core_index()
    column, line = place_of(2), place_of(8)
    rate = half_of(rates_ref[...], core)
    refs = (own_ref, one_ref, two_ref, three_ref)
    taps = half_taps(taps_ref, core)
    single = power(rate, 1)
    above, first, halo, _, _ = chain(refs, line, 8 * BLOCK, rate, taps, True)
    steps = (column * (2 * BLOCK)).astype(jnp.float32) * (-1.0 / LENGTH)
    behind = (column * (2 * BLOCK) - 2).astype(jnp.float32) * (-1.0 / LENGTH)
    inside = inside_ref[0:modes, :]
    opened = inside + jnp.exp(rate * behind) * (single * first[0] + first[1])
    carry = jnp.exp(rate * steps) * above + jnp.where(column > 0, opened, inside)
    within = [inside_ref[2 * modes + i : 2 * modes + i + 1, :] for i in range(2)]
    first = [jnp.where(column > 0, a, b) for a, b in zip(within, first)]
    halo = jnp.where(column > 0, inside_ref[modes : 2 * modes, :], halo)
    lower = lower_ref[...]
    inner = power(rate, BLOCK - 2) * (single * first[0] + first[1])
    carries = carry, power(rate, BLOCK) * carry + lower[:modes] + inner
    halos = halo[TAIL : TAIL + 8], lower[modes + TAIL : modes + TAIL + 8]
    for ref, which in ((mine_ref, core), (other_ref, 1 - core)):
        ref[0:modes, :] = jnp.where(which == 0, *carries)
        ref[modes:, :] = jnp.where(which == 0, *halos)


def local_kernel(*refs):
    blocks = with_sources(refs[: len(SHIFTS)])
    taps_ref, rates_ref, residues_ref, bias_ref, ends_ref, signal_ref, local_ref, front_ref, zero = refs[len(SHIFTS) :]
    modes, channels = rates_ref.shape
    fill_tokens(blocks, 0, zero)
    rows = row_iota()
    step = rows.astype(jnp.float32)
    for start in range(0, channels, LANES):
        lanes = pl.ds(start, LANES)
        front = featurize(zero, 0, lanes, taps_ref)
        for i in range(SUB):
            front_ref[i, :, lanes] = front[i]
        signal = [signal_ref[i, :, lanes] for i in range(SUB)]
        taps = [jnp.zeros((8, LANES), jnp.float32) for _ in range(SUB // 8)]
        for mode in range(modes):
            rate = spread(rates_ref[mode : mode + 1, lanes])
            residue = spread(residues_ref[mode : mode + 1, lanes])
            for part in range(SUB // 8):
                taps[part] = taps[part] + residue * jnp.exp(-rate * ((step + 8.0 * part) * (1.0 / LENGTH)))
        bias = spread(bias_ref[0:1, lanes])
        total = [bias * signal[i] for i in range(SUB)]
        for lag in range(SUB):
            tap = spread(taps[lag // 8][lag % 8 : lag % 8 + 1])
            for i in range(lag, SUB):
                total[i] = total[i] + tap * signal[i - lag]
        for mode in range(modes):
            rate = spread(rates_ref[mode : mode + 1, lanes])
            residue = spread(residues_ref[mode : mode + 1, lanes])
            decay = jnp.exp(rate * (-1.0 / LENGTH))
            state = ends_ref[mode, :, lanes]
            for far in (1, 2, 4):
                state = state + jnp.where(rows >= far, power(rate, far * SUB) * pltpu.roll(state, far, 0), 0.0)
            carried = jnp.where(rows >= 1, pltpu.roll(state, 1, 0), 0.0) * residue
            for i in range(SUB):
                carried = carried * decay
                total[i] = total[i] + carried
        for i in range(SUB):
            local_ref[i, :, lanes] = total[i]


def final_kernel(
    mine_ref, other_ref, edge_ref, taps_ref, rates_ref, residues_ref, bias_ref, local_ref, front_ref, out_ref, natural
):
    modes, channels = rates_ref.shape
    rows = row_iota()
    step = rows.astype(jnp.float32)
    core = core_index()
    half = channels // 2

    def at_first(row):
        return jnp.where(rows == 0, spread(row), 0.0)

    for start in range(0, channels, LANES):
        lanes = pl.ds(start, LANES)
        within = pl.ds(start % half, LANES)
        got = jnp.where(core == start // half, mine_ref[:, within], other_ref[:, within])
        halo = got[modes:]
        taps = [[taps_ref[j, s : s + 1, lanes] for j in range(3)] for s in (1, 2, 0)]
        s0, s1 = edge_signal(halo, edge_ref[:, lanes], taps[:2])
        _, t1, t2 = taps[2]
        bias = bias_ref[0:1, lanes]
        total = [local_ref[i, :, lanes] for i in range(SUB)]
        front = [front_ref[i, :, lanes] for i in range(SUB)]
        total[0] = total[0] + at_first(bias * s0)
        total[1] = total[1] + at_first(bias * s1)
        front[0] = front[0] + at_first(t1 * halo[5:6] + t2 * halo[4:5])
        front[1] = front[1] + at_first(t2 * halo[5:6])
        for mode in range(modes):
            row = rates_ref[mode : mode + 1, lanes]
            residue = residues_ref[mode : mode + 1, lanes]
            grow = jnp.exp(row * (1.0 / LENGTH))
            rate = spread(row)
            decay = jnp.exp(rate * (-1.0 / LENGTH))
            start_row = spread(residue * (got[mode : mode + 1] + grow * s0))
            later = jnp.where(rows >= 1, spread(residue * (grow * (grow * s1))), 0.0)
            carried = (start_row + later) * jnp.exp(-rate * ((step * SUB + 1.0) * (1.0 / LENGTH)))
            total[0] = total[0] + carried
            carried = carried * decay + at_first(residue * s1)
            total[1] = total[1] + carried
            for i in range(2, SUB):
                carried = carried * decay
                total[i] = total[i] + carried
        for i in range(SUB):
            natural[start // LANES, pl.ds(i, 8, stride=SUB), :] = front[i] * total[i]
        out_ref[:, lanes] = natural[start // LANES].astype(out_ref.dtype)


def body(streams, short_taps, residues, rates, bias):
    parts = lax.axis_size("tp")
    ctx = lax.axis_size("ctx")
    modes, channels = rates.shape
    half = channels // 2
    tokens = SUB * parts
    f32 = jnp.float32
    wide = jax.ShapeDtypeStruct((SUB, parts, channels), f32)
    packed = jax.ShapeDtypeStruct((modes + SUB, half), f32)
    carried = jax.ShapeDtypeStruct((modes + 8, half), f32)
    plane = pltpu.VMEM((channels // LANES, tokens, LANES), f32)
    bias = bias[None]

    def kernel(function, out_shape, operands, scratch=(), cost=None, in_specs=None, limit=24):
        several = isinstance(out_shape, tuple)
        return pl.pallas_call(
            function,
            out_shape=out_shape,
            in_specs=in_specs or [VMEM] * len(operands),
            out_specs=(VMEM,) * len(out_shape) if several else VMEM,
            scratch_shapes=list(scratch),
            compiler_params=pltpu.CompilerParams(vmem_limit_bytes=limit << 20),
            cost_estimate=cost,
            name=function.__name__,
        )(*operands)

    by_stream = jnp.transpose(streams, (1, 0, 2))
    blocks = []
    for shift in SHIFTS:
        at = ((lax.axis_index("tp") + shift) % parts) * channels
        block = lax.dynamic_slice(by_stream, (0, 0, at), (3, SUB, channels))
        blocks.append(lax.ppermute(block, "tp", [(i, (i + shift) % parts) for i in range(parts)]) if shift else block)
    kept, sent, edges, ends, signal = kernel(
        state_kernel,
        (
            packed,
            packed,
            jax.ShapeDtypeStruct((SUB, channels), f32),
            jax.ShapeDtypeStruct((modes, parts, channels), f32),
            wide,
        ),
        (*blocks, short_taps, rates, residues, bias),
        [plane, plane, pltpu.VMEM((modes + SUB, channels), f32)],
    )
    swap = [(i, i ^ 1) for i in range(ctx)]
    got = lax.ppermute(sent, "ctx", swap)
    group = jax.ShapeDtypeStruct((3 * SUB, half), jnp.bfloat16)

    def around(value, stride):
        parts = {}
        for by in (3, 1, 2):
            route = [(i, i + ((i // stride + by) % 4 - i // stride % 4) * stride) for i in range(ctx)]
            parts[by] = lax.ppermute(value, "ctx", route)
        return parts[1], parts[3], parts[2]

    pair, lower = kernel(pair_kernel, (group, packed), (kept, got, rates, short_taps))
    row, inside = kernel(
        row_kernel,
        (group, jax.ShapeDtypeStruct((2 * modes + 8, half), f32)),
        (pair, *around(pair, 2), rates, short_taps),
    )
    mine, other = kernel(
        merge_kernel, (carried, carried), (row, *around(row, 8), inside, lower, rates, short_taps)
    )
    other = lax.ppermute(other, "ctx", swap)
    local, front = kernel(
        local_kernel,
        (wide, wide),
        (*blocks, short_taps, rates, residues, bias, ends, signal),
        [plane],
        cost=pl.CostEstimate(flops=8 << 20, bytes_accessed=2 << 20, transcendentals=0),
    )
    return kernel(
        final_kernel,
        jax.ShapeDtypeStruct((tokens, channels), jnp.bfloat16),
        (mine, other, edges, short_taps, rates, residues, bias, local, front),
        [plane],
    )


def solution(mesh):
    in_specs = (
        P(("ctx", "tp"), None, None),
        P(None, None, "tp"),
        P(None, "tp"),
        P(None, "tp"),
        P("tp"),
    )
    out_specs = P("ctx", "tp")
    return jax.shard_map(body, mesh=mesh, in_specs=in_specs, out_specs=out_specs, check_vma=False)
```

```python
import jax
import jax.numpy as jnp
from jax import lax
from jax.experimental import pallas as pl
from jax.experimental.pallas import tpu as pltpu
from jax.sharding import PartitionSpec as P

LENGTH = 4096
SUB = 16
SHIFTS = (1, 6, 2, 5, 3, 4, 7, 0)
LANES = 128
BLOCK = 128
VMEM = pl.BlockSpec(memory_space=pltpu.VMEM)


def row_iota():
    return lax.broadcasted_iota(jnp.int32, (8, LANES), 0)


def spread(row):
    return jnp.broadcast_to(row, (8, LANES))


def fill_tokens(blocks, stream, scratch):
    for block, source in blocks:
        at = pl.multiple_of(source * SUB, SUB)
        for group in range(scratch.shape[0]):
            lanes = pl.ds(group * LANES, LANES)
            scratch[group, pl.ds(at, SUB), :] = block[stream, :, lanes].astype(jnp.float32)


def with_sources(refs):
    me = lax.axis_index("tp")
    return [(ref, lax.rem(me - shift + 8, 8)) for ref, shift in zip(refs, SHIFTS)]


def featurize(scratch, stream, lanes, taps_ref):
    group = lanes.start // LANES
    values = [scratch[group, pl.ds(i, 8, stride=SUB), :] for i in range(SUB)]
    first = row_iota() == 0
    joined = [jnp.where(first, 0.0, pltpu.roll(values[SUB - far], 1, 0)) for far in (2, 1)] + values
    t0, t1, t2 = (spread(taps_ref[j, stream : stream + 1, lanes]) for j in range(3))
    return [t0 * joined[i + 2] + t1 * joined[i + 1] + t2 * joined[i] for i in range(SUB)]


def power(rate, tokens):
    return jnp.exp(rate * (-float(tokens) / LENGTH))


def core_index():
    return lax.rem(lax.axis_index("ctx"), 2)


TAIL = 4


def edge_signal(tail, head, taps):
    result = None
    for n, (t0, t1, t2) in enumerate(taps):
        x0, x1 = (head[2 * n + i : 2 * n + i + 1] for i in range(2))
        h0, h1 = (tail[2 * n + i : 2 * n + i + 1] for i in range(2))
        feats = (t0 * x0 + t1 * h1 + t2 * h0, t0 * x1 + t1 * x0 + t2 * h1)
        result = feats if result is None else tuple(a * b for a, b in zip(result, feats))
    return result


def edge_taps(taps_ref):
    return [[taps_ref[j, s : s + 1, :] for j in range(3)] for s in (1, 2)]


def state_kernel(*refs):
    blocks = with_sources(refs[: len(SHIFTS)])
    taps_ref, rates_ref, _, _, full, ends_ref, signal_ref, one, two = refs[len(SHIFTS) :]
    modes, channels = rates_ref.shape
    fill_tokens(blocks, 1, one)
    fill_tokens(blocks, 2, two)
    rows = row_iota()
    step = rows.astype(jnp.float32)
    remaining = (7.0 - step) * (SUB / LENGTH)
    full[modes:, :] = jnp.zeros((SUB, channels), jnp.float32)
    for group in range(channels // LANES):
        lanes = pl.ds(group * LANES, LANES)
        for n, scratch in enumerate((one, two)):
            full[modes + 2 * n : modes + 2 * n + 2, lanes] = scratch[group, 0:2, :]
            full[modes + TAIL + 2 * n : modes + TAIL + 2 * n + 2, lanes] = scratch[group, BLOCK - 2 : BLOCK, :]
    for block, source in blocks:

        @pl.when(source == 7)
        def _(block=block):
            full[modes + TAIL + 4 : modes + TAIL + 6, :] = block[0].astype(jnp.float32)[SUB - 2 :]

    for start in range(0, channels, LANES):
        lanes = pl.ds(start, LANES)
        left = featurize(one, 1, lanes, taps_ref)
        right = featurize(two, 2, lanes, taps_ref)
        signal = [a * b for a, b in zip(left, right)]
        for i in range(2):
            signal[i] = jnp.where(rows == 0, 0.0, signal[i])
        for i in range(SUB):
            signal_ref[i, :, lanes] = signal[i]
        for mode in range(modes):
            rate = spread(rates_ref[mode : mode + 1, lanes])
            decay = jnp.exp(rate * (-1.0 / LENGTH))
            state = signal[0]
            for i in range(1, SUB):
                state = state * decay + signal[i]
            ends_ref[mode, :, lanes] = state
            weight = jnp.exp(-rate * remaining)
            full[mode : mode + 1, lanes] = jnp.sum(state * weight, axis=0, keepdims=True)


def pack(state, edge, out_ref):
    high = state.astype(jnp.bfloat16)
    out_ref[0:SUB, :] = high
    out_ref[SUB : 2 * SUB, :] = (state - high.astype(jnp.float32)).astype(jnp.bfloat16)
    out_ref[2 * SUB : 3 * SUB, :] = edge.astype(jnp.bfloat16)


def join_edges(first, last):
    rows = lax.broadcasted_iota(jnp.int32, first.shape, 0)
    return jnp.where(rows < TAIL, first, last)


def pair_kernel(kept_ref, got_ref, rates_ref, taps_ref, out_ref, lower_ref):
    modes = rates_ref.shape[0]
    core = core_index()
    rate = rates_ref[...]
    kept, got = kept_ref[...], got_ref[...]
    lower = jnp.where(core == 0, kept, got)
    upper = jnp.where(core == 0, got, kept)
    s0, s1 = edge_signal(lower[modes + TAIL :], upper[modes:], edge_taps(taps_ref))
    inner = power(rate, BLOCK - 2) * (power(rate, 1) * s0 + s1)
    state = upper[:modes] + inner + power(rate, BLOCK) * lower[:modes]
    pack(state, join_edges(lower[modes:], upper[modes:]), out_ref)
    lower_ref[...] = lower


def chain(refs, place, tokens, rate, taps, opened):
    single, whole, last = power(rate, 1), power(rate, tokens), power(rate, tokens - 2)
    size = len(refs)
    carry = halo = before = total = jnp.zeros_like(rate)
    first = (jnp.zeros_like(rate[:1]),) * 2
    head = None
    for k in range(size):
        piece = refs[0][...]
        for by in range(1, size):
            piece = jnp.where(lax.rem(place - k + size, size) == by, refs[by][...], piece)
        state = piece[0:SUB].astype(jnp.float32) + piece[SUB : 2 * SUB].astype(jnp.float32)
        edge = piece[2 * SUB :].astype(jnp.float32)
        pieces = edge_signal(before[TAIL:], edge, taps)
        carry = jnp.where(place == k, total, carry)
        halo = jnp.where(place == k, before, halo)
        first = [jnp.where(place == k, new, old) for new, old in zip(pieces, first)]
        inner = last * (single * pieces[0] + pieces[1])
        if k == 0:
            head = edge
            total = state + inner if opened else state
        else:
            total = total * whole + state + inner
        before = edge
    return carry, first, halo, total, join_edges(head, before)


def place_of(stride):
    return lax.rem(lax.div(lax.axis_index("ctx"), stride), 4)


def row_kernel(own_ref, one_ref, three_ref, two_ref, rates_ref, taps_ref, out_ref, inside_ref):
    modes = rates_ref.shape[0]
    rate = rates_ref[...]
    refs = (own_ref, one_ref, two_ref, three_ref)
    carry, first, halo, total, edges = chain(refs, place_of(2), 2 * BLOCK, rate, edge_taps(taps_ref), False)
    pack(total, edges, out_ref)
    inside_ref[0:modes, :] = carry
    inside_ref[modes : 2 * modes, :] = halo
    for i in range(2):
        inside_ref[2 * modes + i : 2 * modes + i + 1, :] = first[i]


def merge_kernel(
    own_ref, one_ref, three_ref, two_ref, inside_ref, lower_ref, rates_ref, taps_ref, out_ref
):
    modes = rates_ref.shape[0]
    core = core_index()
    column, line = place_of(2), place_of(8)
    rate = rates_ref[...]
    refs = (own_ref, one_ref, two_ref, three_ref)
    taps = edge_taps(taps_ref)
    single = power(rate, 1)
    above, first, halo, _, _ = chain(refs, line, 8 * BLOCK, rate, taps, True)
    steps = (column * (2 * BLOCK)).astype(jnp.float32) * (-1.0 / LENGTH)
    behind = (column * (2 * BLOCK) - 2).astype(jnp.float32) * (-1.0 / LENGTH)
    inside = inside_ref[0:modes, :]
    opened = inside + jnp.exp(rate * behind) * (single * first[0] + first[1])
    carry = jnp.exp(rate * steps) * above + jnp.where(column > 0, opened, inside)
    within = [inside_ref[2 * modes + i : 2 * modes + i + 1, :] for i in range(2)]
    first = [jnp.where(column > 0, a, b) for a, b in zip(within, first)]
    halo = jnp.where(column > 0, inside_ref[modes : 2 * modes, :], halo)
    lower = lower_ref[...]
    inner = power(rate, BLOCK - 2) * (single * first[0] + first[1])
    carries = carry, power(rate, BLOCK) * carry + lower[:modes] + inner
    halos = halo[TAIL : TAIL + 8], lower[modes + TAIL : modes + TAIL + 8]
    out_ref[0:modes, :] = jnp.where(core == 0, *carries)
    out_ref[modes:, :] = jnp.where(core == 0, *halos)


def local_kernel(*refs):
    blocks = with_sources(refs[: len(SHIFTS)])
    taps_ref, rates_ref, residues_ref, bias_ref, ends_ref, signal_ref, local_ref, front_ref, zero = refs[len(SHIFTS) :]
    modes, channels = rates_ref.shape
    fill_tokens(blocks, 0, zero)
    rows = row_iota()
    step = rows.astype(jnp.float32)
    for start in range(0, channels, LANES):
        lanes = pl.ds(start, LANES)
        front = featurize(zero, 0, lanes, taps_ref)
        for i in range(SUB):
            front_ref[i, :, lanes] = front[i]
        signal = [signal_ref[i, :, lanes] for i in range(SUB)]
        taps = [jnp.zeros((8, LANES), jnp.float32) for _ in range(SUB // 8)]
        for mode in range(modes):
            rate = spread(rates_ref[mode : mode + 1, lanes])
            residue = spread(residues_ref[mode : mode + 1, lanes])
            for part in range(SUB // 8):
                taps[part] = taps[part] + residue * jnp.exp(-rate * ((step + 8.0 * part) * (1.0 / LENGTH)))
        bias = spread(bias_ref[0:1, lanes])
        total = [bias * signal[i] for i in range(SUB)]
        for lag in range(SUB):
            tap = spread(taps[lag // 8][lag % 8 : lag % 8 + 1])
            for i in range(lag, SUB):
                total[i] = total[i] + tap * signal[i - lag]
        for mode in range(modes):
            rate = spread(rates_ref[mode : mode + 1, lanes])
            residue = spread(residues_ref[mode : mode + 1, lanes])
            decay = jnp.exp(rate * (-1.0 / LENGTH))
            state = ends_ref[mode, :, lanes]
            for far in (1, 2, 4):
                state = state + jnp.where(rows >= far, power(rate, far * SUB) * pltpu.roll(state, far, 0), 0.0)
            carried = jnp.where(rows >= 1, pltpu.roll(state, 1, 0), 0.0) * residue
            for i in range(SUB):
                carried = carried * decay
                total[i] = total[i] + carried
        for i in range(SUB):
            local_ref[i, :, lanes] = total[i]


def final_kernel(
    carry_ref, summary_ref, taps_ref, rates_ref, residues_ref, bias_ref, local_ref, front_ref, out_ref, natural
):
    modes, channels = rates_ref.shape
    rows = row_iota()
    step = rows.astype(jnp.float32)

    def at_first(row):
        return jnp.where(rows == 0, spread(row), 0.0)

    for start in range(0, channels, LANES):
        lanes = pl.ds(start, LANES)
        got = carry_ref[:, lanes]
        halo = got[modes:]
        taps = [[taps_ref[j, s : s + 1, lanes] for j in range(3)] for s in (1, 2, 0)]
        s0, s1 = edge_signal(halo, summary_ref[modes:, lanes], taps[:2])
        _, t1, t2 = taps[2]
        bias = bias_ref[0:1, lanes]
        total = [local_ref[i, :, lanes] for i in range(SUB)]
        front = [front_ref[i, :, lanes] for i in range(SUB)]
        total[0] = total[0] + at_first(bias * s0)
        total[1] = total[1] + at_first(bias * s1)
        front[0] = front[0] + at_first(t1 * halo[5:6] + t2 * halo[4:5])
        front[1] = front[1] + at_first(t2 * halo[5:6])
        for mode in range(modes):
            row = rates_ref[mode : mode + 1, lanes]
            residue = residues_ref[mode : mode + 1, lanes]
            grow = jnp.exp(row * (1.0 / LENGTH))
            rate = spread(row)
            decay = jnp.exp(rate * (-1.0 / LENGTH))
            start_row = spread(residue * (got[mode : mode + 1] + grow * s0))
            later = jnp.where(rows >= 1, spread(residue * (grow * (grow * s1))), 0.0)
            carried = (start_row + later) * jnp.exp(-rate * ((step * SUB + 1.0) * (1.0 / LENGTH)))
            total[0] = total[0] + carried
            carried = carried * decay + at_first(residue * s1)
            total[1] = total[1] + carried
            for i in range(2, SUB):
                carried = carried * decay
                total[i] = total[i] + carried
        for i in range(SUB):
            natural[start // LANES, pl.ds(i, 8, stride=SUB), :] = front[i] * total[i]
        out_ref[:, lanes] = natural[start // LANES].astype(out_ref.dtype)


def body(streams, short_taps, residues, rates, bias):
    parts = lax.axis_size("tp")
    ctx = lax.axis_size("ctx")
    modes, channels = rates.shape
    tokens = SUB * parts
    f32 = jnp.float32
    wide = jax.ShapeDtypeStruct((SUB, parts, channels), f32)
    packed = jax.ShapeDtypeStruct((modes + SUB, channels), f32)
    carried = jax.ShapeDtypeStruct((modes + 8, channels), f32)
    plane = pltpu.VMEM((channels // LANES, tokens, LANES), f32)
    bias = bias[None]

    def kernel(function, out_shape, operands, scratch=(), cost=None, in_specs=None, limit=24):
        several = isinstance(out_shape, tuple)
        return pl.pallas_call(
            function,
            out_shape=out_shape,
            in_specs=in_specs or [VMEM] * len(operands),
            out_specs=(VMEM,) * len(out_shape) if several else VMEM,
            scratch_shapes=list(scratch),
            compiler_params=pltpu.CompilerParams(vmem_limit_bytes=limit << 20),
            cost_estimate=cost,
            name=function.__name__,
        )(*operands)

    by_stream = jnp.transpose(streams, (1, 0, 2))
    blocks = []
    for shift in SHIFTS:
        at = ((lax.axis_index("tp") + shift) % parts) * channels
        block = lax.dynamic_slice(by_stream, (0, 0, at), (3, SUB, channels))
        blocks.append(lax.ppermute(block, "tp", [(i, (i + shift) % parts) for i in range(parts)]) if shift else block)
    summary, ends, signal = kernel(
        state_kernel,
        (packed, jax.ShapeDtypeStruct((modes, parts, channels), f32), wide),
        (*blocks, short_taps, rates, residues, bias),
        [plane, plane],
    )
    got = lax.ppermute(summary, "ctx", [(i, i ^ 1) for i in range(ctx)])
    group = jax.ShapeDtypeStruct((3 * SUB, channels), jnp.bfloat16)

    def around(value, stride):
        parts = {}
        for by in (3, 1, 2):
            route = [(i, i + ((i // stride + by) % 4 - i // stride % 4) * stride) for i in range(ctx)]
            parts[by] = lax.ppermute(value, "ctx", route)
        return parts[1], parts[3], parts[2]

    pair, lower = kernel(pair_kernel, (group, packed), (summary, got, rates, short_taps))
    row, inside = kernel(
        row_kernel,
        (group, jax.ShapeDtypeStruct((2 * modes + 8, channels), f32)),
        (pair, *around(pair, 2), rates, short_taps),
    )
    carry = kernel(merge_kernel, carried, (row, *around(row, 8), inside, lower, rates, short_taps))
    local, front = kernel(
        local_kernel,
        (wide, wide),
        (*blocks, short_taps, rates, residues, bias, ends, signal),
        [plane],
        cost=pl.CostEstimate(flops=8 << 20, bytes_accessed=2 << 20, transcendentals=0),
    )
    return kernel(
        final_kernel,
        jax.ShapeDtypeStruct((tokens, channels), jnp.bfloat16),
        (carry, summary, short_taps, rates, residues, bias, local, front),
        [plane],
    )


def solution(mesh):
    in_specs = (
        P(("ctx", "tp"), None, None),
        P(None, None, "tp"),
        P(None, "tp"),
        P(None, "tp"),
        P("tp"),
    )
    out_specs = P("ctx", "tp")
    return jax.shard_map(body, mesh=mesh, in_specs=in_specs, out_specs=out_specs, check_vma=False)
```

```python
import functools

import jax
import jax.numpy as jnp
from jax import lax
from jax.experimental import pallas as pl
from jax.experimental.pallas import tpu as pltpu
from jax.sharding import PartitionSpec as P

LENGTH = 4096
SUB = 16
PIECES = 6
LANES = 128
BLOCK = 128
VMEM = pl.BlockSpec(memory_space=pltpu.VMEM)


def row_iota():
    return lax.broadcasted_iota(jnp.int32, (8, LANES), 0)


def spread(row):
    return jnp.broadcast_to(row, (8, LANES))


def fill_tokens(blocks, stream, scratch):
    for block, source in blocks:
        at = pl.multiple_of(source * SUB, SUB)
        for group in range(scratch.shape[0]):
            lanes = pl.ds(group * LANES, LANES)
            scratch[group, pl.ds(at, SUB), :] = block[stream, :, lanes].astype(jnp.float32)


def join_kernel(at, own_ref, passed_ref, *refs):
    out_ref = refs[-1]
    out_ref[0] = own_ref[...]
    out_ref[1] = passed_ref[at]


def back_kernel(third_ref, second_ref, first_ref, out_ref):
    for at, ref in enumerate((first_ref, second_ref, third_ref)):
        out_ref[at] = ref[1]


def with_sources(refs):
    far, third, second, first, back, own = refs
    me = lax.axis_index("tp")
    turn = 1 - 2 * core_index()
    places = [(own, 0), (far, 4), (first.at[0], 1), (second.at[0], 2), (third.at[0], 3)]
    places += [(back.at[k - 1], -k) for k in (1, 2, 3)]
    return [(ref, lax.rem(me - turn * shift + 8, 8)) for ref, shift in places]


def featurize(scratch, stream, lanes, taps_ref):
    group = lanes.start // LANES
    values = [scratch[group, pl.ds(i, 8, stride=SUB), :] for i in range(SUB)]
    first = row_iota() == 0
    joined = [jnp.where(first, 0.0, pltpu.roll(values[SUB - far], 1, 0)) for far in (2, 1)] + values
    t0, t1, t2 = (spread(taps_ref[j, stream : stream + 1, lanes]) for j in range(3))
    return [t0 * joined[i + 2] + t1 * joined[i + 1] + t2 * joined[i] for i in range(SUB)]


def power(rate, tokens):
    return jnp.exp(rate * (-float(tokens) / LENGTH))


def core_index():
    return lax.rem(lax.axis_index("ctx"), 2)


TAIL = 4


def edge_signal(tail, head, taps):
    result = None
    for n, (t0, t1, t2) in enumerate(taps):
        x0, x1 = (head[2 * n + i : 2 * n + i + 1] for i in range(2))
        h0, h1 = (tail[2 * n + i : 2 * n + i + 1] for i in range(2))
        feats = (t0 * x0 + t1 * h1 + t2 * h0, t0 * x1 + t1 * x0 + t2 * h1)
        result = feats if result is None else tuple(a * b for a, b in zip(result, feats))
    return result


def edge_taps(taps_ref):
    return [[taps_ref[j, s : s + 1, :] for j in range(3)] for s in (1, 2)]


def state_kernel(*refs):
    blocks = with_sources(refs[: PIECES])
    taps_ref, rates_ref, _, _, full, ends_ref, signal_ref, one, two = refs[PIECES :]
    modes, channels = rates_ref.shape
    fill_tokens(blocks, 1, one)
    fill_tokens(blocks, 2, two)
    rows = row_iota()
    step = rows.astype(jnp.float32)
    remaining = (7.0 - step) * (SUB / LENGTH)
    full[modes:, :] = jnp.zeros((SUB, channels), jnp.float32)
    for group in range(channels // LANES):
        lanes = pl.ds(group * LANES, LANES)
        for n, scratch in enumerate((one, two)):
            full[modes + 2 * n : modes + 2 * n + 2, lanes] = scratch[group, 0:2, :]
            full[modes + TAIL + 2 * n : modes + TAIL + 2 * n + 2, lanes] = scratch[group, BLOCK - 2 : BLOCK, :]
    for block, source in blocks:

        @pl.when(source == 7)
        def _(block=block):
            full[modes + TAIL + 4 : modes + TAIL + 6, :] = block[0].astype(jnp.float32)[SUB - 2 :]

    for start in range(0, channels, LANES):
        lanes = pl.ds(start, LANES)
        left = featurize(one, 1, lanes, taps_ref)
        right = featurize(two, 2, lanes, taps_ref)
        signal = [a * b for a, b in zip(left, right)]
        for i in range(2):
            signal[i] = jnp.where(rows == 0, 0.0, signal[i])
        for i in range(SUB):
            signal_ref[i, :, lanes] = signal[i]
        for mode in range(modes):
            rate = spread(rates_ref[mode : mode + 1, lanes])
            decay = jnp.exp(rate * (-1.0 / LENGTH))
            state = signal[0]
            for i in range(1, SUB):
                state = state * decay + signal[i]
            ends_ref[mode, :, lanes] = state
            weight = jnp.exp(-rate * remaining)
            full[mode : mode + 1, lanes] = jnp.sum(state * weight, axis=0, keepdims=True)


def pack(state, edge, out_ref):
    high = state.astype(jnp.bfloat16)
    out_ref[0:SUB, :] = high
    out_ref[SUB : 2 * SUB, :] = (state - high.astype(jnp.float32)).astype(jnp.bfloat16)
    out_ref[2 * SUB : 3 * SUB, :] = edge.astype(jnp.bfloat16)


def join_edges(first, last):
    rows = lax.broadcasted_iota(jnp.int32, first.shape, 0)
    return jnp.where(rows < TAIL, first, last)


def pair_kernel(kept_ref, got_ref, rates_ref, taps_ref, out_ref, lower_ref):
    modes = rates_ref.shape[0]
    core = core_index()
    rate = rates_ref[...]
    kept, got = kept_ref[...], got_ref[...]
    lower = jnp.where(core == 0, kept, got)
    upper = jnp.where(core == 0, got, kept)
    s0, s1 = edge_signal(lower[modes + TAIL :], upper[modes:], edge_taps(taps_ref))
    inner = power(rate, BLOCK - 2) * (power(rate, 1) * s0 + s1)
    state = upper[:modes] + inner + power(rate, BLOCK) * lower[:modes]
    pack(state, join_edges(lower[modes:], upper[modes:]), out_ref)
    lower_ref[...] = lower


def chain(refs, place, tokens, rate, taps, opened):
    single, whole, last = power(rate, 1), power(rate, tokens), power(rate, tokens - 2)
    size = len(refs)
    carry = halo = before = total = jnp.zeros_like(rate)
    first = (jnp.zeros_like(rate[:1]),) * 2
    head = None
    for k in range(size):
        piece = refs[0][...]
        for by in range(1, size):
            piece = jnp.where(lax.rem(place - k + size, size) == by, refs[by][...], piece)
        state = piece[0:SUB].astype(jnp.float32) + piece[SUB : 2 * SUB].astype(jnp.float32)
        edge = piece[2 * SUB :].astype(jnp.float32)
        pieces = edge_signal(before[TAIL:], edge, taps)
        carry = jnp.where(place == k, total, carry)
        halo = jnp.where(place == k, before, halo)
        first = [jnp.where(place == k, new, old) for new, old in zip(pieces, first)]
        inner = last * (single * pieces[0] + pieces[1])
        if k == 0:
            head = edge
            total = state + inner if opened else state
        else:
            total = total * whole + state + inner
        before = edge
    return carry, first, halo, total, join_edges(head, before)


def place_of(stride):
    return lax.rem(lax.div(lax.axis_index("ctx"), stride), 4)


def row_kernel(own_ref, one_ref, three_ref, two_ref, rates_ref, taps_ref, out_ref, inside_ref):
    modes = rates_ref.shape[0]
    rate = rates_ref[...]
    refs = (own_ref, one_ref, two_ref, three_ref)
    carry, first, halo, total, edges = chain(refs, place_of(2), 2 * BLOCK, rate, edge_taps(taps_ref), False)
    pack(total, edges, out_ref)
    inside_ref[0:modes, :] = carry
    inside_ref[modes : 2 * modes, :] = halo
    for i in range(2):
        inside_ref[2 * modes + i : 2 * modes + i + 1, :] = first[i]


def merge_kernel(
    own_ref, one_ref, three_ref, two_ref, inside_ref, lower_ref, rates_ref, taps_ref, out_ref
):
    modes = rates_ref.shape[0]
    core = core_index()
    column, line = place_of(2), place_of(8)
    rate = rates_ref[...]
    refs = (own_ref, one_ref, two_ref, three_ref)
    taps = edge_taps(taps_ref)
    single = power(rate, 1)
    above, first, halo, _, _ = chain(refs, line, 8 * BLOCK, rate, taps, True)
    steps = (column * (2 * BLOCK)).astype(jnp.float32) * (-1.0 / LENGTH)
    behind = (column * (2 * BLOCK) - 2).astype(jnp.float32) * (-1.0 / LENGTH)
    inside = inside_ref[0:modes, :]
    opened = inside + jnp.exp(rate * behind) * (single * first[0] + first[1])
    carry = jnp.exp(rate * steps) * above + jnp.where(column > 0, opened, inside)
    within = [inside_ref[2 * modes + i : 2 * modes + i + 1, :] for i in range(2)]
    first = [jnp.where(column > 0, a, b) for a, b in zip(within, first)]
    halo = jnp.where(column > 0, inside_ref[modes : 2 * modes, :], halo)
    lower = lower_ref[...]
    inner = power(rate, BLOCK - 2) * (single * first[0] + first[1])
    carries = carry, power(rate, BLOCK) * carry + lower[:modes] + inner
    halos = halo[TAIL : TAIL + 8], lower[modes + TAIL : modes + TAIL + 8]
    out_ref[0:modes, :] = jnp.where(core == 0, *carries)
    out_ref[modes:, :] = jnp.where(core == 0, *halos)


def local_kernel(*refs):
    blocks = with_sources(refs[: PIECES])
    taps_ref, rates_ref, residues_ref, bias_ref, ends_ref, signal_ref, local_ref, front_ref, zero = refs[PIECES :]
    modes, channels = rates_ref.shape
    fill_tokens(blocks, 0, zero)
    rows = row_iota()
    step = rows.astype(jnp.float32)
    for start in range(0, channels, LANES):
        lanes = pl.ds(start, LANES)
        front = featurize(zero, 0, lanes, taps_ref)
        for i in range(SUB):
            front_ref[i, :, lanes] = front[i]
        signal = [signal_ref[i, :, lanes] for i in range(SUB)]
        taps = [jnp.zeros((8, LANES), jnp.float32) for _ in range(SUB // 8)]
        for mode in range(modes):
            rate = spread(rates_ref[mode : mode + 1, lanes])
            residue = spread(residues_ref[mode : mode + 1, lanes])
            for part in range(SUB // 8):
                taps[part] = taps[part] + residue * jnp.exp(-rate * ((step + 8.0 * part) * (1.0 / LENGTH)))
        bias = spread(bias_ref[0:1, lanes])
        total = [bias * signal[i] for i in range(SUB)]
        for lag in range(SUB):
            tap = spread(taps[lag // 8][lag % 8 : lag % 8 + 1])
            for i in range(lag, SUB):
                total[i] = total[i] + tap * signal[i - lag]
        for mode in range(modes):
            rate = spread(rates_ref[mode : mode + 1, lanes])
            residue = spread(residues_ref[mode : mode + 1, lanes])
            decay = jnp.exp(rate * (-1.0 / LENGTH))
            state = ends_ref[mode, :, lanes]
            for far in (1, 2, 4):
                state = state + jnp.where(rows >= far, power(rate, far * SUB) * pltpu.roll(state, far, 0), 0.0)
            carried = jnp.where(rows >= 1, pltpu.roll(state, 1, 0), 0.0) * residue
            for i in range(SUB):
                carried = carried * decay
                total[i] = total[i] + carried
        for i in range(SUB):
            local_ref[i, :, lanes] = total[i]


def final_kernel(
    carry_ref, summary_ref, taps_ref, rates_ref, residues_ref, bias_ref, local_ref, front_ref, out_ref, natural
):
    modes, channels = rates_ref.shape
    rows = row_iota()
    step = rows.astype(jnp.float32)

    def at_first(row):
        return jnp.where(rows == 0, spread(row), 0.0)

    for start in range(0, channels, LANES):
        lanes = pl.ds(start, LANES)
        got = carry_ref[:, lanes]
        halo = got[modes:]
        taps = [[taps_ref[j, s : s + 1, lanes] for j in range(3)] for s in (1, 2, 0)]
        s0, s1 = edge_signal(halo, summary_ref[modes:, lanes], taps[:2])
        _, t1, t2 = taps[2]
        bias = bias_ref[0:1, lanes]
        total = [local_ref[i, :, lanes] for i in range(SUB)]
        front = [front_ref[i, :, lanes] for i in range(SUB)]
        total[0] = total[0] + at_first(bias * s0)
        total[1] = total[1] + at_first(bias * s1)
        front[0] = front[0] + at_first(t1 * halo[5:6] + t2 * halo[4:5])
        front[1] = front[1] + at_first(t2 * halo[5:6])
        for mode in range(modes):
            row = rates_ref[mode : mode + 1, lanes]
            residue = residues_ref[mode : mode + 1, lanes]
            grow = jnp.exp(row * (1.0 / LENGTH))
            rate = spread(row)
            decay = jnp.exp(rate * (-1.0 / LENGTH))
            start_row = spread(residue * (got[mode : mode + 1] + grow * s0))
            later = jnp.where(rows >= 1, spread(residue * (grow * (grow * s1))), 0.0)
            carried = (start_row + later) * jnp.exp(-rate * ((step * SUB + 1.0) * (1.0 / LENGTH)))
            total[0] = total[0] + carried
            carried = carried * decay + at_first(residue * s1)
            total[1] = total[1] + carried
            for i in range(2, SUB):
                carried = carried * decay
                total[i] = total[i] + carried
        for i in range(SUB):
            natural[start // LANES, pl.ds(i, 8, stride=SUB), :] = front[i] * total[i]
        out_ref[:, lanes] = natural[start // LANES].astype(out_ref.dtype)


def body(streams, short_taps, residues, rates, bias):
    parts = lax.axis_size("tp")
    ctx = lax.axis_size("ctx")
    modes, channels = rates.shape
    tokens = SUB * parts
    f32 = jnp.float32
    wide = jax.ShapeDtypeStruct((SUB, parts, channels), f32)
    packed = jax.ShapeDtypeStruct((modes + SUB, channels), f32)
    carried = jax.ShapeDtypeStruct((modes + 8, channels), f32)
    plane = pltpu.VMEM((channels // LANES, tokens, LANES), f32)
    bias = bias[None]

    def kernel(function, out_shape, operands, scratch=(), cost=None, name=None):
        several = isinstance(out_shape, tuple)
        return pl.pallas_call(
            function,
            out_shape=out_shape,
            in_specs=[VMEM] * len(operands),
            out_specs=(VMEM,) * len(out_shape) if several else VMEM,
            scratch_shapes=list(scratch),
            compiler_params=pltpu.CompilerParams(vmem_limit_bytes=24 << 20),
            cost_estimate=cost,
            name=name or function.__name__,
        )(*operands)

    by_stream = jnp.transpose(streams, (1, 0, 2))
    turn = 1 - 2 * core_index()
    swap = [(i, i ^ 1) for i in range(ctx)]

    def block_for(shift):
        at = ((lax.axis_index("tp") + turn * shift) % parts) * channels
        return lax.dynamic_slice(by_stream, (0, 0, at), (3, SUB, channels))

    def along(value, shift):
        route = []
        for c in range(ctx):
            step = -shift if c % 2 else shift
            route += [(c * parts + z, c * parts + (z + step) % parts) for z in range(parts)]
        return lax.ppermute(value, ("ctx", "tp"), route)

    passed = lax.ppermute(jnp.stack([block_for(-k) for k in (1, 2, 3)]), "ctx", swap)
    far = along(block_for(4), 4)
    two = jax.ShapeDtypeStruct((2, 3, SUB, channels), streams.dtype)
    three = jax.ShapeDtypeStruct((3, 3, SUB, channels), streams.dtype)

    def both(shift, *after):
        return kernel(functools.partial(join_kernel, shift - 1), two, (block_for(shift), passed, *after), name="join")

    third, second = (along(both(k), k) for k in (3, 2))
    first = along(both(1, far), 1)
    back = lax.ppermute(kernel(back_kernel, three, (third, second, first)), "ctx", swap)
    blocks = [far, third, second, first, back, block_for(0)]
    summary, ends, signal = kernel(
        state_kernel,
        (packed, jax.ShapeDtypeStruct((modes, parts, channels), f32), wide),
        (*blocks, short_taps, rates, residues, bias),
        [plane, plane],
    )
    got = lax.ppermute(summary, "ctx", swap)
    group = jax.ShapeDtypeStruct((3 * SUB, channels), jnp.bfloat16)

    def around(value, stride):
        parts = {}
        for by in (3, 1, 2):
            route = [(i, i + ((i // stride + by) % 4 - i // stride % 4) * stride) for i in range(ctx)]
            parts[by] = lax.ppermute(value, "ctx", route)
        return parts[1], parts[3], parts[2]

    pair, lower = kernel(pair_kernel, (group, packed), (summary, got, rates, short_taps))
    row, inside = kernel(
        row_kernel,
        (group, jax.ShapeDtypeStruct((2 * modes + 8, channels), f32)),
        (pair, *around(pair, 2), rates, short_taps),
    )
    carry = kernel(merge_kernel, carried, (row, *around(row, 8), inside, lower, rates, short_taps))
    local, front = kernel(
        local_kernel,
        (wide, wide),
        (*blocks, short_taps, rates, residues, bias, ends, signal),
        [plane],
        cost=pl.CostEstimate(flops=8 << 20, bytes_accessed=2 << 20, transcendentals=0),
    )
    return kernel(
        final_kernel,
        jax.ShapeDtypeStruct((tokens, channels), jnp.bfloat16),
        (carry, summary, short_taps, rates, residues, bias, local, front),
        [plane],
    )


def solution(mesh):
    in_specs = (
        P(("ctx", "tp"), None, None),
        P(None, None, "tp"),
        P(None, "tp"),
        P(None, "tp"),
        P("tp"),
    )
    out_specs = P("ctx", "tp")
    return jax.shard_map(body, mesh=mesh, in_specs=in_specs, out_specs=out_specs, check_vma=False)
```

```python
import functools

import jax
import jax.numpy as jnp
from jax import lax
from jax.experimental import pallas as pl
from jax.experimental.pallas import tpu as pltpu
from jax.sharding import PartitionSpec as P

LENGTH = 4096
SUB = 16
PIECES = 6
LANES = 128
BLOCK = 128
VMEM = pl.BlockSpec(memory_space=pltpu.VMEM)


def row_iota():
    return lax.broadcasted_iota(jnp.int32, (8, LANES), 0)


def spread(row):
    return jnp.broadcast_to(row, (8, LANES))


def fill_tokens(blocks, stream, scratch):
    for block, source in blocks:
        at = pl.multiple_of(source * SUB, SUB)
        for group in range(scratch.shape[0]):
            lanes = pl.ds(group * LANES, LANES)
            scratch[group, pl.ds(at, SUB), :] = block[stream, :, lanes].astype(jnp.float32)


def join_kernel(at, own_ref, passed_ref, *refs):
    out_ref = refs[-1]
    out_ref[0] = own_ref[...]
    out_ref[1] = passed_ref[at]


def back_kernel(third_ref, second_ref, first_ref, out_ref):
    for at, ref in enumerate((first_ref, second_ref, third_ref)):
        out_ref[at] = ref[1]


def with_sources(refs):
    far, third, second, first, back, own = refs
    me = lax.axis_index("tp")
    turn = 1 - 2 * core_index()
    places = [(own, 0), (far, 4), (first.at[0], 1), (second.at[0], 2), (third.at[0], 3)]
    places += [(back.at[k - 1], -k) for k in (1, 2, 3)]
    return [(ref, lax.rem(me - turn * shift + 8, 8)) for ref, shift in places]


def featurize(scratch, stream, lanes, taps_ref):
    group = lanes.start // LANES
    values = [scratch[group, pl.ds(i, 8, stride=SUB), :] for i in range(SUB)]
    first = row_iota() == 0
    joined = [jnp.where(first, 0.0, pltpu.roll(values[SUB - far], 1, 0)) for far in (2, 1)] + values
    t0, t1, t2 = (spread(taps_ref[j, stream : stream + 1, lanes]) for j in range(3))
    return [t0 * joined[i + 2] + t1 * joined[i + 1] + t2 * joined[i] for i in range(SUB)]


def power(rate, tokens):
    return jnp.exp(rate * (-float(tokens) / LENGTH))


def core_index():
    return lax.rem(lax.axis_index("ctx"), 2)


TAIL = 4


def edge_signal(tail, head, taps):
    result = None
    for n, (t0, t1, t2) in enumerate(taps):
        x0, x1 = (head[2 * n + i : 2 * n + i + 1] for i in range(2))
        h0, h1 = (tail[2 * n + i : 2 * n + i + 1] for i in range(2))
        feats = (t0 * x0 + t1 * h1 + t2 * h0, t0 * x1 + t1 * x0 + t2 * h1)
        result = feats if result is None else tuple(a * b for a, b in zip(result, feats))
    return result


def edge_taps(taps_ref):
    return [[taps_ref[j, s : s + 1, :] for j in range(3)] for s in (1, 2)]


def weights_kernel(rates_ref, residues_ref, _, decay_ref, ends_ref, carry_ref):
    modes, channels = rates_ref.shape
    step = row_iota().astype(jnp.float32)
    remaining = (7.0 - step) * (SUB / LENGTH)
    elapsed = (step * SUB + 1.0) * (1.0 / LENGTH)
    decay_ref[...] = power(rates_ref[...], 1)
    for start in range(0, channels, LANES):
        lanes = pl.ds(start, LANES)
        for mode in range(modes):
            rate = spread(rates_ref[mode : mode + 1, lanes])
            ends_ref[mode, :, lanes] = jnp.exp(-rate * remaining)
            carry_ref[mode, :, lanes] = spread(residues_ref[mode : mode + 1, lanes]) * jnp.exp(-rate * elapsed)


def state_kernel(*refs):
    blocks = with_sources(refs[: PIECES])
    taps_ref, decay_ref, weight_ref, full, ends_ref, signal_ref, one, two = refs[PIECES :]
    modes, channels = decay_ref.shape
    fill_tokens(blocks, 1, one)
    fill_tokens(blocks, 2, two)
    rows = row_iota()
    full[modes:, :] = jnp.zeros((SUB, channels), jnp.float32)
    for group in range(channels // LANES):
        lanes = pl.ds(group * LANES, LANES)
        for n, scratch in enumerate((one, two)):
            full[modes + 2 * n : modes + 2 * n + 2, lanes] = scratch[group, 0:2, :]
            full[modes + TAIL + 2 * n : modes + TAIL + 2 * n + 2, lanes] = scratch[group, BLOCK - 2 : BLOCK, :]
    for block, source in blocks:

        @pl.when(source == 7)
        def _(block=block):
            full[modes + TAIL + 4 : modes + TAIL + 6, :] = block[0].astype(jnp.float32)[SUB - 2 :]

    for start in range(0, channels, LANES):
        lanes = pl.ds(start, LANES)
        left = featurize(one, 1, lanes, taps_ref)
        right = featurize(two, 2, lanes, taps_ref)
        signal = [a * b for a, b in zip(left, right)]
        for i in range(2):
            signal[i] = jnp.where(rows == 0, 0.0, signal[i])
        for i in range(SUB):
            signal_ref[i, :, lanes] = signal[i]
        for mode in range(modes):
            decay = spread(decay_ref[mode : mode + 1, lanes])
            state = signal[0]
            for i in range(1, SUB):
                state = state * decay + signal[i]
            ends_ref[mode, :, lanes] = state
            full[mode : mode + 1, lanes] = jnp.sum(state * weight_ref[mode, :, lanes], axis=0, keepdims=True)


def pack(state, edge, out_ref):
    high = state.astype(jnp.bfloat16)
    out_ref[0:SUB, :] = high
    out_ref[SUB : 2 * SUB, :] = (state - high.astype(jnp.float32)).astype(jnp.bfloat16)
    out_ref[2 * SUB : 3 * SUB, :] = edge.astype(jnp.bfloat16)


def join_edges(first, last):
    rows = lax.broadcasted_iota(jnp.int32, first.shape, 0)
    return jnp.where(rows < TAIL, first, last)


def pair_kernel(kept_ref, got_ref, rates_ref, taps_ref, out_ref, lower_ref):
    modes = rates_ref.shape[0]
    core = core_index()
    rate = rates_ref[...]
    kept, got = kept_ref[...], got_ref[...]
    lower = jnp.where(core == 0, kept, got)
    upper = jnp.where(core == 0, got, kept)
    s0, s1 = edge_signal(lower[modes + TAIL :], upper[modes:], edge_taps(taps_ref))
    inner = power(rate, BLOCK - 2) * (power(rate, 1) * s0 + s1)
    state = upper[:modes] + inner + power(rate, BLOCK) * lower[:modes]
    pack(state, join_edges(lower[modes:], upper[modes:]), out_ref)
    lower_ref[...] = lower


def chain(refs, place, tokens, rate, taps, opened):
    single, whole, last = power(rate, 1), power(rate, tokens), power(rate, tokens - 2)
    size = len(refs)
    carry = halo = before = total = jnp.zeros_like(rate)
    first = (jnp.zeros_like(rate[:1]),) * 2
    head = None
    for k in range(size):
        piece = refs[0][...]
        for by in range(1, size):
            piece = jnp.where(lax.rem(place - k + size, size) == by, refs[by][...], piece)
        state = piece[0:SUB].astype(jnp.float32) + piece[SUB : 2 * SUB].astype(jnp.float32)
        edge = piece[2 * SUB :].astype(jnp.float32)
        pieces = edge_signal(before[TAIL:], edge, taps)
        carry = jnp.where(place == k, total, carry)
        halo = jnp.where(place == k, before, halo)
        first = [jnp.where(place == k, new, old) for new, old in zip(pieces, first)]
        inner = last * (single * pieces[0] + pieces[1])
        if k == 0:
            head = edge
            total = state + inner if opened else state
        else:
            total = total * whole + state + inner
        before = edge
    return carry, first, halo, total, join_edges(head, before)


def place_of(stride):
    return lax.rem(lax.div(lax.axis_index("ctx"), stride), 4)


def row_kernel(own_ref, one_ref, three_ref, two_ref, rates_ref, taps_ref, out_ref, inside_ref):
    modes = rates_ref.shape[0]
    rate = rates_ref[...]
    refs = (own_ref, one_ref, two_ref, three_ref)
    carry, first, halo, total, edges = chain(refs, place_of(2), 2 * BLOCK, rate, edge_taps(taps_ref), False)
    pack(total, edges, out_ref)
    inside_ref[0:modes, :] = carry
    inside_ref[modes : 2 * modes, :] = halo
    for i in range(2):
        inside_ref[2 * modes + i : 2 * modes + i + 1, :] = first[i]


def merge_kernel(
    own_ref, one_ref, three_ref, two_ref, inside_ref, lower_ref, rates_ref, taps_ref, out_ref
):
    modes = rates_ref.shape[0]
    core = core_index()
    column, line = place_of(2), place_of(8)
    rate = rates_ref[...]
    refs = (own_ref, one_ref, two_ref, three_ref)
    taps = edge_taps(taps_ref)
    single = power(rate, 1)
    above, first, halo, _, _ = chain(refs, line, 8 * BLOCK, rate, taps, True)
    steps = (column * (2 * BLOCK)).astype(jnp.float32) * (-1.0 / LENGTH)
    behind = (column * (2 * BLOCK) - 2).astype(jnp.float32) * (-1.0 / LENGTH)
    inside = inside_ref[0:modes, :]
    opened = inside + jnp.exp(rate * behind) * (single * first[0] + first[1])
    carry = jnp.exp(rate * steps) * above + jnp.where(column > 0, opened, inside)
    within = [inside_ref[2 * modes + i : 2 * modes + i + 1, :] for i in range(2)]
    first = [jnp.where(column > 0, a, b) for a, b in zip(within, first)]
    halo = jnp.where(column > 0, inside_ref[modes : 2 * modes, :], halo)
    lower = lower_ref[...]
    inner = power(rate, BLOCK - 2) * (single * first[0] + first[1])
    carries = carry, power(rate, BLOCK) * carry + lower[:modes] + inner
    halos = halo[TAIL : TAIL + 8], lower[modes + TAIL : modes + TAIL + 8]
    out_ref[0:modes, :] = jnp.where(core == 0, *carries)
    out_ref[modes:, :] = jnp.where(core == 0, *halos)


def local_kernel(*refs):
    blocks = with_sources(refs[: PIECES])
    taps_ref, rates_ref, residues_ref, bias_ref, ends_ref, signal_ref, local_ref, front_ref, zero = refs[PIECES :]
    modes, channels = rates_ref.shape
    fill_tokens(blocks, 0, zero)
    rows = row_iota()
    step = rows.astype(jnp.float32)
    for start in range(0, channels, LANES):
        lanes = pl.ds(start, LANES)
        front = featurize(zero, 0, lanes, taps_ref)
        for i in range(SUB):
            front_ref[i, :, lanes] = front[i]
        signal = [signal_ref[i, :, lanes] for i in range(SUB)]
        taps = [jnp.zeros((8, LANES), jnp.float32) for _ in range(SUB // 8)]
        for mode in range(modes):
            rate = spread(rates_ref[mode : mode + 1, lanes])
            residue = spread(residues_ref[mode : mode + 1, lanes])
            for part in range(SUB // 8):
                taps[part] = taps[part] + residue * jnp.exp(-rate * ((step + 8.0 * part) * (1.0 / LENGTH)))
        bias = spread(bias_ref[0:1, lanes])
        total = [bias * signal[i] for i in range(SUB)]
        for lag in range(SUB):
            tap = spread(taps[lag // 8][lag % 8 : lag % 8 + 1])
            for i in range(lag, SUB):
                total[i] = total[i] + tap * signal[i - lag]
        for mode in range(modes):
            rate = spread(rates_ref[mode : mode + 1, lanes])
            residue = spread(residues_ref[mode : mode + 1, lanes])
            decay = jnp.exp(rate * (-1.0 / LENGTH))
            state = ends_ref[mode, :, lanes]
            for far in (1, 2, 4):
                state = state + jnp.where(rows >= far, power(rate, far * SUB) * pltpu.roll(state, far, 0), 0.0)
            carried = jnp.where(rows >= 1, pltpu.roll(state, 1, 0), 0.0) * residue
            for i in range(SUB):
                carried = carried * decay
                total[i] = total[i] + carried
        for i in range(SUB):
            local_ref[i, :, lanes] = total[i]


def final_kernel(
    carry_ref, summary_ref, taps_ref, rates_ref, residues_ref, bias_ref, decay_ref, weight_ref, local_ref, front_ref, out_ref, natural
):
    modes, channels = rates_ref.shape
    rows = row_iota()

    def at_first(row):
        return jnp.where(rows == 0, spread(row), 0.0)

    for start in range(0, channels, LANES):
        lanes = pl.ds(start, LANES)
        halo = carry_ref[modes:, lanes]
        taps = [[taps_ref[j, s : s + 1, lanes] for j in range(3)] for s in (1, 2, 0)]
        s0, s1 = edge_signal(halo, summary_ref[modes:, lanes], taps[:2])
        _, t1, t2 = taps[2]
        bias = bias_ref[0:1, lanes]
        grow = power(rates_ref[:, lanes], -1)
        carry = carry_ref[:modes, lanes] + grow * (s0 + grow * s1)
        excess = jnp.sum(residues_ref[:, lanes] * grow, axis=0, keepdims=True) * s1
        total = [local_ref[i, :, lanes] for i in range(SUB)]
        front = [front_ref[i, :, lanes] for i in range(SUB)]
        total[0] = total[0] + at_first(bias * s0 - excess)
        total[1] = total[1] + at_first(bias * s1)
        front[0] = front[0] + at_first(t1 * halo[5:6] + t2 * halo[4:5])
        front[1] = front[1] + at_first(t2 * halo[5:6])
        for mode in range(modes):
            decay = spread(decay_ref[mode : mode + 1, lanes])
            carried = spread(carry[mode : mode + 1]) * weight_ref[mode, :, lanes]
            total[0] = total[0] + carried
            for i in range(1, SUB):
                carried = carried * decay
                total[i] = total[i] + carried
        for i in range(SUB):
            natural[start // LANES, pl.ds(i, 8, stride=SUB), :] = front[i] * total[i]
        out_ref[:, lanes] = natural[start // LANES].astype(out_ref.dtype)


def body(streams, short_taps, residues, rates, bias):
    parts = lax.axis_size("tp")
    ctx = lax.axis_size("ctx")
    modes, channels = rates.shape
    tokens = SUB * parts
    f32 = jnp.float32
    wide = jax.ShapeDtypeStruct((SUB, parts, channels), f32)
    packed = jax.ShapeDtypeStruct((modes + SUB, channels), f32)
    carried = jax.ShapeDtypeStruct((modes + 8, channels), f32)
    plane = pltpu.VMEM((channels // LANES, tokens, LANES), f32)
    bias = bias[None]

    def kernel(function, out_shape, operands, scratch=(), cost=None, name=None):
        several = isinstance(out_shape, tuple)
        return pl.pallas_call(
            function,
            out_shape=out_shape,
            in_specs=[VMEM] * len(operands),
            out_specs=(VMEM,) * len(out_shape) if several else VMEM,
            scratch_shapes=list(scratch),
            compiler_params=pltpu.CompilerParams(vmem_limit_bytes=24 << 20),
            cost_estimate=cost,
            name=name or function.__name__,
        )(*operands)

    spans = jax.ShapeDtypeStruct((modes, parts, channels), f32)
    small = pl.CostEstimate(flops=8 << 20, bytes_accessed=2 << 20, transcendentals=0)
    decay, ends_weight, carry_weight = kernel(
        weights_kernel, (jax.ShapeDtypeStruct(rates.shape, f32), spans, spans), (rates, residues, bias), cost=small
    )
    by_stream = jnp.transpose(streams, (1, 0, 2))
    turn = 1 - 2 * core_index()
    swap = [(i, i ^ 1) for i in range(ctx)]

    def block_for(shift):
        at = ((lax.axis_index("tp") + turn * shift) % parts) * channels
        return lax.dynamic_slice(by_stream, (0, 0, at), (3, SUB, channels))

    def along(value, shift):
        route = []
        for c in range(ctx):
            step = -shift if c % 2 else shift
            route += [(c * parts + z, c * parts + (z + step) % parts) for z in range(parts)]
        return lax.ppermute(value, ("ctx", "tp"), route)

    passed = lax.ppermute(jnp.stack([block_for(-k) for k in (1, 2, 3)]), "ctx", swap)
    far = along(block_for(4), 4)
    two = jax.ShapeDtypeStruct((2, 3, SUB, channels), streams.dtype)
    three = jax.ShapeDtypeStruct((3, 3, SUB, channels), streams.dtype)

    def both(shift, *after):
        return kernel(functools.partial(join_kernel, shift - 1), two, (block_for(shift), passed, *after), name="join")

    third, second = (along(both(k), k) for k in (3, 2))
    first = along(both(1, far), 1)
    back = lax.ppermute(kernel(back_kernel, three, (third, second, first)), "ctx", swap)
    blocks = [far, third, second, first, back, block_for(0)]
    summary, ends, signal = kernel(
        state_kernel,
        (packed, spans, wide),
        (*blocks, short_taps, decay, ends_weight),
        [plane, plane],
    )
    got = lax.ppermute(summary, "ctx", swap)
    group = jax.ShapeDtypeStruct((3 * SUB, channels), jnp.bfloat16)

    def around(value, stride):
        parts = {}
        for by in (3, 1, 2):
            route = [(i, i + ((i // stride + by) % 4 - i // stride % 4) * stride) for i in range(ctx)]
            parts[by] = lax.ppermute(value, "ctx", route)
        return parts[1], parts[3], parts[2]

    pair, lower = kernel(pair_kernel, (group, packed), (summary, got, rates, short_taps))
    row, inside = kernel(
        row_kernel,
        (group, jax.ShapeDtypeStruct((2 * modes + 8, channels), f32)),
        (pair, *around(pair, 2), rates, short_taps),
    )
    carry = kernel(merge_kernel, carried, (row, *around(row, 8), inside, lower, rates, short_taps))
    local, front = kernel(
        local_kernel,
        (wide, wide),
        (*blocks, short_taps, rates, residues, bias, ends, signal),
        [plane],
        cost=small,
    )
    return kernel(
        final_kernel,
        jax.ShapeDtypeStruct((tokens, channels), jnp.bfloat16),
        (carry, summary, short_taps, rates, residues, bias, decay, carry_weight, local, front),
        [plane],
    )


def solution(mesh):
    in_specs = (
        P(("ctx", "tp"), None, None),
        P(None, None, "tp"),
        P(None, "tp"),
        P(None, "tp"),
        P("tp"),
    )
    out_specs = P("ctx", "tp")
    return jax.shard_map(body, mesh=mesh, in_specs=in_specs, out_specs=out_specs, check_vma=False)
```

```python
import jax
import jax.numpy as jnp
from jax import lax
from jax.experimental import pallas as pl
from jax.experimental.pallas import tpu as pltpu
from jax.sharding import PartitionSpec as P

LENGTH = 4096
SUB = 16
PIECES = 8
LANES = 128
BLOCK = 128
VMEM = pl.BlockSpec(memory_space=pltpu.VMEM)


def row_iota():
    return lax.broadcasted_iota(jnp.int32, (8, LANES), 0)


def spread(row):
    return jnp.broadcast_to(row, (8, LANES))


def fill_tokens(blocks, stream, scratch):
    for block, source in blocks:
        at = pl.multiple_of(source * SUB, SUB)
        for group in range(scratch.shape[0]):
            lanes = pl.ds(group * LANES, LANES)
            scratch[group, pl.ds(at, SUB), :] = block[stream, :, lanes].astype(jnp.float32)


def join_kernel(own_ref, passed_ref, out_ref):
    out_ref[0] = own_ref[...]
    out_ref[1] = passed_ref[...]


def back_kernel(third_ref, _far, _near, out_ref):
    out_ref[...] = third_ref[1]


def with_sources(refs):
    *near, third, far, back, own = refs
    me = lax.axis_index("tp")
    turn = 1 - 2 * core_index()
    places = [(own, 0), (far, 4), (third.at[0], 3), (back, -3), *zip(near, (1, -1, 2, -2))]
    return [(ref, lax.rem(me - turn * shift + 8, 8)) for ref, shift in places]


def featurize(scratch, stream, lanes, taps_ref):
    group = lanes.start // LANES
    values = [scratch[group, pl.ds(i, 8, stride=SUB), :] for i in range(SUB)]
    first = row_iota() == 0
    joined = [jnp.where(first, 0.0, pltpu.roll(values[SUB - far], 1, 0)) for far in (2, 1)] + values
    t0, t1, t2 = (spread(taps_ref[j, stream : stream + 1, lanes]) for j in range(3))
    return [t0 * joined[i + 2] + t1 * joined[i + 1] + t2 * joined[i] for i in range(SUB)]


def power(rate, tokens):
    return jnp.exp(rate * (-float(tokens) / LENGTH))


def core_index():
    return lax.rem(lax.axis_index("ctx"), 2)


TAIL = 4


def edge_signal(tail, head, taps):
    result = None
    for n, (t0, t1, t2) in enumerate(taps):
        x0, x1 = (head[2 * n + i : 2 * n + i + 1] for i in range(2))
        h0, h1 = (tail[2 * n + i : 2 * n + i + 1] for i in range(2))
        feats = (t0 * x0 + t1 * h1 + t2 * h0, t0 * x1 + t1 * x0 + t2 * h1)
        result = feats if result is None else tuple(a * b for a, b in zip(result, feats))
    return result


def edge_taps(taps_ref):
    return [[taps_ref[j, s : s + 1, :] for j in range(3)] for s in (1, 2)]


def weights_kernel(rates_ref, residues_ref, _, decay_ref, ends_ref, carry_ref):
    modes, channels = rates_ref.shape
    step = row_iota().astype(jnp.float32)
    remaining = (7.0 - step) * (SUB / LENGTH)
    elapsed = (step * SUB + 1.0) * (1.0 / LENGTH)
    decay_ref[...] = power(rates_ref[...], 1)
    for start in range(0, channels, LANES):
        lanes = pl.ds(start, LANES)
        for mode in range(modes):
            rate = spread(rates_ref[mode : mode + 1, lanes])
            ends_ref[mode, :, lanes] = jnp.exp(-rate * remaining)
            carry_ref[mode, :, lanes] = spread(residues_ref[mode : mode + 1, lanes]) * jnp.exp(-rate * elapsed)


def state_kernel(*refs):
    blocks = with_sources(refs[: PIECES])
    taps_ref, decay_ref, weight_ref, full, ends_ref, signal_ref, one, two = refs[PIECES :]
    modes, channels = decay_ref.shape
    fill_tokens(blocks, 1, one)
    fill_tokens(blocks, 2, two)
    rows = row_iota()
    full[modes:, :] = jnp.zeros((SUB, channels), jnp.float32)
    for group in range(channels // LANES):
        lanes = pl.ds(group * LANES, LANES)
        for n, scratch in enumerate((one, two)):
            full[modes + 2 * n : modes + 2 * n + 2, lanes] = scratch[group, 0:2, :]
            full[modes + TAIL + 2 * n : modes + TAIL + 2 * n + 2, lanes] = scratch[group, BLOCK - 2 : BLOCK, :]
    for block, source in blocks:

        @pl.when(source == 7)
        def _(block=block):
            full[modes + TAIL + 4 : modes + TAIL + 6, :] = block[0].astype(jnp.float32)[SUB - 2 :]

    for start in range(0, channels, LANES):
        lanes = pl.ds(start, LANES)
        left = featurize(one, 1, lanes, taps_ref)
        right = featurize(two, 2, lanes, taps_ref)
        signal = [a * b for a, b in zip(left, right)]
        for i in range(2):
            signal[i] = jnp.where(rows == 0, 0.0, signal[i])
        for i in range(SUB):
            signal_ref[i, :, lanes] = signal[i]
        for mode in range(modes):
            decay = spread(decay_ref[mode : mode + 1, lanes])
            state = signal[0]
            for i in range(1, SUB):
                state = state * decay + signal[i]
            ends_ref[mode, :, lanes] = state
            full[mode : mode + 1, lanes] = jnp.sum(state * weight_ref[mode, :, lanes], axis=0, keepdims=True)


def pack(state, edge, out_ref):
    high = state.astype(jnp.bfloat16)
    out_ref[0:SUB, :] = high
    out_ref[SUB : 2 * SUB, :] = (state - high.astype(jnp.float32)).astype(jnp.bfloat16)
    out_ref[2 * SUB : 3 * SUB, :] = edge.astype(jnp.bfloat16)


def join_edges(first, last):
    rows = lax.broadcasted_iota(jnp.int32, first.shape, 0)
    return jnp.where(rows < TAIL, first, last)


def pair_kernel(kept_ref, got_ref, rates_ref, taps_ref, out_ref, lower_ref):
    modes = rates_ref.shape[0]
    core = core_index()
    rate = rates_ref[...]
    kept, got = kept_ref[...], got_ref[...]
    lower = jnp.where(core == 0, kept, got)
    upper = jnp.where(core == 0, got, kept)
    s0, s1 = edge_signal(lower[modes + TAIL :], upper[modes:], edge_taps(taps_ref))
    inner = power(rate, BLOCK - 2) * (power(rate, 1) * s0 + s1)
    state = upper[:modes] + inner + power(rate, BLOCK) * lower[:modes]
    pack(state, join_edges(lower[modes:], upper[modes:]), out_ref)
    lower_ref[...] = lower


def chain(refs, place, tokens, rate, taps, opened):
    single, whole, last = power(rate, 1), power(rate, tokens), power(rate, tokens - 2)
    size = len(refs)
    carry = halo = before = total = jnp.zeros_like(rate)
    first = (jnp.zeros_like(rate[:1]),) * 2
    head = None
    for k in range(size):
        piece = refs[0][...]
        for by in range(1, size):
            piece = jnp.where(lax.rem(place - k + size, size) == by, refs[by][...], piece)
        state = piece[0:SUB].astype(jnp.float32) + piece[SUB : 2 * SUB].astype(jnp.float32)
        edge = piece[2 * SUB :].astype(jnp.float32)
        pieces = edge_signal(before[TAIL:], edge, taps)
        carry = jnp.where(place == k, total, carry)
        halo = jnp.where(place == k, before, halo)
        first = [jnp.where(place == k, new, old) for new, old in zip(pieces, first)]
        inner = last * (single * pieces[0] + pieces[1])
        if k == 0:
            head = edge
            total = state + inner if opened else state
        else:
            total = total * whole + state + inner
        before = edge
    return carry, first, halo, total, join_edges(head, before)


def place_of(stride):
    return lax.rem(lax.div(lax.axis_index("ctx"), stride), 4)


def row_kernel(own_ref, one_ref, three_ref, two_ref, rates_ref, taps_ref, out_ref, inside_ref):
    modes = rates_ref.shape[0]
    rate = rates_ref[...]
    refs = (own_ref, one_ref, two_ref, three_ref)
    carry, first, halo, total, edges = chain(refs, place_of(2), 2 * BLOCK, rate, edge_taps(taps_ref), False)
    pack(total, edges, out_ref)
    inside_ref[0:modes, :] = carry
    inside_ref[modes : 2 * modes, :] = halo
    for i in range(2):
        inside_ref[2 * modes + i : 2 * modes + i + 1, :] = first[i]


def merge_kernel(
    own_ref, one_ref, three_ref, two_ref, inside_ref, lower_ref, rates_ref, taps_ref, out_ref
):
    modes = rates_ref.shape[0]
    core = core_index()
    column, line = place_of(2), place_of(8)
    rate = rates_ref[...]
    refs = (own_ref, one_ref, two_ref, three_ref)
    taps = edge_taps(taps_ref)
    single = power(rate, 1)
    above, first, halo, _, _ = chain(refs, line, 8 * BLOCK, rate, taps, True)
    steps = (column * (2 * BLOCK)).astype(jnp.float32) * (-1.0 / LENGTH)
    behind = (column * (2 * BLOCK) - 2).astype(jnp.float32) * (-1.0 / LENGTH)
    inside = inside_ref[0:modes, :]
    opened = inside + jnp.exp(rate * behind) * (single * first[0] + first[1])
    carry = jnp.exp(rate * steps) * above + jnp.where(column > 0, opened, inside)
    within = [inside_ref[2 * modes + i : 2 * modes + i + 1, :] for i in range(2)]
    first = [jnp.where(column > 0, a, b) for a, b in zip(within, first)]
    halo = jnp.where(column > 0, inside_ref[modes : 2 * modes, :], halo)
    lower = lower_ref[...]
    inner = power(rate, BLOCK - 2) * (single * first[0] + first[1])
    carries = carry, power(rate, BLOCK) * carry + lower[:modes] + inner
    halos = halo[TAIL : TAIL + 8], lower[modes + TAIL : modes + TAIL + 8]
    out_ref[0:modes, :] = jnp.where(core == 0, *carries)
    out_ref[modes:, :] = jnp.where(core == 0, *halos)


def local_kernel(*refs):
    blocks = with_sources(refs[: PIECES])
    taps_ref, rates_ref, residues_ref, bias_ref, ends_ref, signal_ref, local_ref, front_ref, zero = refs[PIECES :]
    modes, channels = rates_ref.shape
    fill_tokens(blocks, 0, zero)
    rows = row_iota()
    step = rows.astype(jnp.float32)
    for start in range(0, channels, LANES):
        lanes = pl.ds(start, LANES)
        front = featurize(zero, 0, lanes, taps_ref)
        for i in range(SUB):
            front_ref[i, :, lanes] = front[i]
        signal = [signal_ref[i, :, lanes] for i in range(SUB)]
        taps = [jnp.zeros((8, LANES), jnp.float32) for _ in range(SUB // 8)]
        for mode in range(modes):
            rate = spread(rates_ref[mode : mode + 1, lanes])
            residue = spread(residues_ref[mode : mode + 1, lanes])
            for part in range(SUB // 8):
                taps[part] = taps[part] + residue * jnp.exp(-rate * ((step + 8.0 * part) * (1.0 / LENGTH)))
        bias = spread(bias_ref[0:1, lanes])
        total = [bias * signal[i] for i in range(SUB)]
        for lag in range(SUB):
            tap = spread(taps[lag // 8][lag % 8 : lag % 8 + 1])
            for i in range(lag, SUB):
                total[i] = total[i] + tap * signal[i - lag]
        for mode in range(modes):
            rate = spread(rates_ref[mode : mode + 1, lanes])
            residue = spread(residues_ref[mode : mode + 1, lanes])
            decay = jnp.exp(rate * (-1.0 / LENGTH))
            state = ends_ref[mode, :, lanes]
            for far in (1, 2, 4):
                state = state + jnp.where(rows >= far, power(rate, far * SUB) * pltpu.roll(state, far, 0), 0.0)
            carried = jnp.where(rows >= 1, pltpu.roll(state, 1, 0), 0.0) * residue
            for i in range(SUB):
                carried = carried * decay
                total[i] = total[i] + carried
        for i in range(SUB):
            local_ref[i, :, lanes] = total[i]


def final_kernel(
    carry_ref, summary_ref, taps_ref, rates_ref, residues_ref, bias_ref, decay_ref, weight_ref, local_ref, front_ref, out_ref, natural
):
    modes, channels = rates_ref.shape
    rows = row_iota()

    def at_first(row):
        return jnp.where(rows == 0, spread(row), 0.0)

    for start in range(0, channels, LANES):
        lanes = pl.ds(start, LANES)
        halo = carry_ref[modes:, lanes]
        taps = [[taps_ref[j, s : s + 1, lanes] for j in range(3)] for s in (1, 2, 0)]
        s0, s1 = edge_signal(halo, summary_ref[modes:, lanes], taps[:2])
        _, t1, t2 = taps[2]
        bias = bias_ref[0:1, lanes]
        grow = power(rates_ref[:, lanes], -1)
        carry = carry_ref[:modes, lanes] + grow * (s0 + grow * s1)
        excess = jnp.sum(residues_ref[:, lanes] * grow, axis=0, keepdims=True) * s1
        total = [local_ref[i, :, lanes] for i in range(SUB)]
        front = [front_ref[i, :, lanes] for i in range(SUB)]
        total[0] = total[0] + at_first(bias * s0 - excess)
        total[1] = total[1] + at_first(bias * s1)
        front[0] = front[0] + at_first(t1 * halo[5:6] + t2 * halo[4:5])
        front[1] = front[1] + at_first(t2 * halo[5:6])
        for mode in range(modes):
            decay = spread(decay_ref[mode : mode + 1, lanes])
            carried = spread(carry[mode : mode + 1]) * weight_ref[mode, :, lanes]
            total[0] = total[0] + carried
            for i in range(1, SUB):
                carried = carried * decay
                total[i] = total[i] + carried
        for i in range(SUB):
            natural[start // LANES, pl.ds(i, 8, stride=SUB), :] = front[i] * total[i]
        out_ref[:, lanes] = natural[start // LANES].astype(out_ref.dtype)


def body(streams, short_taps, residues, rates, bias):
    parts = lax.axis_size("tp")
    ctx = lax.axis_size("ctx")
    modes, channels = rates.shape
    tokens = SUB * parts
    f32 = jnp.float32
    wide = jax.ShapeDtypeStruct((SUB, parts, channels), f32)
    packed = jax.ShapeDtypeStruct((modes + SUB, channels), f32)
    carried = jax.ShapeDtypeStruct((modes + 8, channels), f32)
    plane = pltpu.VMEM((channels // LANES, tokens, LANES), f32)
    bias = bias[None]

    def kernel(function, out_shape, operands, scratch=(), cost=None, name=None):
        several = isinstance(out_shape, tuple)
        return pl.pallas_call(
            function,
            out_shape=out_shape,
            in_specs=[VMEM] * len(operands),
            out_specs=(VMEM,) * len(out_shape) if several else VMEM,
            scratch_shapes=list(scratch),
            compiler_params=pltpu.CompilerParams(vmem_limit_bytes=24 << 20),
            cost_estimate=cost,
            name=name or function.__name__,
        )(*operands)

    spans = jax.ShapeDtypeStruct((modes, parts, channels), f32)
    small = pl.CostEstimate(flops=8 << 20, bytes_accessed=2 << 20, transcendentals=0)
    decay, ends_weight, carry_weight = kernel(
        weights_kernel, (jax.ShapeDtypeStruct(rates.shape, f32), spans, spans), (rates, residues, bias), cost=small
    )
    by_stream = jnp.transpose(streams, (1, 0, 2))
    turn = 1 - 2 * core_index()
    swap = [(i, i ^ 1) for i in range(ctx)]

    def block_for(shift):
        at = ((lax.axis_index("tp") + turn * shift) % parts) * channels
        return lax.dynamic_slice(by_stream, (0, 0, at), (3, SUB, channels))

    def along(value, shift):
        route = []
        for c in range(ctx):
            step = -shift if c % 2 else shift
            route += [(c * parts + z, c * parts + (z + step) % parts) for z in range(parts)]
        return lax.ppermute(value, ("ctx", "tp"), route)

    passed = lax.ppermute(block_for(-3), "ctx", swap)
    far = along(block_for(4), 4)
    one = jax.ShapeDtypeStruct((3, SUB, channels), streams.dtype)
    two = jax.ShapeDtypeStruct((2, 3, SUB, channels), streams.dtype)
    third = along(kernel(join_kernel, two, (block_for(3), passed)), 3)
    near = {k: along(block_for(k), k) for k in (2, -2, 1, -1)}
    back = lax.ppermute(kernel(back_kernel, one, (third, far, near[-1])), "ctx", swap)
    blocks = [near[1], near[-1], near[2], near[-2], third, far, back, block_for(0)]
    summary, ends, signal = kernel(
        state_kernel,
        (packed, spans, wide),
        (*blocks, short_taps, decay, ends_weight),
        [plane, plane],
    )
    got = lax.ppermute(summary, "ctx", swap)
    group = jax.ShapeDtypeStruct((3 * SUB, channels), jnp.bfloat16)

    def around(value, stride):
        parts = {}
        for by in (3, 1, 2):
            route = [(i, i + ((i // stride + by) % 4 - i // stride % 4) * stride) for i in range(ctx)]
            parts[by] = lax.ppermute(value, "ctx", route)
        return parts[1], parts[3], parts[2]

    pair, lower = kernel(pair_kernel, (group, packed), (summary, got, rates, short_taps))
    row, inside = kernel(
        row_kernel,
        (group, jax.ShapeDtypeStruct((2 * modes + 8, channels), f32)),
        (pair, *around(pair, 2), rates, short_taps),
    )
    carry = kernel(merge_kernel, carried, (row, *around(row, 8), inside, lower, rates, short_taps))
    local, front = kernel(
        local_kernel,
        (wide, wide),
        (*blocks, short_taps, rates, residues, bias, ends, signal),
        [plane],
        cost=small,
    )
    return kernel(
        final_kernel,
        jax.ShapeDtypeStruct((tokens, channels), jnp.bfloat16),
        (carry, summary, short_taps, rates, residues, bias, decay, carry_weight, local, front),
        [plane],
    )


def solution(mesh):
    in_specs = (
        P(("ctx", "tp"), None, None),
        P(None, None, "tp"),
        P(None, "tp"),
        P(None, "tp"),
        P("tp"),
    )
    out_specs = P("ctx", "tp")
    return jax.shard_map(body, mesh=mesh, in_specs=in_specs, out_specs=out_specs, check_vma=False)
```

```python
import jax
import jax.numpy as jnp
from jax import lax
from jax.experimental import pallas as pl
from jax.experimental.pallas import tpu as pltpu
from jax.sharding import PartitionSpec as P

LENGTH = 4096
SUB = 16
PIECES = 8
LANES = 128
BLOCK = 128
VMEM = pl.BlockSpec(memory_space=pltpu.VMEM)


def row_iota():
    return lax.broadcasted_iota(jnp.int32, (8, LANES), 0)


def spread(row):
    return jnp.broadcast_to(row, (8, LANES))


def fill_tokens(blocks, stream, scratch):
    for block, source in blocks:
        at = pl.multiple_of(source * SUB, SUB)
        for group in range(scratch.shape[0]):
            lanes = pl.ds(group * LANES, LANES)
            scratch[group, pl.ds(at, SUB), :] = block[stream, :, lanes].astype(jnp.float32)


def join_kernel(own_ref, passed_ref, out_ref):
    out_ref[0] = own_ref[...]
    out_ref[1] = passed_ref[...]


def hold_kernel(own_ref, _, out_ref):
    out_ref[...] = own_ref[...]


def back_kernel(third_ref, _, out_ref):
    out_ref[...] = third_ref[1]


def with_sources(refs):
    *near, third, far, back, own = refs
    me = lax.axis_index("tp")
    turn = 1 - 2 * core_index()
    places = [(own, 0), (far, 4), (third.at[0], 3), (back, -3), *zip(near, (1, -1, 2, -2))]
    return [(ref, lax.rem(me - turn * shift + 8, 8)) for ref, shift in places]


def featurize(scratch, stream, lanes, taps_ref):
    group = lanes.start // LANES
    values = [scratch[group, pl.ds(i, 8, stride=SUB), :] for i in range(SUB)]
    first = row_iota() == 0
    joined = [jnp.where(first, 0.0, pltpu.roll(values[SUB - far], 1, 0)) for far in (2, 1)] + values
    t0, t1, t2 = (spread(taps_ref[j, stream : stream + 1, lanes]) for j in range(3))
    return [t0 * joined[i + 2] + t1 * joined[i + 1] + t2 * joined[i] for i in range(SUB)]


def power(rate, tokens):
    return jnp.exp(rate * (-float(tokens) / LENGTH))


def core_index():
    return lax.rem(lax.axis_index("ctx"), 2)


TAIL = 4


def edge_signal(tail, head, taps):
    result = None
    for n, (t0, t1, t2) in enumerate(taps):
        x0, x1 = (head[2 * n + i : 2 * n + i + 1] for i in range(2))
        h0, h1 = (tail[2 * n + i : 2 * n + i + 1] for i in range(2))
        feats = (t0 * x0 + t1 * h1 + t2 * h0, t0 * x1 + t1 * x0 + t2 * h1)
        result = feats if result is None else tuple(a * b for a, b in zip(result, feats))
    return result


def edge_taps(taps_ref):
    return [[taps_ref[j, s : s + 1, :] for j in range(3)] for s in (1, 2)]


def weights_kernel(rates_ref, residues_ref, _, decay_ref, ends_ref, carry_ref):
    modes, channels = rates_ref.shape
    step = row_iota().astype(jnp.float32)
    remaining = (7.0 - step) * (SUB / LENGTH)
    elapsed = (step * SUB + 1.0) * (1.0 / LENGTH)
    decay_ref[...] = power(rates_ref[...], 1)
    for start in range(0, channels, LANES):
        lanes = pl.ds(start, LANES)
        for mode in range(modes):
            rate = spread(rates_ref[mode : mode + 1, lanes])
            ends_ref[mode, :, lanes] = jnp.exp(-rate * remaining)
            carry_ref[mode, :, lanes] = spread(residues_ref[mode : mode + 1, lanes]) * jnp.exp(-rate * elapsed)


def state_kernel(*refs):
    blocks = with_sources(refs[: PIECES])
    taps_ref, decay_ref, weight_ref, full, ends_ref, signal_ref, one, two = refs[PIECES :]
    modes, channels = decay_ref.shape
    fill_tokens(blocks, 1, one)
    fill_tokens(blocks, 2, two)
    rows = row_iota()
    full[modes:, :] = jnp.zeros((SUB, channels), jnp.float32)
    for group in range(channels // LANES):
        lanes = pl.ds(group * LANES, LANES)
        for n, scratch in enumerate((one, two)):
            full[modes + 2 * n : modes + 2 * n + 2, lanes] = scratch[group, 0:2, :]
            full[modes + TAIL + 2 * n : modes + TAIL + 2 * n + 2, lanes] = scratch[group, BLOCK - 2 : BLOCK, :]
    for block, source in blocks:

        @pl.when(source == 7)
        def _(block=block):
            full[modes + TAIL + 4 : modes + TAIL + 6, :] = block[0].astype(jnp.float32)[SUB - 2 :]

    for start in range(0, channels, LANES):
        lanes = pl.ds(start, LANES)
        left = featurize(one, 1, lanes, taps_ref)
        right = featurize(two, 2, lanes, taps_ref)
        signal = [a * b for a, b in zip(left, right)]
        for i in range(2):
            signal[i] = jnp.where(rows == 0, 0.0, signal[i])
        for i in range(SUB):
            signal_ref[i, :, lanes] = signal[i]
        for mode in range(modes):
            decay = spread(decay_ref[mode : mode + 1, lanes])
            state = signal[0]
            for i in range(1, SUB):
                state = state * decay + signal[i]
            ends_ref[mode, :, lanes] = state
            full[mode : mode + 1, lanes] = jnp.sum(state * weight_ref[mode, :, lanes], axis=0, keepdims=True)


def pack(state, edge, out_ref):
    high = state.astype(jnp.bfloat16)
    out_ref[0:SUB, :] = high
    out_ref[SUB : 2 * SUB, :] = (state - high.astype(jnp.float32)).astype(jnp.bfloat16)
    out_ref[2 * SUB : 3 * SUB, :] = edge.astype(jnp.bfloat16)


def join_edges(first, last):
    rows = lax.broadcasted_iota(jnp.int32, first.shape, 0)
    return jnp.where(rows < TAIL, first, last)


def pair_kernel(kept_ref, got_ref, rates_ref, taps_ref, out_ref, lower_ref):
    modes = rates_ref.shape[0]
    core = core_index()
    rate = rates_ref[...]
    kept, got = kept_ref[...], got_ref[...]
    lower = jnp.where(core == 0, kept, got)
    upper = jnp.where(core == 0, got, kept)
    s0, s1 = edge_signal(lower[modes + TAIL :], upper[modes:], edge_taps(taps_ref))
    inner = power(rate, BLOCK - 2) * (power(rate, 1) * s0 + s1)
    state = upper[:modes] + inner + power(rate, BLOCK) * lower[:modes]
    pack(state, join_edges(lower[modes:], upper[modes:]), out_ref)
    lower_ref[...] = lower


def chain(refs, place, tokens, rate, taps, opened):
    single, whole, last = power(rate, 1), power(rate, tokens), power(rate, tokens - 2)
    size = len(refs)
    carry = halo = before = total = jnp.zeros_like(rate)
    first = (jnp.zeros_like(rate[:1]),) * 2
    head = None
    for k in range(size):
        piece = refs[0][...]
        for by in range(1, size):
            piece = jnp.where(lax.rem(place - k + size, size) == by, refs[by][...], piece)
        state = piece[0:SUB].astype(jnp.float32) + piece[SUB : 2 * SUB].astype(jnp.float32)
        edge = piece[2 * SUB :].astype(jnp.float32)
        pieces = edge_signal(before[TAIL:], edge, taps)
        carry = jnp.where(place == k, total, carry)
        halo = jnp.where(place == k, before, halo)
        first = [jnp.where(place == k, new, old) for new, old in zip(pieces, first)]
        inner = last * (single * pieces[0] + pieces[1])
        if k == 0:
            head = edge
            total = state + inner if opened else state
        else:
            total = total * whole + state + inner
        before = edge
    return carry, first, halo, total, join_edges(head, before)


def place_of(stride):
    return lax.rem(lax.div(lax.axis_index("ctx"), stride), 4)


def row_kernel(own_ref, one_ref, three_ref, two_ref, rates_ref, taps_ref, out_ref, inside_ref):
    modes = rates_ref.shape[0]
    rate = rates_ref[...]
    refs = (own_ref, one_ref, two_ref, three_ref)
    carry, first, halo, total, edges = chain(refs, place_of(2), 2 * BLOCK, rate, edge_taps(taps_ref), False)
    pack(total, edges, out_ref)
    inside_ref[0:modes, :] = carry
    inside_ref[modes : 2 * modes, :] = halo
    for i in range(2):
        inside_ref[2 * modes + i : 2 * modes + i + 1, :] = first[i]


def merge_kernel(
    own_ref, one_ref, three_ref, two_ref, inside_ref, lower_ref, rates_ref, taps_ref, out_ref
):
    modes = rates_ref.shape[0]
    core = core_index()
    column, line = place_of(2), place_of(8)
    rate = rates_ref[...]
    refs = (own_ref, one_ref, two_ref, three_ref)
    taps = edge_taps(taps_ref)
    single = power(rate, 1)
    above, first, halo, _, _ = chain(refs, line, 8 * BLOCK, rate, taps, True)
    steps = (column * (2 * BLOCK)).astype(jnp.float32) * (-1.0 / LENGTH)
    behind = (column * (2 * BLOCK) - 2).astype(jnp.float32) * (-1.0 / LENGTH)
    inside = inside_ref[0:modes, :]
    opened = inside + jnp.exp(rate * behind) * (single * first[0] + first[1])
    carry = jnp.exp(rate * steps) * above + jnp.where(column > 0, opened, inside)
    within = [inside_ref[2 * modes + i : 2 * modes + i + 1, :] for i in range(2)]
    first = [jnp.where(column > 0, a, b) for a, b in zip(within, first)]
    halo = jnp.where(column > 0, inside_ref[modes : 2 * modes, :], halo)
    lower = lower_ref[...]
    inner = power(rate, BLOCK - 2) * (single * first[0] + first[1])
    carries = carry, power(rate, BLOCK) * carry + lower[:modes] + inner
    halos = halo[TAIL : TAIL + 8], lower[modes + TAIL : modes + TAIL + 8]
    out_ref[0:modes, :] = jnp.where(core == 0, *carries)
    out_ref[modes:, :] = jnp.where(core == 0, *halos)


def local_kernel(*refs):
    blocks = with_sources(refs[: PIECES])
    taps_ref, rates_ref, residues_ref, bias_ref, ends_ref, signal_ref, local_ref, front_ref, zero = refs[PIECES :]
    modes, channels = rates_ref.shape
    fill_tokens(blocks, 0, zero)
    rows = row_iota()
    step = rows.astype(jnp.float32)
    for start in range(0, channels, LANES):
        lanes = pl.ds(start, LANES)
        front = featurize(zero, 0, lanes, taps_ref)
        for i in range(SUB):
            front_ref[i, :, lanes] = front[i]
        signal = [signal_ref[i, :, lanes] for i in range(SUB)]
        taps = [jnp.zeros((8, LANES), jnp.float32) for _ in range(SUB // 8)]
        for mode in range(modes):
            rate = spread(rates_ref[mode : mode + 1, lanes])
            residue = spread(residues_ref[mode : mode + 1, lanes])
            for part in range(SUB // 8):
                taps[part] = taps[part] + residue * jnp.exp(-rate * ((step + 8.0 * part) * (1.0 / LENGTH)))
        bias = spread(bias_ref[0:1, lanes])
        total = [bias * signal[i] for i in range(SUB)]
        for lag in range(SUB):
            tap = spread(taps[lag // 8][lag % 8 : lag % 8 + 1])
            for i in range(lag, SUB):
                total[i] = total[i] + tap * signal[i - lag]
        for mode in range(modes):
            rate = spread(rates_ref[mode : mode + 1, lanes])
            residue = spread(residues_ref[mode : mode + 1, lanes])
            decay = jnp.exp(rate * (-1.0 / LENGTH))
            state = ends_ref[mode, :, lanes]
            for far in (1, 2, 4):
                state = state + jnp.where(rows >= far, power(rate, far * SUB) * pltpu.roll(state, far, 0), 0.0)
            carried = jnp.where(rows >= 1, pltpu.roll(state, 1, 0), 0.0) * residue
            for i in range(SUB):
                carried = carried * decay
                total[i] = total[i] + carried
        for i in range(SUB):
            local_ref[i, :, lanes] = total[i]


def final_kernel(
    carry_ref, summary_ref, taps_ref, rates_ref, residues_ref, bias_ref, decay_ref, weight_ref, local_ref, front_ref, out_ref, natural
):
    modes, channels = rates_ref.shape
    rows = row_iota()

    def at_first(row):
        return jnp.where(rows == 0, spread(row), 0.0)

    for start in range(0, channels, LANES):
        lanes = pl.ds(start, LANES)
        halo = carry_ref[modes:, lanes]
        taps = [[taps_ref[j, s : s + 1, lanes] for j in range(3)] for s in (1, 2, 0)]
        s0, s1 = edge_signal(halo, summary_ref[modes:, lanes], taps[:2])
        _, t1, t2 = taps[2]
        bias = bias_ref[0:1, lanes]
        grow = power(rates_ref[:, lanes], -1)
        carry = carry_ref[:modes, lanes] + grow * (s0 + grow * s1)
        excess = jnp.sum(residues_ref[:, lanes] * grow, axis=0, keepdims=True) * s1
        total = [local_ref[i, :, lanes] for i in range(SUB)]
        front = [front_ref[i, :, lanes] for i in range(SUB)]
        total[0] = total[0] + at_first(bias * s0 - excess)
        total[1] = total[1] + at_first(bias * s1)
        front[0] = front[0] + at_first(t1 * halo[5:6] + t2 * halo[4:5])
        front[1] = front[1] + at_first(t2 * halo[5:6])
        for mode in range(modes):
            decay = spread(decay_ref[mode : mode + 1, lanes])
            carried = spread(carry[mode : mode + 1]) * weight_ref[mode, :, lanes]
            total[0] = total[0] + carried
            for i in range(1, SUB):
                carried = carried * decay
                total[i] = total[i] + carried
        for i in range(SUB):
            natural[start // LANES, pl.ds(i, 8, stride=SUB), :] = front[i] * total[i]
        out_ref[:, lanes] = natural[start // LANES].astype(out_ref.dtype)


def body(streams, short_taps, residues, rates, bias):
    parts = lax.axis_size("tp")
    ctx = lax.axis_size("ctx")
    modes, channels = rates.shape
    tokens = SUB * parts
    f32 = jnp.float32
    wide = jax.ShapeDtypeStruct((SUB, parts, channels), f32)
    packed = jax.ShapeDtypeStruct((modes + SUB, channels), f32)
    carried = jax.ShapeDtypeStruct((modes + 8, channels), f32)
    plane = pltpu.VMEM((channels // LANES, tokens, LANES), f32)
    bias = bias[None]

    def kernel(function, out_shape, operands, scratch=(), cost=None, name=None):
        several = isinstance(out_shape, tuple)
        return pl.pallas_call(
            function,
            out_shape=out_shape,
            in_specs=[VMEM] * len(operands),
            out_specs=(VMEM,) * len(out_shape) if several else VMEM,
            scratch_shapes=list(scratch),
            compiler_params=pltpu.CompilerParams(vmem_limit_bytes=24 << 20),
            cost_estimate=cost,
            name=name or function.__name__,
        )(*operands)

    spans = jax.ShapeDtypeStruct((modes, parts, channels), f32)
    small = pl.CostEstimate(flops=8 << 20, bytes_accessed=2 << 20, transcendentals=0)
    decay, ends_weight, carry_weight = kernel(
        weights_kernel, (jax.ShapeDtypeStruct(rates.shape, f32), spans, spans), (rates, residues, bias), cost=small
    )
    by_stream = jnp.transpose(streams, (1, 0, 2))
    turn = 1 - 2 * core_index()
    swap = [(i, i ^ 1) for i in range(ctx)]

    def block_for(shift):
        at = ((lax.axis_index("tp") + turn * shift) % parts) * channels
        return lax.dynamic_slice(by_stream, (0, 0, at), (3, SUB, channels))

    def along(value, shift):
        route = []
        for c in range(ctx):
            step = -shift if c % 2 else shift
            route += [(c * parts + z, c * parts + (z + step) % parts) for z in range(parts)]
        return lax.ppermute(value, ("ctx", "tp"), route)

    passed = lax.ppermute(block_for(-3), "ctx", swap)
    far = along(block_for(4), 4)
    one = jax.ShapeDtypeStruct((3, SUB, channels), streams.dtype)
    two = jax.ShapeDtypeStruct((2, 3, SUB, channels), streams.dtype)
    third = along(kernel(join_kernel, two, (block_for(3), passed)), 3)
    near = {k: along(block_for(k), k) for k in (2, -2)}
    near |= {k: along(kernel(hold_kernel, one, (block_for(k), far)), k) for k in (1, -1)}
    back = lax.ppermute(kernel(back_kernel, one, (third, near[1])), "ctx", swap)
    blocks = [near[1], near[-1], near[2], near[-2], third, far, back, block_for(0)]
    summary, ends, signal = kernel(
        state_kernel,
        (packed, spans, wide),
        (*blocks, short_taps, decay, ends_weight),
        [plane, plane],
    )
    got = lax.ppermute(summary, "ctx", swap)
    group = jax.ShapeDtypeStruct((3 * SUB, channels), jnp.bfloat16)

    def around(value, stride):
        parts = {}
        for by in (3, 1, 2):
            route = [(i, i + ((i // stride + by) % 4 - i // stride % 4) * stride) for i in range(ctx)]
            parts[by] = lax.ppermute(value, "ctx", route)
        return parts[1], parts[3], parts[2]

    pair, lower = kernel(pair_kernel, (group, packed), (summary, got, rates, short_taps))
    row, inside = kernel(
        row_kernel,
        (group, jax.ShapeDtypeStruct((2 * modes + 8, channels), f32)),
        (pair, *around(pair, 2), rates, short_taps),
    )
    carry = kernel(merge_kernel, carried, (row, *around(row, 8), inside, lower, rates, short_taps))
    local, front = kernel(
        local_kernel,
        (wide, wide),
        (*blocks, short_taps, rates, residues, bias, ends, signal),
        [plane],
        cost=small,
    )
    return kernel(
        final_kernel,
        jax.ShapeDtypeStruct((tokens, channels), jnp.bfloat16),
        (carry, summary, short_taps, rates, residues, bias, decay, carry_weight, local, front),
        [plane],
    )


def solution(mesh):
    in_specs = (
        P(("ctx", "tp"), None, None),
        P(None, None, "tp"),
        P(None, "tp"),
        P(None, "tp"),
        P("tp"),
    )
    out_specs = P("ctx", "tp")
    return jax.shard_map(body, mesh=mesh, in_specs=in_specs, out_specs=out_specs, check_vma=False)
```

```python
import functools

import jax
import jax.numpy as jnp
from jax import lax
from jax.experimental import pallas as pl
from jax.experimental.pallas import tpu as pltpu
from jax.sharding import PartitionSpec as P

LENGTH = 4096
SUB = 16
PIECES = 6
LANES = 128
BLOCK = 128
VMEM = pl.BlockSpec(memory_space=pltpu.VMEM)


def row_iota():
    return lax.broadcasted_iota(jnp.int32, (8, LANES), 0)


def spread(row):
    return jnp.broadcast_to(row, (8, LANES))


def fill_tokens(blocks, stream, scratch):
    for block, source in blocks:
        at = pl.multiple_of(source * SUB, SUB)
        for group in range(scratch.shape[0]):
            lanes = pl.ds(group * LANES, LANES)
            scratch[group, pl.ds(at, SUB), :] = block[stream, :, lanes].astype(jnp.float32)


def join_kernel(at, own_ref, passed_ref, out_ref):
    out_ref[0] = own_ref[...]
    out_ref[1] = passed_ref[at]


def back_kernel(first_ref, second_ref, third_ref, _, out_ref):
    for at, ref in enumerate((first_ref, second_ref, third_ref)):
        out_ref[at] = ref[1]


def with_sources(refs):
    first, second, third, back, far, own = refs
    me = lax.axis_index("tp")
    turn = 1 - 2 * core_index()
    places = [(own, 0), (far, 4), (first.at[0], 1), (second.at[0], 2), (third.at[0], 3)]
    places += [(back.at[k - 1], -k) for k in (1, 2, 3)]
    return [(ref, lax.rem(me - turn * shift + 8, 8)) for ref, shift in places]


def featurize(scratch, stream, lanes, taps_ref):
    group = lanes.start // LANES
    values = [scratch[group, pl.ds(i, 8, stride=SUB), :] for i in range(SUB)]
    first = row_iota() == 0
    joined = [jnp.where(first, 0.0, pltpu.roll(values[SUB - far], 1, 0)) for far in (2, 1)] + values
    t0, t1, t2 = (spread(taps_ref[j, stream : stream + 1, lanes]) for j in range(3))
    return [t0 * joined[i + 2] + t1 * joined[i + 1] + t2 * joined[i] for i in range(SUB)]


def power(rate, tokens):
    return jnp.exp(rate * (-float(tokens) / LENGTH))


def core_index():
    return lax.rem(lax.axis_index("ctx"), 2)


TAIL = 4


def edge_signal(tail, head, taps):
    result = None
    for n, (t0, t1, t2) in enumerate(taps):
        x0, x1 = (head[2 * n + i : 2 * n + i + 1] for i in range(2))
        h0, h1 = (tail[2 * n + i : 2 * n + i + 1] for i in range(2))
        feats = (t0 * x0 + t1 * h1 + t2 * h0, t0 * x1 + t1 * x0 + t2 * h1)
        result = feats if result is None else tuple(a * b for a, b in zip(result, feats))
    return result


def edge_taps(taps_ref):
    return [[taps_ref[j, s : s + 1, :] for j in range(3)] for s in (1, 2)]


def weights_kernel(rates_ref, residues_ref, _, decay_ref, ends_ref, carry_ref):
    modes, channels = rates_ref.shape
    step = row_iota().astype(jnp.float32)
    remaining = (7.0 - step) * (SUB / LENGTH)
    elapsed = (step * SUB + 1.0) * (1.0 / LENGTH)
    decay_ref[...] = power(rates_ref[...], 1)
    for start in range(0, channels, LANES):
        lanes = pl.ds(start, LANES)
        for mode in range(modes):
            rate = spread(rates_ref[mode : mode + 1, lanes])
            ends_ref[mode, :, lanes] = jnp.exp(-rate * remaining)
            carry_ref[mode, :, lanes] = spread(residues_ref[mode : mode + 1, lanes]) * jnp.exp(-rate * elapsed)


def state_kernel(*refs):
    blocks = with_sources(refs[: PIECES])
    taps_ref, decay_ref, weight_ref, full, ends_ref, signal_ref, one, two = refs[PIECES :]
    modes, channels = decay_ref.shape
    fill_tokens(blocks, 1, one)
    fill_tokens(blocks, 2, two)
    rows = row_iota()
    full[modes:, :] = jnp.zeros((SUB, channels), jnp.float32)
    for group in range(channels // LANES):
        lanes = pl.ds(group * LANES, LANES)
        for n, scratch in enumerate((one, two)):
            full[modes + 2 * n : modes + 2 * n + 2, lanes] = scratch[group, 0:2, :]
            full[modes + TAIL + 2 * n : modes + TAIL + 2 * n + 2, lanes] = scratch[group, BLOCK - 2 : BLOCK, :]
    for block, source in blocks:

        @pl.when(source == 7)
        def _(block=block):
            full[modes + TAIL + 4 : modes + TAIL + 6, :] = block[0].astype(jnp.float32)[SUB - 2 :]

    for start in range(0, channels, LANES):
        lanes = pl.ds(start, LANES)
        left = featurize(one, 1, lanes, taps_ref)
        right = featurize(two, 2, lanes, taps_ref)
        signal = [a * b for a, b in zip(left, right)]
        for i in range(2):
            signal[i] = jnp.where(rows == 0, 0.0, signal[i])
        for i in range(SUB):
            signal_ref[i, :, lanes] = signal[i]
        for mode in range(modes):
            decay = spread(decay_ref[mode : mode + 1, lanes])
            state = signal[0]
            for i in range(1, SUB):
                state = state * decay + signal[i]
            ends_ref[mode, :, lanes] = state
            full[mode : mode + 1, lanes] = jnp.sum(state * weight_ref[mode, :, lanes], axis=0, keepdims=True)


def pack(state, edge, out_ref):
    high = state.astype(jnp.bfloat16)
    out_ref[0:SUB, :] = high
    out_ref[SUB : 2 * SUB, :] = (state - high.astype(jnp.float32)).astype(jnp.bfloat16)
    out_ref[2 * SUB : 3 * SUB, :] = edge.astype(jnp.bfloat16)


def join_edges(first, last):
    rows = lax.broadcasted_iota(jnp.int32, first.shape, 0)
    return jnp.where(rows < TAIL, first, last)


def pair_kernel(kept_ref, got_ref, rates_ref, taps_ref, out_ref, lower_ref):
    modes = rates_ref.shape[0]
    core = core_index()
    rate = rates_ref[...]
    kept, got = kept_ref[...], got_ref[...]
    lower = jnp.where(core == 0, kept, got)
    upper = jnp.where(core == 0, got, kept)
    s0, s1 = edge_signal(lower[modes + TAIL :], upper[modes:], edge_taps(taps_ref))
    inner = power(rate, BLOCK - 2) * (power(rate, 1) * s0 + s1)
    state = upper[:modes] + inner + power(rate, BLOCK) * lower[:modes]
    pack(state, join_edges(lower[modes:], upper[modes:]), out_ref)
    lower_ref[...] = lower


def chain(refs, place, tokens, rate, taps, opened):
    single, whole, last = power(rate, 1), power(rate, tokens), power(rate, tokens - 2)
    size = len(refs)
    carry = halo = before = total = jnp.zeros_like(rate)
    first = (jnp.zeros_like(rate[:1]),) * 2
    head = None
    for k in range(size):
        piece = refs[0][...]
        for by in range(1, size):
            piece = jnp.where(lax.rem(place - k + size, size) == by, refs[by][...], piece)
        state = piece[0:SUB].astype(jnp.float32) + piece[SUB : 2 * SUB].astype(jnp.float32)
        edge = piece[2 * SUB :].astype(jnp.float32)
        pieces = edge_signal(before[TAIL:], edge, taps)
        carry = jnp.where(place == k, total, carry)
        halo = jnp.where(place == k, before, halo)
        first = [jnp.where(place == k, new, old) for new, old in zip(pieces, first)]
        inner = last * (single * pieces[0] + pieces[1])
        if k == 0:
            head = edge
            total = state + inner if opened else state
        else:
            total = total * whole + state + inner
        before = edge
    return carry, first, halo, total, join_edges(head, before)


def place_of(stride):
    return lax.rem(lax.div(lax.axis_index("ctx"), stride), 4)


def row_kernel(own_ref, one_ref, three_ref, two_ref, rates_ref, taps_ref, out_ref, inside_ref):
    modes = rates_ref.shape[0]
    rate = rates_ref[...]
    refs = (own_ref, one_ref, two_ref, three_ref)
    carry, first, halo, total, edges = chain(refs, place_of(2), 2 * BLOCK, rate, edge_taps(taps_ref), False)
    pack(total, edges, out_ref)
    inside_ref[0:modes, :] = carry
    inside_ref[modes : 2 * modes, :] = halo
    for i in range(2):
        inside_ref[2 * modes + i : 2 * modes + i + 1, :] = first[i]


def merge_kernel(
    own_ref, one_ref, three_ref, two_ref, inside_ref, lower_ref, rates_ref, taps_ref, out_ref
):
    modes = rates_ref.shape[0]
    core = core_index()
    column, line = place_of(2), place_of(8)
    rate = rates_ref[...]
    refs = (own_ref, one_ref, two_ref, three_ref)
    taps = edge_taps(taps_ref)
    single = power(rate, 1)
    above, first, halo, _, _ = chain(refs, line, 8 * BLOCK, rate, taps, True)
    steps = (column * (2 * BLOCK)).astype(jnp.float32) * (-1.0 / LENGTH)
    behind = (column * (2 * BLOCK) - 2).astype(jnp.float32) * (-1.0 / LENGTH)
    inside = inside_ref[0:modes, :]
    opened = inside + jnp.exp(rate * behind) * (single * first[0] + first[1])
    carry = jnp.exp(rate * steps) * above + jnp.where(column > 0, opened, inside)
    within = [inside_ref[2 * modes + i : 2 * modes + i + 1, :] for i in range(2)]
    first = [jnp.where(column > 0, a, b) for a, b in zip(within, first)]
    halo = jnp.where(column > 0, inside_ref[modes : 2 * modes, :], halo)
    lower = lower_ref[...]
    inner = power(rate, BLOCK - 2) * (single * first[0] + first[1])
    carries = carry, power(rate, BLOCK) * carry + lower[:modes] + inner
    halos = halo[TAIL : TAIL + 8], lower[modes + TAIL : modes + TAIL + 8]
    out_ref[0:modes, :] = jnp.where(core == 0, *carries)
    out_ref[modes:, :] = jnp.where(core == 0, *halos)


def local_kernel(*refs):
    blocks = with_sources(refs[: PIECES])
    taps_ref, rates_ref, residues_ref, bias_ref, ends_ref, signal_ref, local_ref, front_ref, zero = refs[PIECES :]
    modes, channels = rates_ref.shape
    fill_tokens(blocks, 0, zero)
    rows = row_iota()
    step = rows.astype(jnp.float32)
    for start in range(0, channels, LANES):
        lanes = pl.ds(start, LANES)
        front = featurize(zero, 0, lanes, taps_ref)
        for i in range(SUB):
            front_ref[i, :, lanes] = front[i]
        signal = [signal_ref[i, :, lanes] for i in range(SUB)]
        taps = [jnp.zeros((8, LANES), jnp.float32) for _ in range(SUB // 8)]
        for mode in range(modes):
            rate = spread(rates_ref[mode : mode + 1, lanes])
            residue = spread(residues_ref[mode : mode + 1, lanes])
            for part in range(SUB // 8):
                taps[part] = taps[part] + residue * jnp.exp(-rate * ((step + 8.0 * part) * (1.0 / LENGTH)))
        bias = spread(bias_ref[0:1, lanes])
        total = [bias * signal[i] for i in range(SUB)]
        for lag in range(SUB):
            tap = spread(taps[lag // 8][lag % 8 : lag % 8 + 1])
            for i in range(lag, SUB):
                total[i] = total[i] + tap * signal[i - lag]
        for mode in range(modes):
            rate = spread(rates_ref[mode : mode + 1, lanes])
            residue = spread(residues_ref[mode : mode + 1, lanes])
            decay = jnp.exp(rate * (-1.0 / LENGTH))
            state = ends_ref[mode, :, lanes]
            for far in (1, 2, 4):
                state = state + jnp.where(rows >= far, power(rate, far * SUB) * pltpu.roll(state, far, 0), 0.0)
            carried = jnp.where(rows >= 1, pltpu.roll(state, 1, 0), 0.0) * residue
            for i in range(SUB):
                carried = carried * decay
                total[i] = total[i] + carried
        for i in range(SUB):
            local_ref[i, :, lanes] = total[i]


def final_kernel(
    carry_ref, summary_ref, taps_ref, rates_ref, residues_ref, bias_ref, decay_ref, weight_ref, local_ref, front_ref, out_ref, natural
):
    modes, channels = rates_ref.shape
    rows = row_iota()

    def at_first(row):
        return jnp.where(rows == 0, spread(row), 0.0)

    for start in range(0, channels, LANES):
        lanes = pl.ds(start, LANES)
        halo = carry_ref[modes:, lanes]
        taps = [[taps_ref[j, s : s + 1, lanes] for j in range(3)] for s in (1, 2, 0)]
        s0, s1 = edge_signal(halo, summary_ref[modes:, lanes], taps[:2])
        _, t1, t2 = taps[2]
        bias = bias_ref[0:1, lanes]
        grow = power(rates_ref[:, lanes], -1)
        carry = carry_ref[:modes, lanes] + grow * (s0 + grow * s1)
        excess = jnp.sum(residues_ref[:, lanes] * grow, axis=0, keepdims=True) * s1
        total = [local_ref[i, :, lanes] for i in range(SUB)]
        front = [front_ref[i, :, lanes] for i in range(SUB)]
        total[0] = total[0] + at_first(bias * s0 - excess)
        total[1] = total[1] + at_first(bias * s1)
        front[0] = front[0] + at_first(t1 * halo[5:6] + t2 * halo[4:5])
        front[1] = front[1] + at_first(t2 * halo[5:6])
        for mode in range(modes):
            decay = spread(decay_ref[mode : mode + 1, lanes])
            carried = spread(carry[mode : mode + 1]) * weight_ref[mode, :, lanes]
            total[0] = total[0] + carried
            for i in range(1, SUB):
                carried = carried * decay
                total[i] = total[i] + carried
        for i in range(SUB):
            natural[start // LANES, pl.ds(i, 8, stride=SUB), :] = front[i] * total[i]
        out_ref[:, lanes] = natural[start // LANES].astype(out_ref.dtype)


def body(streams, short_taps, residues, rates, bias):
    parts = lax.axis_size("tp")
    ctx = lax.axis_size("ctx")
    modes, channels = rates.shape
    tokens = SUB * parts
    f32 = jnp.float32
    wide = jax.ShapeDtypeStruct((SUB, parts, channels), f32)
    packed = jax.ShapeDtypeStruct((modes + SUB, channels), f32)
    carried = jax.ShapeDtypeStruct((modes + 8, channels), f32)
    plane = pltpu.VMEM((channels // LANES, tokens, LANES), f32)
    bias = bias[None]

    def kernel(function, out_shape, operands, scratch=(), cost=None, name=None):
        several = isinstance(out_shape, tuple)
        return pl.pallas_call(
            function,
            out_shape=out_shape,
            in_specs=[VMEM] * len(operands),
            out_specs=(VMEM,) * len(out_shape) if several else VMEM,
            scratch_shapes=list(scratch),
            compiler_params=pltpu.CompilerParams(vmem_limit_bytes=24 << 20),
            cost_estimate=cost,
            name=name or function.__name__,
        )(*operands)

    spans = jax.ShapeDtypeStruct((modes, parts, channels), f32)
    small = pl.CostEstimate(flops=8 << 20, bytes_accessed=2 << 20, transcendentals=0)
    decay, ends_weight, carry_weight = kernel(
        weights_kernel, (jax.ShapeDtypeStruct(rates.shape, f32), spans, spans), (rates, residues, bias), cost=small
    )
    by_stream = jnp.transpose(streams, (1, 0, 2))
    turn = 1 - 2 * core_index()
    swap = [(i, i ^ 1) for i in range(ctx)]

    def block_for(shift):
        at = ((lax.axis_index("tp") + turn * shift) % parts) * channels
        return lax.dynamic_slice(by_stream, (0, 0, at), (3, SUB, channels))

    def along(value, shift):
        route = []
        for c in range(ctx):
            step = -shift if c % 2 else shift
            route += [(c * parts + z, c * parts + (z + step) % parts) for z in range(parts)]
        return lax.ppermute(value, ("ctx", "tp"), route)

    passed = lax.ppermute(jnp.stack([block_for(-k) for k in (1, 2, 3)]), "ctx", swap)
    far = along(block_for(4), 4)
    two = jax.ShapeDtypeStruct((2, 3, SUB, channels), streams.dtype)
    three = jax.ShapeDtypeStruct((3, 3, SUB, channels), streams.dtype)

    def both(shift):
        return kernel(functools.partial(join_kernel, shift - 1), two, (block_for(shift), passed), name="join")

    first, second, third = (along(both(k), k) for k in (1, 2, 3))
    back = lax.ppermute(kernel(back_kernel, three, (first, second, third, far)), "ctx", swap)
    blocks = [first, second, third, back, far, block_for(0)]
    summary, ends, signal = kernel(
        state_kernel,
        (packed, spans, wide),
        (*blocks, short_taps, decay, ends_weight),
        [plane, plane],
    )
    got = lax.ppermute(summary, "ctx", swap)
    group = jax.ShapeDtypeStruct((3 * SUB, channels), jnp.bfloat16)

    def around(value, stride):
        parts = {}
        for by in (3, 1, 2):
            route = [(i, i + ((i // stride + by) % 4 - i // stride % 4) * stride) for i in range(ctx)]
            parts[by] = lax.ppermute(value, "ctx", route)
        return parts[1], parts[3], parts[2]

    pair, lower = kernel(pair_kernel, (group, packed), (summary, got, rates, short_taps))
    row, inside = kernel(
        row_kernel,
        (group, jax.ShapeDtypeStruct((2 * modes + 8, channels), f32)),
        (pair, *around(pair, 2), rates, short_taps),
    )
    carry = kernel(merge_kernel, carried, (row, *around(row, 8), inside, lower, rates, short_taps))
    local, front = kernel(
        local_kernel,
        (wide, wide),
        (*blocks, short_taps, rates, residues, bias, ends, signal),
        [plane],
        cost=small,
    )
    return kernel(
        final_kernel,
        jax.ShapeDtypeStruct((tokens, channels), jnp.bfloat16),
        (carry, summary, short_taps, rates, residues, bias, decay, carry_weight, local, front),
        [plane],
    )


def solution(mesh):
    in_specs = (
        P(("ctx", "tp"), None, None),
        P(None, None, "tp"),
        P(None, "tp"),
        P(None, "tp"),
        P("tp"),
    )
    out_specs = P("ctx", "tp")
    return jax.shard_map(body, mesh=mesh, in_specs=in_specs, out_specs=out_specs, check_vma=False)
```

```python
import functools

import jax
import jax.numpy as jnp
from jax import lax
from jax.experimental import pallas as pl
from jax.experimental.pallas import tpu as pltpu
from jax.sharding import PartitionSpec as P

LENGTH = 4096
SUB = 16
PIECES = 6
LANES = 128
BLOCK = 128
VMEM = pl.BlockSpec(memory_space=pltpu.VMEM)


def row_iota():
    return lax.broadcasted_iota(jnp.int32, (8, LANES), 0)


def spread(row):
    return jnp.broadcast_to(row, (8, LANES))


def fill_tokens(blocks, stream, scratch):
    for block, source in blocks:
        at = pl.multiple_of(source * SUB, SUB)
        for group in range(scratch.shape[0]):
            lanes = pl.ds(group * LANES, LANES)
            scratch[group, pl.ds(at, SUB), :] = block[stream, :, lanes].astype(jnp.float32)


def join_kernel(at, own_ref, passed_ref, *refs):
    out_ref = refs[-1]
    out_ref[0] = own_ref[...]
    out_ref[1] = passed_ref[at]


def back_kernel(third_ref, second_ref, first_ref, out_ref):
    for at, ref in enumerate((first_ref, second_ref, third_ref)):
        out_ref[at] = ref[1]


def with_sources(refs):
    far, third, second, first, back, own = refs
    me = lax.axis_index("tp")
    turn = 1 - 2 * core_index()
    places = [(own, 0), (far, 4), (first.at[0], 1), (second.at[0], 2), (third.at[0], 3)]
    places += [(back.at[k - 1], -k) for k in (1, 2, 3)]
    return [(ref, lax.rem(me - turn * shift + 8, 8)) for ref, shift in places]


def featurize(scratch, stream, lanes, taps_ref):
    group = lanes.start // LANES
    values = [scratch[group, pl.ds(i, 8, stride=SUB), :] for i in range(SUB)]
    first = row_iota() == 0
    joined = [jnp.where(first, 0.0, pltpu.roll(values[SUB - far], 1, 0)) for far in (2, 1)] + values
    t0, t1, t2 = (spread(taps_ref[j, stream : stream + 1, lanes]) for j in range(3))
    return [t0 * joined[i + 2] + t1 * joined[i + 1] + t2 * joined[i] for i in range(SUB)]


def power(rate, tokens):
    return jnp.exp(rate * (-float(tokens) / LENGTH))


def core_index():
    return lax.rem(lax.axis_index("ctx"), 2)


TAIL = 4


def edge_signal(tail, head, taps):
    result = None
    for n, (t0, t1, t2) in enumerate(taps):
        x0, x1 = (head[2 * n + i : 2 * n + i + 1] for i in range(2))
        h0, h1 = (tail[2 * n + i : 2 * n + i + 1] for i in range(2))
        feats = (t0 * x0 + t1 * h1 + t2 * h0, t0 * x1 + t1 * x0 + t2 * h1)
        result = feats if result is None else tuple(a * b for a, b in zip(result, feats))
    return result


def edge_taps(taps_ref):
    return [[taps_ref[j, s : s + 1, :] for j in range(3)] for s in (1, 2)]


def weights_kernel(rates_ref, residues_ref, _, decay_ref, ends_ref, carry_ref):
    modes, channels = rates_ref.shape
    step = row_iota().astype(jnp.float32)
    remaining = (7.0 - step) * (SUB / LENGTH)
    elapsed = (step * SUB + 1.0) * (1.0 / LENGTH)
    decay_ref[...] = power(rates_ref[...], 1)
    for start in range(0, channels, LANES):
        lanes = pl.ds(start, LANES)
        for mode in range(modes):
            rate = spread(rates_ref[mode : mode + 1, lanes])
            ends_ref[mode, :, lanes] = jnp.exp(-rate * remaining)
            carry_ref[mode, :, lanes] = spread(residues_ref[mode : mode + 1, lanes]) * jnp.exp(-rate * elapsed)


def state_kernel(*refs):
    blocks = with_sources(refs[: PIECES])
    taps_ref, decay_ref, weight_ref, full, ends_ref, signal_ref, one, two = refs[PIECES :]
    modes, channels = decay_ref.shape
    fill_tokens(blocks, 1, one)
    fill_tokens(blocks, 2, two)
    rows = row_iota()
    full[modes:, :] = jnp.zeros((SUB, channels), jnp.float32)
    for group in range(channels // LANES):
        lanes = pl.ds(group * LANES, LANES)
        for n, scratch in enumerate((one, two)):
            full[modes + 2 * n : modes + 2 * n + 2, lanes] = scratch[group, 0:2, :]
            full[modes + TAIL + 2 * n : modes + TAIL + 2 * n + 2, lanes] = scratch[group, BLOCK - 2 : BLOCK, :]
    for block, source in blocks:

        @pl.when(source == 7)
        def _(block=block):
            full[modes + TAIL + 4 : modes + TAIL + 6, :] = block[0].astype(jnp.float32)[SUB - 2 :]

    for start in range(0, channels, LANES):
        lanes = pl.ds(start, LANES)
        left = featurize(one, 1, lanes, taps_ref)
        right = featurize(two, 2, lanes, taps_ref)
        signal = [a * b for a, b in zip(left, right)]
        for i in range(2):
            signal[i] = jnp.where(rows == 0, 0.0, signal[i])
        for i in range(SUB):
            signal_ref[i, :, lanes] = signal[i]
        for mode in range(modes):
            decay = spread(decay_ref[mode : mode + 1, lanes])
            state = signal[0]
            for i in range(1, SUB):
                state = state * decay + signal[i]
            ends_ref[mode, :, lanes] = state
            full[mode : mode + 1, lanes] = jnp.sum(state * weight_ref[mode, :, lanes], axis=0, keepdims=True)


def pack(state, edge, out_ref):
    high = state.astype(jnp.bfloat16)
    out_ref[0:SUB, :] = high
    out_ref[SUB : 2 * SUB, :] = (state - high.astype(jnp.float32)).astype(jnp.bfloat16)
    out_ref[2 * SUB : 3 * SUB, :] = edge.astype(jnp.bfloat16)


def join_edges(first, last):
    rows = lax.broadcasted_iota(jnp.int32, first.shape, 0)
    return jnp.where(rows < TAIL, first, last)


def pair_kernel(kept_ref, got_ref, rates_ref, taps_ref, out_ref, lower_ref):
    modes = rates_ref.shape[0]
    core = core_index()
    rate = rates_ref[...]
    kept, got = kept_ref[...], got_ref[...]
    lower = jnp.where(core == 0, kept, got)
    upper = jnp.where(core == 0, got, kept)
    s0, s1 = edge_signal(lower[modes + TAIL :], upper[modes:], edge_taps(taps_ref))
    inner = power(rate, BLOCK - 2) * (power(rate, 1) * s0 + s1)
    state = upper[:modes] + inner + power(rate, BLOCK) * lower[:modes]
    pack(state, join_edges(lower[modes:], upper[modes:]), out_ref)
    lower_ref[...] = lower


def chain(refs, place, tokens, rate, taps, opened):
    single, whole, last = power(rate, 1), power(rate, tokens), power(rate, tokens - 2)
    size = len(refs)
    carry = halo = before = total = jnp.zeros_like(rate)
    first = (jnp.zeros_like(rate[:1]),) * 2
    head = None
    for k in range(size):
        piece = refs[0][...]
        for by in range(1, size):
            piece = jnp.where(lax.rem(place - k + size, size) == by, refs[by][...], piece)
        state = piece[0:SUB].astype(jnp.float32) + piece[SUB : 2 * SUB].astype(jnp.float32)
        edge = piece[2 * SUB :].astype(jnp.float32)
        pieces = edge_signal(before[TAIL:], edge, taps)
        carry = jnp.where(place == k, total, carry)
        halo = jnp.where(place == k, before, halo)
        first = [jnp.where(place == k, new, old) for new, old in zip(pieces, first)]
        inner = last * (single * pieces[0] + pieces[1])
        if k == 0:
            head = edge
            total = state + inner if opened else state
        else:
            total = total * whole + state + inner
        before = edge
    return carry, first, halo, total, join_edges(head, before)


def place_of(stride):
    return lax.rem(lax.div(lax.axis_index("ctx"), stride), 4)


def row_kernel(own_ref, one_ref, three_ref, two_ref, rates_ref, taps_ref, out_ref, inside_ref):
    modes = rates_ref.shape[0]
    rate = rates_ref[...]
    refs = (own_ref, one_ref, two_ref, three_ref)
    carry, first, halo, total, edges = chain(refs, place_of(2), 2 * BLOCK, rate, edge_taps(taps_ref), False)
    pack(total, edges, out_ref)
    inside_ref[0:modes, :] = carry
    inside_ref[modes : 2 * modes, :] = halo
    for i in range(2):
        inside_ref[2 * modes + i : 2 * modes + i + 1, :] = first[i]


def merge_kernel(
    own_ref, one_ref, three_ref, two_ref, inside_ref, lower_ref, rates_ref, taps_ref, out_ref
):
    modes = rates_ref.shape[0]
    core = core_index()
    column, line = place_of(2), place_of(8)
    rate = rates_ref[...]
    refs = (own_ref, one_ref, two_ref, three_ref)
    taps = edge_taps(taps_ref)
    single = power(rate, 1)
    above, first, halo, _, _ = chain(refs, line, 8 * BLOCK, rate, taps, True)
    steps = (column * (2 * BLOCK)).astype(jnp.float32) * (-1.0 / LENGTH)
    behind = (column * (2 * BLOCK) - 2).astype(jnp.float32) * (-1.0 / LENGTH)
    inside = inside_ref[0:modes, :]
    opened = inside + jnp.exp(rate * behind) * (single * first[0] + first[1])
    carry = jnp.exp(rate * steps) * above + jnp.where(column > 0, opened, inside)
    within = [inside_ref[2 * modes + i : 2 * modes + i + 1, :] for i in range(2)]
    first = [jnp.where(column > 0, a, b) for a, b in zip(within, first)]
    halo = jnp.where(column > 0, inside_ref[modes : 2 * modes, :], halo)
    lower = lower_ref[...]
    inner = power(rate, BLOCK - 2) * (single * first[0] + first[1])
    carries = carry, power(rate, BLOCK) * carry + lower[:modes] + inner
    halos = halo[TAIL : TAIL + 8], lower[modes + TAIL : modes + TAIL + 8]
    out_ref[0:modes, :] = jnp.where(core == 0, *carries)
    out_ref[modes:, :] = jnp.where(core == 0, *halos)


def local_kernel(*refs):
    blocks = with_sources(refs[: PIECES])
    taps_ref, rates_ref, residues_ref, bias_ref, ends_ref, signal_ref, local_ref, front_ref, zero = refs[PIECES :]
    modes, channels = rates_ref.shape
    fill_tokens(blocks, 0, zero)
    rows = row_iota()
    step = rows.astype(jnp.float32)
    for start in range(0, channels, LANES):
        lanes = pl.ds(start, LANES)
        front = featurize(zero, 0, lanes, taps_ref)
        for i in range(SUB):
            front_ref[i, :, lanes] = front[i]
        signal = [signal_ref[i, :, lanes] for i in range(SUB)]
        taps = [jnp.zeros((8, LANES), jnp.float32) for _ in range(SUB // 8)]
        for mode in range(modes):
            rate = spread(rates_ref[mode : mode + 1, lanes])
            residue = spread(residues_ref[mode : mode + 1, lanes])
            for part in range(SUB // 8):
                taps[part] = taps[part] + residue * jnp.exp(-rate * ((step + 8.0 * part) * (1.0 / LENGTH)))
        bias = spread(bias_ref[0:1, lanes])
        total = [bias * signal[i] for i in range(SUB)]
        for lag in range(SUB):
            tap = spread(taps[lag // 8][lag % 8 : lag % 8 + 1])
            for i in range(lag, SUB):
                total[i] = total[i] + tap * signal[i - lag]
        for mode in range(modes):
            rate = spread(rates_ref[mode : mode + 1, lanes])
            residue = spread(residues_ref[mode : mode + 1, lanes])
            decay = jnp.exp(rate * (-1.0 / LENGTH))
            state = ends_ref[mode, :, lanes]
            for far in (1, 2, 4):
                state = state + jnp.where(rows >= far, power(rate, far * SUB) * pltpu.roll(state, far, 0), 0.0)
            carried = jnp.where(rows >= 1, pltpu.roll(state, 1, 0), 0.0) * residue
            for i in range(SUB):
                carried = carried * decay
                total[i] = total[i] + carried
        for i in range(SUB):
            local_ref[i, :, lanes] = total[i]


def final_kernel(
    carry_ref, summary_ref, taps_ref, rates_ref, residues_ref, bias_ref, decay_ref, weight_ref, local_ref, front_ref, out_ref, natural
):
    modes, channels = rates_ref.shape
    rows = row_iota()

    def at_first(row):
        return jnp.where(rows == 0, spread(row), 0.0)

    for start in range(0, channels, LANES):
        lanes = pl.ds(start, LANES)
        halo = carry_ref[modes:, lanes]
        taps = [[taps_ref[j, s : s + 1, lanes] for j in range(3)] for s in (1, 2, 0)]
        s0, s1 = edge_signal(halo, summary_ref[modes:, lanes], taps[:2])
        _, t1, t2 = taps[2]
        bias = bias_ref[0:1, lanes]
        grow = power(rates_ref[:, lanes], -1)
        carry = carry_ref[:modes, lanes] + grow * (s0 + grow * s1)
        excess = jnp.sum(residues_ref[:, lanes] * grow, axis=0, keepdims=True) * s1
        total = [local_ref[i, :, lanes] for i in range(SUB)]
        front = [front_ref[i, :, lanes] for i in range(SUB)]
        total[0] = total[0] + at_first(bias * s0 - excess)
        total[1] = total[1] + at_first(bias * s1)
        front[0] = front[0] + at_first(t1 * halo[5:6] + t2 * halo[4:5])
        front[1] = front[1] + at_first(t2 * halo[5:6])
        for mode in range(modes):
            decay = spread(decay_ref[mode : mode + 1, lanes])
            carried = spread(carry[mode : mode + 1]) * weight_ref[mode, :, lanes]
            total[0] = total[0] + carried
            for i in range(1, SUB):
                carried = carried * decay
                total[i] = total[i] + carried
        for i in range(SUB):
            natural[start // LANES, pl.ds(i, 8, stride=SUB), :] = front[i] * total[i]
        out_ref[:, lanes] = natural[start // LANES].astype(out_ref.dtype)


def body(streams, short_taps, residues, rates, bias):
    parts = lax.axis_size("tp")
    ctx = lax.axis_size("ctx")
    modes, channels = rates.shape
    tokens = SUB * parts
    f32 = jnp.float32
    wide = jax.ShapeDtypeStruct((SUB, parts, channels), f32)
    packed = jax.ShapeDtypeStruct((modes + SUB, channels), f32)
    carried = jax.ShapeDtypeStruct((modes + 8, channels), f32)
    plane = pltpu.VMEM((channels // LANES, tokens, LANES), f32)
    bias = bias[None]

    def kernel(function, out_shape, operands, scratch=(), cost=None, name=None):
        several = isinstance(out_shape, tuple)
        return pl.pallas_call(
            function,
            out_shape=out_shape,
            in_specs=[VMEM] * len(operands),
            out_specs=(VMEM,) * len(out_shape) if several else VMEM,
            scratch_shapes=list(scratch),
            compiler_params=pltpu.CompilerParams(vmem_limit_bytes=24 << 20),
            cost_estimate=cost,
            name=name or function.__name__,
        )(*operands)

    spans = jax.ShapeDtypeStruct((modes, parts, channels), f32)
    small = pl.CostEstimate(flops=8 << 20, bytes_accessed=2 << 20, transcendentals=0)
    decay, ends_weight, carry_weight = kernel(
        weights_kernel, (jax.ShapeDtypeStruct(rates.shape, f32), spans, spans), (rates, residues, bias), cost=small
    )
    by_stream = jnp.transpose(streams, (1, 0, 2))
    turn = 1 - 2 * core_index()
    swap = [(i, i ^ 1) for i in range(ctx)]

    def block_for(shift, source):
        at = ((lax.axis_index("tp") + turn * shift) % parts) * channels
        return lax.dynamic_slice(source, (0, 0, at), (3, SUB, channels))

    def along(value, shift):
        route = []
        for c in range(ctx):
            step = -shift if c % 2 else shift
            route += [(c * parts + z, c * parts + (z + step) % parts) for z in range(parts)]
        return lax.ppermute(value, ("ctx", "tp"), route)

    away = jnp.stack([block_for(-k, by_stream) for k in (1, 2, 3)])
    passed = lax.ppermute(away, "ctx", swap)
    far = along(block_for(4, by_stream), 4)
    later, _ = lax.optimization_barrier((by_stream, away))
    two = jax.ShapeDtypeStruct((2, 3, SUB, channels), streams.dtype)
    three = jax.ShapeDtypeStruct((3, 3, SUB, channels), streams.dtype)

    def both(shift, *after):
        return kernel(functools.partial(join_kernel, shift - 1), two, (block_for(shift, later), passed, *after), name="join")

    third, second = (along(both(k), k) for k in (3, 2))
    first = along(both(1, far), 1)
    back = lax.ppermute(kernel(back_kernel, three, (third, second, first)), "ctx", swap)
    blocks = [far, third, second, first, back, block_for(0, later)]
    summary, ends, signal = kernel(
        state_kernel,
        (packed, spans, wide),
        (*blocks, short_taps, decay, ends_weight),
        [plane, plane],
    )
    got = lax.ppermute(summary, "ctx", swap)
    group = jax.ShapeDtypeStruct((3 * SUB, channels), jnp.bfloat16)

    def around(value, stride):
        parts = {}
        for by in (3, 1, 2):
            route = [(i, i + ((i // stride + by) % 4 - i // stride % 4) * stride) for i in range(ctx)]
            parts[by] = lax.ppermute(value, "ctx", route)
        return parts[1], parts[3], parts[2]

    pair, lower = kernel(pair_kernel, (group, packed), (summary, got, rates, short_taps))
    row, inside = kernel(
        row_kernel,
        (group, jax.ShapeDtypeStruct((2 * modes + 8, channels), f32)),
        (pair, *around(pair, 2), rates, short_taps),
    )
    carry = kernel(merge_kernel, carried, (row, *around(row, 8), inside, lower, rates, short_taps))
    local, front = kernel(
        local_kernel,
        (wide, wide),
        (*blocks, short_taps, rates, residues, bias, ends, signal),
        [plane],
        cost=small,
    )
    return kernel(
        final_kernel,
        jax.ShapeDtypeStruct((tokens, channels), jnp.bfloat16),
        (carry, summary, short_taps, rates, residues, bias, decay, carry_weight, local, front),
        [plane],
    )


def solution(mesh):
    in_specs = (
        P(("ctx", "tp"), None, None),
        P(None, None, "tp"),
        P(None, "tp"),
        P(None, "tp"),
        P("tp"),
    )
    out_specs = P("ctx", "tp")
    return jax.shard_map(body, mesh=mesh, in_specs=in_specs, out_specs=out_specs, check_vma=False)
```

```python
import functools

import jax
import jax.numpy as jnp
from jax import lax
from jax.experimental import pallas as pl
from jax.experimental.pallas import tpu as pltpu
from jax.sharding import PartitionSpec as P

LENGTH = 4096
SUB = 16
PIECES = 6
LANES = 128
BLOCK = 128
VMEM = pl.BlockSpec(memory_space=pltpu.VMEM)


def row_iota():
    return lax.broadcasted_iota(jnp.int32, (8, LANES), 0)


def spread(row):
    return jnp.broadcast_to(row, (8, LANES))


def fill_tokens(blocks, stream, scratch):
    for block, source in blocks:
        at = pl.multiple_of(source * SUB, SUB)
        for group in range(scratch.shape[0]):
            lanes = pl.ds(group * LANES, LANES)
            scratch[group, pl.ds(at, SUB), :] = block[stream, :, lanes].astype(jnp.float32)


def join_kernel(at, own_ref, passed_ref, *refs):
    out_ref = refs[-1]
    out_ref[0] = own_ref[...]
    out_ref[1] = passed_ref[at]


def back_kernel(third_ref, second_ref, first_ref, out_ref):
    for at, ref in enumerate((first_ref, second_ref, third_ref)):
        out_ref[at] = ref[1]


def with_sources(refs):
    far, third, second, first, back, own = refs
    me = lax.axis_index("tp")
    turn = 1 - 2 * core_index()
    places = [(own, 0), (far, 4), (first.at[0], 1), (second.at[0], 2), (third.at[0], 3)]
    places += [(back.at[k - 1], -k) for k in (1, 2, 3)]
    return [(ref, lax.rem(me - turn * shift + 8, 8)) for ref, shift in places]


def featurize(scratch, stream, lanes, taps_ref):
    group = lanes.start // LANES
    values = [scratch[group, pl.ds(i, 8, stride=SUB), :] for i in range(SUB)]
    first = row_iota() == 0
    joined = [jnp.where(first, 0.0, pltpu.roll(values[SUB - far], 1, 0)) for far in (2, 1)] + values
    t0, t1, t2 = (spread(taps_ref[j, stream : stream + 1, lanes]) for j in range(3))
    return [t0 * joined[i + 2] + t1 * joined[i + 1] + t2 * joined[i] for i in range(SUB)]


def power(rate, tokens):
    return jnp.exp(rate * (-float(tokens) / LENGTH))


def core_index():
    return lax.rem(lax.axis_index("ctx"), 2)


TAIL = 4


def edge_signal(tail, head, taps):
    result = None
    for n, (t0, t1, t2) in enumerate(taps):
        x0, x1 = (head[2 * n + i : 2 * n + i + 1] for i in range(2))
        h0, h1 = (tail[2 * n + i : 2 * n + i + 1] for i in range(2))
        feats = (t0 * x0 + t1 * h1 + t2 * h0, t0 * x1 + t1 * x0 + t2 * h1)
        result = feats if result is None else tuple(a * b for a, b in zip(result, feats))
    return result


def edge_taps(taps_ref):
    return [[taps_ref[j, s : s + 1, :] for j in range(3)] for s in (1, 2)]


def weights_kernel(rates_ref, residues_ref, _, decay_ref, ends_ref, carry_ref):
    modes, channels = rates_ref.shape
    step = row_iota().astype(jnp.float32)
    remaining = (7.0 - step) * (SUB / LENGTH)
    elapsed = (step * SUB + 1.0) * (1.0 / LENGTH)
    decay_ref[...] = power(rates_ref[...], 1)
    for start in range(0, channels, LANES):
        lanes = pl.ds(start, LANES)
        for mode in range(modes):
            rate = spread(rates_ref[mode : mode + 1, lanes])
            ends_ref[mode, :, lanes] = jnp.exp(-rate * remaining)
            carry_ref[mode, :, lanes] = spread(residues_ref[mode : mode + 1, lanes]) * jnp.exp(-rate * elapsed)


def state_kernel(*refs):
    blocks = with_sources(refs[: PIECES])
    taps_ref, decay_ref, weight_ref, full, ends_ref, signal_ref, one, two = refs[PIECES :]
    modes, channels = decay_ref.shape
    fill_tokens(blocks, 1, one)
    fill_tokens(blocks, 2, two)
    rows = row_iota()
    full[modes:, :] = jnp.zeros((SUB, channels), jnp.float32)
    for group in range(channels // LANES):
        lanes = pl.ds(group * LANES, LANES)
        for n, scratch in enumerate((one, two)):
            full[modes + 2 * n : modes + 2 * n + 2, lanes] = scratch[group, 0:2, :]
            full[modes + TAIL + 2 * n : modes + TAIL + 2 * n + 2, lanes] = scratch[group, BLOCK - 2 : BLOCK, :]
    for block, source in blocks:

        @pl.when(source == 7)
        def _(block=block):
            full[modes + TAIL + 4 : modes + TAIL + 6, :] = block[0].astype(jnp.float32)[SUB - 2 :]

    for start in range(0, channels, LANES):
        lanes = pl.ds(start, LANES)
        left = featurize(one, 1, lanes, taps_ref)
        right = featurize(two, 2, lanes, taps_ref)
        signal = [a * b for a, b in zip(left, right)]
        for i in range(2):
            signal[i] = jnp.where(rows == 0, 0.0, signal[i])
        for i in range(SUB):
            signal_ref[i, :, lanes] = signal[i]
        for mode in range(modes):
            decay = spread(decay_ref[mode : mode + 1, lanes])
            state = signal[0]
            for i in range(1, SUB):
                state = state * decay + signal[i]
            ends_ref[mode, :, lanes] = state
            full[mode : mode + 1, lanes] = jnp.sum(state * weight_ref[mode, :, lanes], axis=0, keepdims=True)


def pack(state, edge, out_ref):
    high = state.astype(jnp.bfloat16)
    out_ref[0:SUB, :] = high
    out_ref[SUB : 2 * SUB, :] = (state - high.astype(jnp.float32)).astype(jnp.bfloat16)
    out_ref[2 * SUB : 3 * SUB, :] = edge.astype(jnp.bfloat16)


def join_edges(first, last):
    rows = lax.broadcasted_iota(jnp.int32, first.shape, 0)
    return jnp.where(rows < TAIL, first, last)


def pair_kernel(kept_ref, got_ref, rates_ref, taps_ref, out_ref, lower_ref):
    modes = rates_ref.shape[0]
    core = core_index()
    rate = rates_ref[...]
    kept, got = kept_ref[...], got_ref[...]
    lower = jnp.where(core == 0, kept, got)
    upper = jnp.where(core == 0, got, kept)
    s0, s1 = edge_signal(lower[modes + TAIL :], upper[modes:], edge_taps(taps_ref))
    inner = power(rate, BLOCK - 2) * (power(rate, 1) * s0 + s1)
    state = upper[:modes] + inner + power(rate, BLOCK) * lower[:modes]
    pack(state, join_edges(lower[modes:], upper[modes:]), out_ref)
    lower_ref[...] = lower


def chain(refs, place, tokens, rate, taps, opened):
    single, whole, last = power(rate, 1), power(rate, tokens), power(rate, tokens - 2)
    size = len(refs)
    carry = halo = before = total = jnp.zeros_like(rate)
    first = (jnp.zeros_like(rate[:1]),) * 2
    head = None
    for k in range(size):
        piece = refs[0][...]
        for by in range(1, size):
            piece = jnp.where(lax.rem(place - k + size, size) == by, refs[by][...], piece)
        state = piece[0:SUB].astype(jnp.float32) + piece[SUB : 2 * SUB].astype(jnp.float32)
        edge = piece[2 * SUB :].astype(jnp.float32)
        pieces = edge_signal(before[TAIL:], edge, taps)
        carry = jnp.where(place == k, total, carry)
        halo = jnp.where(place == k, before, halo)
        first = [jnp.where(place == k, new, old) for new, old in zip(pieces, first)]
        inner = last * (single * pieces[0] + pieces[1])
        if k == 0:
            head = edge
            total = state + inner if opened else state
        else:
            total = total * whole + state + inner
        before = edge
    return carry, first, halo, total, join_edges(head, before)


def place_of(stride):
    return lax.rem(lax.div(lax.axis_index("ctx"), stride), 4)


def row_kernel(own_ref, one_ref, three_ref, two_ref, rates_ref, taps_ref, out_ref, inside_ref):
    modes = rates_ref.shape[0]
    rate = rates_ref[...]
    refs = (own_ref, one_ref, two_ref, three_ref)
    carry, first, halo, total, edges = chain(refs, place_of(2), 2 * BLOCK, rate, edge_taps(taps_ref), False)
    pack(total, edges, out_ref)
    inside_ref[0:modes, :] = carry
    inside_ref[modes : 2 * modes, :] = halo
    for i in range(2):
        inside_ref[2 * modes + i : 2 * modes + i + 1, :] = first[i]


def merge_kernel(
    own_ref, one_ref, three_ref, two_ref, inside_ref, lower_ref, rates_ref, taps_ref, out_ref
):
    modes = rates_ref.shape[0]
    core = core_index()
    column, line = place_of(2), place_of(8)
    rate = rates_ref[...]
    refs = (own_ref, one_ref, two_ref, three_ref)
    taps = edge_taps(taps_ref)
    single = power(rate, 1)
    above, first, halo, _, _ = chain(refs, line, 8 * BLOCK, rate, taps, True)
    steps = (column * (2 * BLOCK)).astype(jnp.float32) * (-1.0 / LENGTH)
    behind = (column * (2 * BLOCK) - 2).astype(jnp.float32) * (-1.0 / LENGTH)
    inside = inside_ref[0:modes, :]
    opened = inside + jnp.exp(rate * behind) * (single * first[0] + first[1])
    carry = jnp.exp(rate * steps) * above + jnp.where(column > 0, opened, inside)
    within = [inside_ref[2 * modes + i : 2 * modes + i + 1, :] for i in range(2)]
    first = [jnp.where(column > 0, a, b) for a, b in zip(within, first)]
    halo = jnp.where(column > 0, inside_ref[modes : 2 * modes, :], halo)
    lower = lower_ref[...]
    inner = power(rate, BLOCK - 2) * (single * first[0] + first[1])
    carries = carry, power(rate, BLOCK) * carry + lower[:modes] + inner
    halos = halo[TAIL : TAIL + 8], lower[modes + TAIL : modes + TAIL + 8]
    out_ref[0:modes, :] = jnp.where(core == 0, *carries)
    out_ref[modes:, :] = jnp.where(core == 0, *halos)


def local_kernel(*refs):
    blocks = with_sources(refs[: PIECES])
    taps_ref, rates_ref, residues_ref, bias_ref, ends_ref, signal_ref, local_ref, front_ref, zero = refs[PIECES :]
    modes, channels = rates_ref.shape
    fill_tokens(blocks, 0, zero)
    rows = row_iota()
    step = rows.astype(jnp.float32)
    for start in range(0, channels, LANES):
        lanes = pl.ds(start, LANES)
        front = featurize(zero, 0, lanes, taps_ref)
        for i in range(SUB):
            front_ref[i, :, lanes] = front[i]
        signal = [signal_ref[i, :, lanes] for i in range(SUB)]
        taps = [jnp.zeros((8, LANES), jnp.float32) for _ in range(SUB // 8)]
        for mode in range(modes):
            rate = spread(rates_ref[mode : mode + 1, lanes])
            residue = spread(residues_ref[mode : mode + 1, lanes])
            for part in range(SUB // 8):
                taps[part] = taps[part] + residue * jnp.exp(-rate * ((step + 8.0 * part) * (1.0 / LENGTH)))
        bias = spread(bias_ref[0:1, lanes])
        total = [bias * signal[i] for i in range(SUB)]
        for lag in range(SUB):
            tap = spread(taps[lag // 8][lag % 8 : lag % 8 + 1])
            for i in range(lag, SUB):
                total[i] = total[i] + tap * signal[i - lag]
        for mode in range(modes):
            rate = spread(rates_ref[mode : mode + 1, lanes])
            residue = spread(residues_ref[mode : mode + 1, lanes])
            decay = jnp.exp(rate * (-1.0 / LENGTH))
            state = ends_ref[mode, :, lanes]
            for far in (1, 2, 4):
                state = state + jnp.where(rows >= far, power(rate, far * SUB) * pltpu.roll(state, far, 0), 0.0)
            carried = jnp.where(rows >= 1, pltpu.roll(state, 1, 0), 0.0) * residue
            for i in range(SUB):
                carried = carried * decay
                total[i] = total[i] + carried
        for i in range(SUB):
            local_ref[i, :, lanes] = total[i]


def final_kernel(
    carry_ref, summary_ref, taps_ref, rates_ref, residues_ref, bias_ref, decay_ref, weight_ref, local_ref, front_ref, out_ref, natural, rounded, sems
):
    modes, channels = rates_ref.shape
    rows = row_iota()
    copies = []

    def at_first(row):
        return jnp.where(rows == 0, spread(row), 0.0)

    for start in range(0, channels, LANES):
        lanes = pl.ds(start, LANES)
        halo = carry_ref[modes:, lanes]
        taps = [[taps_ref[j, s : s + 1, lanes] for j in range(3)] for s in (1, 2, 0)]
        s0, s1 = edge_signal(halo, summary_ref[modes:, lanes], taps[:2])
        _, t1, t2 = taps[2]
        bias = bias_ref[0:1, lanes]
        grow = power(rates_ref[:, lanes], -1)
        carry = carry_ref[:modes, lanes] + grow * (s0 + grow * s1)
        excess = jnp.sum(residues_ref[:, lanes] * grow, axis=0, keepdims=True) * s1
        total = [local_ref[i, :, lanes] for i in range(SUB)]
        front = [front_ref[i, :, lanes] for i in range(SUB)]
        total[0] = total[0] + at_first(bias * s0 - excess)
        total[1] = total[1] + at_first(bias * s1)
        front[0] = front[0] + at_first(t1 * halo[5:6] + t2 * halo[4:5])
        front[1] = front[1] + at_first(t2 * halo[5:6])
        for mode in range(modes):
            decay = spread(decay_ref[mode : mode + 1, lanes])
            carried = spread(carry[mode : mode + 1]) * weight_ref[mode, :, lanes]
            total[0] = total[0] + carried
            for i in range(1, SUB):
                carried = carried * decay
                total[i] = total[i] + carried
        for i in range(SUB):
            natural[start // LANES, pl.ds(i, 8, stride=SUB), :] = front[i] * total[i]
        group = start // LANES
        rounded[group] = natural[group].astype(out_ref.dtype)
        copies.append(pltpu.make_async_copy(rounded.at[group], out_ref.at[:, lanes], sems.at[group]))
        copies[-1].start()
    for copy in copies:
        copy.wait()


def body(streams, short_taps, residues, rates, bias):
    parts = lax.axis_size("tp")
    ctx = lax.axis_size("ctx")
    modes, channels = rates.shape
    tokens = SUB * parts
    f32 = jnp.float32
    wide = jax.ShapeDtypeStruct((SUB, parts, channels), f32)
    packed = jax.ShapeDtypeStruct((modes + SUB, channels), f32)
    carried = jax.ShapeDtypeStruct((modes + 8, channels), f32)
    plane = pltpu.VMEM((channels // LANES, tokens, LANES), f32)
    bias = bias[None]

    def kernel(function, out_shape, operands, scratch=(), cost=None, name=None, out_specs=VMEM):
        several = isinstance(out_shape, tuple)
        return pl.pallas_call(
            function,
            out_shape=out_shape,
            in_specs=[VMEM] * len(operands),
            out_specs=(VMEM,) * len(out_shape) if several else out_specs,
            scratch_shapes=list(scratch),
            compiler_params=pltpu.CompilerParams(vmem_limit_bytes=24 << 20),
            cost_estimate=cost,
            name=name or function.__name__,
        )(*operands)

    spans = jax.ShapeDtypeStruct((modes, parts, channels), f32)
    small = pl.CostEstimate(flops=8 << 20, bytes_accessed=2 << 20, transcendentals=0)
    decay, ends_weight, carry_weight = kernel(
        weights_kernel, (jax.ShapeDtypeStruct(rates.shape, f32), spans, spans), (rates, residues, bias), cost=small
    )
    by_stream = jnp.transpose(streams, (1, 0, 2))
    turn = 1 - 2 * core_index()
    swap = [(i, i ^ 1) for i in range(ctx)]

    def block_for(shift):
        at = ((lax.axis_index("tp") + turn * shift) % parts) * channels
        return lax.dynamic_slice(by_stream, (0, 0, at), (3, SUB, channels))

    def along(value, shift):
        route = []
        for c in range(ctx):
            step = -shift if c % 2 else shift
            route += [(c * parts + z, c * parts + (z + step) % parts) for z in range(parts)]
        return lax.ppermute(value, ("ctx", "tp"), route)

    passed = lax.ppermute(jnp.stack([block_for(-k) for k in (1, 2, 3)]), "ctx", swap)
    far = along(block_for(4), 4)
    two = jax.ShapeDtypeStruct((2, 3, SUB, channels), streams.dtype)
    three = jax.ShapeDtypeStruct((3, 3, SUB, channels), streams.dtype)

    def both(shift, *after):
        return kernel(functools.partial(join_kernel, shift - 1), two, (block_for(shift), passed, *after), name="join")

    third, second = (along(both(k), k) for k in (3, 2))
    first = along(both(1, far), 1)
    back = lax.ppermute(kernel(back_kernel, three, (third, second, first)), "ctx", swap)
    blocks = [far, third, second, first, back, block_for(0)]
    summary, ends, signal = kernel(
        state_kernel,
        (packed, spans, wide),
        (*blocks, short_taps, decay, ends_weight),
        [plane, plane],
    )
    got = lax.ppermute(summary, "ctx", swap)
    group = jax.ShapeDtypeStruct((3 * SUB, channels), jnp.bfloat16)

    def around(value, stride):
        parts = {}
        for by in (3, 1, 2):
            route = [(i, i + ((i // stride + by) % 4 - i // stride % 4) * stride) for i in range(ctx)]
            parts[by] = lax.ppermute(value, "ctx", route)
        return parts[1], parts[3], parts[2]

    pair, lower = kernel(pair_kernel, (group, packed), (summary, got, rates, short_taps))
    row, inside = kernel(
        row_kernel,
        (group, jax.ShapeDtypeStruct((2 * modes + 8, channels), f32)),
        (pair, *around(pair, 2), rates, short_taps),
    )
    carry = kernel(merge_kernel, carried, (row, *around(row, 8), inside, lower, rates, short_taps))
    local, front = kernel(
        local_kernel,
        (wide, wide),
        (*blocks, short_taps, rates, residues, bias, ends, signal),
        [plane],
        cost=small,
    )
    return kernel(
        final_kernel,
        jax.ShapeDtypeStruct((tokens, channels), jnp.bfloat16),
        (carry, summary, short_taps, rates, residues, bias, decay, carry_weight, local, front),
        [
            plane,
            pltpu.VMEM((channels // LANES, tokens, LANES), jnp.bfloat16),
            pltpu.SemaphoreType.DMA((channels // LANES,)),
        ],
        out_specs=pl.BlockSpec(memory_space=pl.ANY),
    )


def solution(mesh):
    in_specs = (
        P(("ctx", "tp"), None, None),
        P(None, None, "tp"),
        P(None, "tp"),
        P(None, "tp"),
        P("tp"),
    )
    out_specs = P("ctx", "tp")
    return jax.shard_map(body, mesh=mesh, in_specs=in_specs, out_specs=out_specs, check_vma=False)
```

```python
import functools

import jax
import jax.numpy as jnp
from jax import lax
from jax.experimental import pallas as pl
from jax.experimental.pallas import tpu as pltpu
from jax.sharding import PartitionSpec as P

LENGTH = 4096
SUB = 16
PIECES = 7
LANES = 128
BLOCK = 128
VMEM = pl.BlockSpec(memory_space=pltpu.VMEM)


def row_iota():
    return lax.broadcasted_iota(jnp.int32, (8, LANES), 0)


def spread(row):
    return jnp.broadcast_to(row, (8, LANES))


def fill_tokens(blocks, stream, scratch):
    for block, source in blocks:
        at = pl.multiple_of(source * SUB, SUB)
        for group in range(scratch.shape[0]):
            lanes = pl.ds(group * LANES, LANES)
            scratch[group, pl.ds(at, SUB), :] = block[stream, :, lanes].astype(jnp.float32)


def join_kernel(at, own_ref, passed_ref, *refs):
    out_ref = refs[-1]
    out_ref[0] = own_ref[...]
    out_ref[1] = passed_ref[at]


def back_kernel(*refs):
    for at, ref in enumerate(refs[:-1]):
        refs[-1][at] = ref[1]


def with_sources(refs):
    far, third, second, first, back, last, own = refs
    me = lax.axis_index("tp")
    turn = 1 - 2 * core_index()
    places = [(own, 0), (far, 4), (first.at[0], 1), (second.at[0], 2), (third.at[0], 3)]
    places += [(last.at[0], -1), (back.at[1], -2), (back.at[0], -3)]
    return [(ref, lax.rem(me - turn * shift + 8, 8)) for ref, shift in places]


def featurize(scratch, stream, lanes, taps_ref):
    group = lanes.start // LANES
    values = [scratch[group, pl.ds(i, 8, stride=SUB), :] for i in range(SUB)]
    first = row_iota() == 0
    joined = [jnp.where(first, 0.0, pltpu.roll(values[SUB - far], 1, 0)) for far in (2, 1)] + values
    t0, t1, t2 = (spread(taps_ref[j, stream : stream + 1, lanes]) for j in range(3))
    return [t0 * joined[i + 2] + t1 * joined[i + 1] + t2 * joined[i] for i in range(SUB)]


def power(rate, tokens):
    return jnp.exp(rate * (-float(tokens) / LENGTH))


def core_index():
    return lax.rem(lax.axis_index("ctx"), 2)


TAIL = 4


def edge_signal(tail, head, taps):
    result = None
    for n, (t0, t1, t2) in enumerate(taps):
        x0, x1 = (head[2 * n + i : 2 * n + i + 1] for i in range(2))
        h0, h1 = (tail[2 * n + i : 2 * n + i + 1] for i in range(2))
        feats = (t0 * x0 + t1 * h1 + t2 * h0, t0 * x1 + t1 * x0 + t2 * h1)
        result = feats if result is None else tuple(a * b for a, b in zip(result, feats))
    return result


def edge_taps(taps_ref):
    return [[taps_ref[j, s : s + 1, :] for j in range(3)] for s in (1, 2)]


def weights_kernel(rates_ref, residues_ref, _, decay_ref, ends_ref, carry_ref):
    modes, channels = rates_ref.shape
    step = row_iota().astype(jnp.float32)
    remaining = (7.0 - step) * (SUB / LENGTH)
    elapsed = (step * SUB + 1.0) * (1.0 / LENGTH)
    decay_ref[...] = power(rates_ref[...], 1)
    for start in range(0, channels, LANES):
        lanes = pl.ds(start, LANES)
        for mode in range(modes):
            rate = spread(rates_ref[mode : mode + 1, lanes])
            ends_ref[mode, :, lanes] = jnp.exp(-rate * remaining)
            carry_ref[mode, :, lanes] = spread(residues_ref[mode : mode + 1, lanes]) * jnp.exp(-rate * elapsed)


def state_kernel(*refs):
    blocks = with_sources(refs[: PIECES])
    taps_ref, decay_ref, weight_ref, full, ends_ref, signal_ref, one, two = refs[PIECES :]
    modes, channels = decay_ref.shape
    fill_tokens(blocks, 1, one)
    fill_tokens(blocks, 2, two)
    rows = row_iota()
    full[modes:, :] = jnp.zeros((SUB, channels), jnp.float32)
    for group in range(channels // LANES):
        lanes = pl.ds(group * LANES, LANES)
        for n, scratch in enumerate((one, two)):
            full[modes + 2 * n : modes + 2 * n + 2, lanes] = scratch[group, 0:2, :]
            full[modes + TAIL + 2 * n : modes + TAIL + 2 * n + 2, lanes] = scratch[group, BLOCK - 2 : BLOCK, :]
    for block, source in blocks:

        @pl.when(source == 7)
        def _(block=block):
            full[modes + TAIL + 4 : modes + TAIL + 6, :] = block[0].astype(jnp.float32)[SUB - 2 :]

    for start in range(0, channels, LANES):
        lanes = pl.ds(start, LANES)
        left = featurize(one, 1, lanes, taps_ref)
        right = featurize(two, 2, lanes, taps_ref)
        signal = [a * b for a, b in zip(left, right)]
        for i in range(2):
            signal[i] = jnp.where(rows == 0, 0.0, signal[i])
        for i in range(SUB):
            signal_ref[i, :, lanes] = signal[i]
        for mode in range(modes):
            decay = spread(decay_ref[mode : mode + 1, lanes])
            state = signal[0]
            for i in range(1, SUB):
                state = state * decay + signal[i]
            ends_ref[mode, :, lanes] = state
            full[mode : mode + 1, lanes] = jnp.sum(state * weight_ref[mode, :, lanes], axis=0, keepdims=True)


def pack(state, edge, out_ref):
    high = state.astype(jnp.bfloat16)
    out_ref[0:SUB, :] = high
    out_ref[SUB : 2 * SUB, :] = (state - high.astype(jnp.float32)).astype(jnp.bfloat16)
    out_ref[2 * SUB : 3 * SUB, :] = edge.astype(jnp.bfloat16)


def join_edges(first, last):
    rows = lax.broadcasted_iota(jnp.int32, first.shape, 0)
    return jnp.where(rows < TAIL, first, last)


def pair_kernel(kept_ref, got_ref, rates_ref, taps_ref, out_ref, lower_ref):
    modes = rates_ref.shape[0]
    core = core_index()
    rate = rates_ref[...]
    kept, got = kept_ref[...], got_ref[...]
    lower = jnp.where(core == 0, kept, got)
    upper = jnp.where(core == 0, got, kept)
    s0, s1 = edge_signal(lower[modes + TAIL :], upper[modes:], edge_taps(taps_ref))
    inner = power(rate, BLOCK - 2) * (power(rate, 1) * s0 + s1)
    state = upper[:modes] + inner + power(rate, BLOCK) * lower[:modes]
    pack(state, join_edges(lower[modes:], upper[modes:]), out_ref)
    lower_ref[...] = lower


def chain(refs, place, tokens, rate, taps, opened):
    single, whole, last = power(rate, 1), power(rate, tokens), power(rate, tokens - 2)
    size = len(refs)
    carry = halo = before = total = jnp.zeros_like(rate)
    first = (jnp.zeros_like(rate[:1]),) * 2
    head = None
    for k in range(size):
        piece = refs[0][...]
        for by in range(1, size):
            piece = jnp.where(lax.rem(place - k + size, size) == by, refs[by][...], piece)
        state = piece[0:SUB].astype(jnp.float32) + piece[SUB : 2 * SUB].astype(jnp.float32)
        edge = piece[2 * SUB :].astype(jnp.float32)
        pieces = edge_signal(before[TAIL:], edge, taps)
        carry = jnp.where(place == k, total, carry)
        halo = jnp.where(place == k, before, halo)
        first = [jnp.where(place == k, new, old) for new, old in zip(pieces, first)]
        inner = last * (single * pieces[0] + pieces[1])
        if k == 0:
            head = edge
            total = state + inner if opened else state
        else:
            total = total * whole + state + inner
        before = edge
    return carry, first, halo, total, join_edges(head, before)


def place_of(stride):
    return lax.rem(lax.div(lax.axis_index("ctx"), stride), 4)


def row_kernel(own_ref, one_ref, three_ref, two_ref, rates_ref, taps_ref, out_ref, inside_ref):
    modes = rates_ref.shape[0]
    rate = rates_ref[...]
    refs = (own_ref, one_ref, two_ref, three_ref)
    carry, first, halo, total, edges = chain(refs, place_of(2), 2 * BLOCK, rate, edge_taps(taps_ref), False)
    pack(total, edges, out_ref)
    inside_ref[0:modes, :] = carry
    inside_ref[modes : 2 * modes, :] = halo
    for i in range(2):
        inside_ref[2 * modes + i : 2 * modes + i + 1, :] = first[i]


def merge_kernel(
    own_ref, one_ref, three_ref, two_ref, inside_ref, lower_ref, rates_ref, taps_ref, out_ref
):
    modes = rates_ref.shape[0]
    core = core_index()
    column, line = place_of(2), place_of(8)
    rate = rates_ref[...]
    refs = (own_ref, one_ref, two_ref, three_ref)
    taps = edge_taps(taps_ref)
    single = power(rate, 1)
    above, first, halo, _, _ = chain(refs, line, 8 * BLOCK, rate, taps, True)
    steps = (column * (2 * BLOCK)).astype(jnp.float32) * (-1.0 / LENGTH)
    behind = (column * (2 * BLOCK) - 2).astype(jnp.float32) * (-1.0 / LENGTH)
    inside = inside_ref[0:modes, :]
    opened = inside + jnp.exp(rate * behind) * (single * first[0] + first[1])
    carry = jnp.exp(rate * steps) * above + jnp.where(column > 0, opened, inside)
    within = [inside_ref[2 * modes + i : 2 * modes + i + 1, :] for i in range(2)]
    first = [jnp.where(column > 0, a, b) for a, b in zip(within, first)]
    halo = jnp.where(column > 0, inside_ref[modes : 2 * modes, :], halo)
    lower = lower_ref[...]
    inner = power(rate, BLOCK - 2) * (single * first[0] + first[1])
    carries = carry, power(rate, BLOCK) * carry + lower[:modes] + inner
    halos = halo[TAIL : TAIL + 8], lower[modes + TAIL : modes + TAIL + 8]
    out_ref[0:modes, :] = jnp.where(core == 0, *carries)
    out_ref[modes:, :] = jnp.where(core == 0, *halos)


def local_kernel(*refs):
    blocks = with_sources(refs[: PIECES])
    taps_ref, rates_ref, residues_ref, bias_ref, ends_ref, signal_ref, local_ref, front_ref, zero = refs[PIECES :]
    modes, channels = rates_ref.shape
    fill_tokens(blocks, 0, zero)
    rows = row_iota()
    step = rows.astype(jnp.float32)
    for start in range(0, channels, LANES):
        lanes = pl.ds(start, LANES)
        front = featurize(zero, 0, lanes, taps_ref)
        for i in range(SUB):
            front_ref[i, :, lanes] = front[i]
        signal = [signal_ref[i, :, lanes] for i in range(SUB)]
        taps = [jnp.zeros((8, LANES), jnp.float32) for _ in range(SUB // 8)]
        for mode in range(modes):
            rate = spread(rates_ref[mode : mode + 1, lanes])
            residue = spread(residues_ref[mode : mode + 1, lanes])
            for part in range(SUB // 8):
                taps[part] = taps[part] + residue * jnp.exp(-rate * ((step + 8.0 * part) * (1.0 / LENGTH)))
        bias = spread(bias_ref[0:1, lanes])
        total = [bias * signal[i] for i in range(SUB)]
        for lag in range(SUB):
            tap = spread(taps[lag // 8][lag % 8 : lag % 8 + 1])
            for i in range(lag, SUB):
                total[i] = total[i] + tap * signal[i - lag]
        for mode in range(modes):
            rate = spread(rates_ref[mode : mode + 1, lanes])
            residue = spread(residues_ref[mode : mode + 1, lanes])
            decay = jnp.exp(rate * (-1.0 / LENGTH))
            state = ends_ref[mode, :, lanes]
            for far in (1, 2, 4):
                state = state + jnp.where(rows >= far, power(rate, far * SUB) * pltpu.roll(state, far, 0), 0.0)
            carried = jnp.where(rows >= 1, pltpu.roll(state, 1, 0), 0.0) * residue
            for i in range(SUB):
                carried = carried * decay
                total[i] = total[i] + carried
        for i in range(SUB):
            local_ref[i, :, lanes] = total[i]


def final_kernel(
    carry_ref, summary_ref, taps_ref, rates_ref, residues_ref, bias_ref, decay_ref, weight_ref, local_ref, front_ref, out_ref, natural
):
    modes, channels = rates_ref.shape
    rows = row_iota()

    def at_first(row):
        return jnp.where(rows == 0, spread(row), 0.0)

    for start in range(0, channels, LANES):
        lanes = pl.ds(start, LANES)
        halo = carry_ref[modes:, lanes]
        taps = [[taps_ref[j, s : s + 1, lanes] for j in range(3)] for s in (1, 2, 0)]
        s0, s1 = edge_signal(halo, summary_ref[modes:, lanes], taps[:2])
        _, t1, t2 = taps[2]
        bias = bias_ref[0:1, lanes]
        grow = power(rates_ref[:, lanes], -1)
        carry = carry_ref[:modes, lanes] + grow * (s0 + grow * s1)
        excess = jnp.sum(residues_ref[:, lanes] * grow, axis=0, keepdims=True) * s1
        total = [local_ref[i, :, lanes] for i in range(SUB)]
        front = [front_ref[i, :, lanes] for i in range(SUB)]
        total[0] = total[0] + at_first(bias * s0 - excess)
        total[1] = total[1] + at_first(bias * s1)
        front[0] = front[0] + at_first(t1 * halo[5:6] + t2 * halo[4:5])
        front[1] = front[1] + at_first(t2 * halo[5:6])
        for mode in range(modes):
            decay = spread(decay_ref[mode : mode + 1, lanes])
            carried = spread(carry[mode : mode + 1]) * weight_ref[mode, :, lanes]
            total[0] = total[0] + carried
            for i in range(1, SUB):
                carried = carried * decay
                total[i] = total[i] + carried
        for i in range(SUB):
            natural[start // LANES, pl.ds(i, 8, stride=SUB), :] = front[i] * total[i]
        out_ref[:, lanes] = natural[start // LANES].astype(out_ref.dtype)


def body(streams, short_taps, residues, rates, bias):
    parts = lax.axis_size("tp")
    ctx = lax.axis_size("ctx")
    modes, channels = rates.shape
    tokens = SUB * parts
    f32 = jnp.float32
    wide = jax.ShapeDtypeStruct((SUB, parts, channels), f32)
    packed = jax.ShapeDtypeStruct((modes + SUB, channels), f32)
    carried = jax.ShapeDtypeStruct((modes + 8, channels), f32)
    plane = pltpu.VMEM((channels // LANES, tokens, LANES), f32)
    bias = bias[None]

    def kernel(function, out_shape, operands, scratch=(), cost=None, name=None):
        several = isinstance(out_shape, tuple)
        return pl.pallas_call(
            function,
            out_shape=out_shape,
            in_specs=[VMEM] * len(operands),
            out_specs=(VMEM,) * len(out_shape) if several else VMEM,
            scratch_shapes=list(scratch),
            compiler_params=pltpu.CompilerParams(vmem_limit_bytes=24 << 20),
            cost_estimate=cost,
            name=name or function.__name__,
        )(*operands)

    spans = jax.ShapeDtypeStruct((modes, parts, channels), f32)
    small = pl.CostEstimate(flops=8 << 20, bytes_accessed=2 << 20, transcendentals=0)
    decay, ends_weight, carry_weight = kernel(
        weights_kernel, (jax.ShapeDtypeStruct(rates.shape, f32), spans, spans), (rates, residues, bias), cost=small
    )
    by_stream = jnp.transpose(streams, (1, 0, 2))
    turn = 1 - 2 * core_index()
    swap = [(i, i ^ 1) for i in range(ctx)]

    def block_for(shift):
        at = ((lax.axis_index("tp") + turn * shift) % parts) * channels
        return lax.dynamic_slice(by_stream, (0, 0, at), (3, SUB, channels))

    def along(value, shift):
        route = []
        for c in range(ctx):
            step = -shift if c % 2 else shift
            route += [(c * parts + z, c * parts + (z + step) % parts) for z in range(parts)]
        return lax.ppermute(value, ("ctx", "tp"), route)

    passed = lax.ppermute(jnp.stack([block_for(-k) for k in (1, 2, 3)]), "ctx", swap)
    far = along(block_for(4), 4)
    two = jax.ShapeDtypeStruct((2, 3, SUB, channels), streams.dtype)
    one = jax.ShapeDtypeStruct((1, 3, SUB, channels), streams.dtype)

    def both(shift, *after):
        return kernel(functools.partial(join_kernel, shift - 1), two, (block_for(shift), passed, *after), name="join")

    third, second = (along(both(k), k) for k in (3, 2))
    first = along(both(1, far), 1)
    back = lax.ppermute(kernel(back_kernel, two, (third, second)), "ctx", swap)
    last = lax.ppermute(kernel(back_kernel, one, (first,)), "ctx", swap)
    blocks = [far, third, second, first, back, last, block_for(0)]
    summary, ends, signal = kernel(
        state_kernel,
        (packed, spans, wide),
        (*blocks, short_taps, decay, ends_weight),
        [plane, plane],
    )
    got = lax.ppermute(summary, "ctx", swap)
    group = jax.ShapeDtypeStruct((3 * SUB, channels), jnp.bfloat16)

    def around(value, stride):
        parts = {}
        for by in (3, 1, 2):
            route = [(i, i + ((i // stride + by) % 4 - i // stride % 4) * stride) for i in range(ctx)]
            parts[by] = lax.ppermute(value, "ctx", route)
        return parts[1], parts[3], parts[2]

    pair, lower = kernel(pair_kernel, (group, packed), (summary, got, rates, short_taps))
    row, inside = kernel(
        row_kernel,
        (group, jax.ShapeDtypeStruct((2 * modes + 8, channels), f32)),
        (pair, *around(pair, 2), rates, short_taps),
    )
    carry = kernel(merge_kernel, carried, (row, *around(row, 8), inside, lower, rates, short_taps))
    local, front = kernel(
        local_kernel,
        (wide, wide),
        (*blocks, short_taps, rates, residues, bias, ends, signal),
        [plane],
        cost=small,
    )
    return kernel(
        final_kernel,
        jax.ShapeDtypeStruct((tokens, channels), jnp.bfloat16),
        (carry, summary, short_taps, rates, residues, bias, decay, carry_weight, local, front),
        [plane],
    )


def solution(mesh):
    in_specs = (
        P(("ctx", "tp"), None, None),
        P(None, None, "tp"),
        P(None, "tp"),
        P(None, "tp"),
        P("tp"),
    )
    out_specs = P("ctx", "tp")
    return jax.shard_map(body, mesh=mesh, in_specs=in_specs, out_specs=out_specs, check_vma=False)
```
